128 devices in a mesh: dp: 16 (over y, x_lo, core), seq: 8 (over z, x_hi).
Axes of the slice: x: 4 (x_hi: 2, x_lo: 2; x = x_hi * 2 + x_lo), y: 4, z: 4, core: 2. Of those that a mesh axis runs over, the one named last changes fastest.
Arguments:
- tokens: bfloat16 [48, 1152, 768], P('dp', 'seq'), may hold values from -6 to 6
- view_counts: int32 [48], P('dp'), may hold values from 2 to 8, as said below
- ln1_gain: float32 [768], replicated, may hold values from 0.25 to 1.75
- ln1_shift: float32 [768], replicated, may hold values from -1.5 to 1.5
- qkv_weight: bfloat16 [768, 2304], replicated, may hold values from -0.21875 to 0.21875
- query_bias: float32 [768], replicated, may hold values from -2.5 to 2.5
- value_bias: float32 [768], replicated, may hold values from -2.5 to 2.5
- out_weight: bfloat16 [768, 768], replicated, may hold values from -1.75 to 1.75
- out_bias: float32 [768], replicated, may hold values from -1.5 to 1.5
- ln2_gain: float32 [768], replicated, may hold values from 0.25 to 1.75
- ln2_shift: float32 [768], replicated, may hold values from -1.5 to 1.5
- up_weight: bfloat16 [768, 3072], replicated, may hold values from -0.21875 to 0.21875
- up_bias: float32 [3072], replicated, may hold values from -2.5 to 2.5
- down_weight: bfloat16 [3072, 768], replicated, may hold values from -0.109375 to 0.109375
- down_bias: float32 [768], replicated, may hold values from -1.5 to 1.5
- cotangent: bfloat16 [48, 1152, 768], P('dp', 'seq'), may hold values from -6 to 6
Outputs:
- output: bfloat16 [48, 1152, 768], P('dp', 'seq')
- input_grad: bfloat16 [48, 1152, 768], P('dp', 'seq')
- ln1_gain_grad: float32 [768], replicated
- ln1_shift_grad: float32 [768], replicated
- qkv_weight_grad: float32 [768, 2304], replicated
- query_bias_grad: float32 [768], replicated
- value_bias_grad: float32 [768], replicated
- out_weight_grad: float32 [768, 768], replicated
- out_bias_grad: float32 [768], replicated
- ln2_gain_grad: float32 [768], replicated
- ln2_shift_grad: float32 [768], replicated
- up_weight_grad: float32 [768, 3072], replicated
- up_bias_grad: float32 [3072], replicated
- down_weight_grad: float32 [3072, 768], replicated
- down_bias_grad: float32 [768], replicated
The draws below stay inside these ranges and needn't reach their ends.
Inputs may be any that keep to these rules, and one draw needn't show every extreme that they name: `view_counts`: each data group's 3 consecutive scenes include at least one with 8 input views.
All inputs are finite; a program needn't handle non-finite values.
Results may differ from the reference program's by a relative error of at most 0.018.
Values may be sent and summed in bfloat16 or wider, within the bound.
No kernel may reach another device: no remote copies, remote signals or barrier semaphores. Data moves between devices by JAX's collectives and lax.ppermute only.
A program may use at most 192 MiB of HBM per device.

```python
import jax
import jax.numpy as jnp
from jax import lax

HEADS = 12
HEAD_DIM = 64
D = 768
FF = 3072
VIEW_TOK = 128
VIEWS_MAX = 8
MICRO = 3
SCENE_LEN = 1152
SCENES = 48


def draw_view_counts(key, part):
    key = jax.random.fold_in(key, 11)
    first_key, second_key = jax.random.split(key)
    counts = jax.random.randint(first_key, (SCENES,), 2, VIEWS_MAX + 1, dtype=jnp.int32)
    groups = SCENES // MICRO
    chosen = jax.random.randint(second_key, (groups,), 0, MICRO, dtype=jnp.int32)
    places = jnp.arange(groups, dtype=jnp.int32) * MICRO + chosen
    return counts.at[places].set(VIEWS_MAX)


def steps_of(key, extent, cuts, smallest, largest):
    gain, own = 1.0, jax.random.fold_in(key, 6)
    for position, parts in cuts:
        draws = jnp.exp(jax.random.uniform(jax.random.fold_in(own, position), (parts,), jnp.float32, smallest / len(cuts), largest / len(cuts)))
        gain = gain * jnp.repeat(draws, extent[position] // parts).reshape([-1 if axis == position else 1 for axis in range(len(extent))])
    return gain


def normal_values(stream_key, extent, scale, limit, shards=(), kind=jnp.bfloat16):
    entries = jax.random.normal(stream_key, extent, jnp.float32) * scale
    if len(shards) > 0:
        entries = steps_of(stream_key, extent, shards, -0.22, 0.18) * entries
    return jnp.clip(entries, min=-limit, max=limit).astype(kind)


def setup_inputs(seed: int = 0) -> dict:
    keys = jax.random.split(jax.random.key(seed), 17)
    return {
        "tokens": normal_values(keys[0], (SCENES, SCENE_LEN, D), 1.0, 6.0, ((0, 16), (1, 8))),
        "view_counts": draw_view_counts(jax.random.fold_in(keys[16], 71), 0),
        "ln1_gain": jnp.clip(1.0 + 0.15 * jax.random.normal(keys[2], (D,), jnp.float32), 0.25, 1.75),
        "ln1_shift": normal_values(keys[3], (D,), 0.3, 1.5, (), jnp.float32),
        "qkv_weight": normal_values(keys[4], (D, 3 * D), D ** -0.5, 0.21875),
        "query_bias": normal_values(keys[5], (D,), 0.5, 2.5, (), jnp.float32),
        "value_bias": normal_values(keys[6], (D,), 0.5, 2.5, (), jnp.float32),
        "out_weight": normal_values(keys[7], (D, D), (D // 64) ** -0.5, 1.75),
        "out_bias": normal_values(keys[8], (D,), 0.3, 1.5, (), jnp.float32),
        "ln2_gain": jnp.clip(1.0 + 0.15 * jax.random.normal(keys[9], (D,), jnp.float32), 0.25, 1.75),
        "ln2_shift": normal_values(keys[10], (D,), 0.3, 1.5, (), jnp.float32),
        "up_weight": normal_values(keys[11], (D, FF), D ** -0.5, 0.21875),
        "up_bias": normal_values(keys[12], (FF,), 0.5, 2.5, (), jnp.float32),
        "down_weight": normal_values(keys[13], (FF, D), FF ** -0.5, 0.109375),
        "down_bias": normal_values(keys[14], (D,), 0.3, 1.5, (), jnp.float32),
        "cotangent": normal_values(keys[15], (SCENES, SCENE_LEN, D), 1.0, 6.0, ((0, 16), (1, 8))),
    }


@jax.custom_vjp
def low(v):
    return lax.optimization_barrier(v.astype(jnp.bfloat16)).astype(jnp.float32)

@jax.custom_vjp
def low_back(v):
    return v

def low_keep(v):
    return (low(v), None)

def low_pass(kept, grad):
    return (grad,)

def back_keep(v):
    return (v, None)

def back_low(kept, grad):
    return (low(grad),)
low.defvjp(low_keep, low_pass)
low_back.defvjp(back_keep, back_low)
highest = lax.Precision.HIGHEST
epsilon = 1e-05
masked_score = -1e+30

def layer_norm(values_in, gain_vector, shift_vector):
    centred = values_in - lax.optimization_barrier(jnp.mean(values_in, axis=-1, keepdims=True))
    spread = lax.optimization_barrier(jnp.mean(centred * centred, axis=-1, keepdims=True))
    return centred * lax.rsqrt(spread + epsilon) * gain_vector + shift_vector

def usable_keys(view_now, offset, length):
    positions = offset + jnp.arange(length, dtype=jnp.int32)
    return (positions < view_now * VIEW_TOK) | (positions >= VIEWS_MAX * VIEW_TOK)

def scene_forward(inputs, params, usable):
    ln1_gain, ln1_shift, qkv_weight, query_bias, value_bias, out_weight, out_bias, ln2_gain, ln2_shift, up_weight, up_bias, down_weight, down_bias = params
    length = inputs.shape[0]
    normed = low(layer_norm(inputs, ln1_gain, ln1_shift))
    joined = jnp.dot(normed, qkv_weight, precision=highest)
    queries = low(low_back(joined[:, :D] + query_bias)).reshape(length, HEADS, HEAD_DIM)
    key_rows = low(low_back(joined[:, D:2 * D])).reshape(length, HEADS, HEAD_DIM)
    value_rows = low(low_back(joined[:, 2 * D:] + value_bias)).reshape(length, HEADS, HEAD_DIM)
    scores = low_back(jnp.einsum('qhd,khd->hqk', queries, key_rows, precision=highest) * 0.125)
    scores = jnp.where(usable[None, None, :], scores, masked_score)
    maxima = lax.optimization_barrier(jnp.max(scores, axis=-1, keepdims=True))
    weights = jnp.exp(scores - maxima)
    weights = weights / lax.optimization_barrier(jnp.sum(weights, axis=-1, keepdims=True))
    attended = jnp.einsum('hqk,khd->qhd', low(weights), value_rows, precision=highest).reshape(length, D)
    attended = low(low_back(attended))
    hidden = inputs + low_back(jnp.dot(attended, out_weight, precision=highest)) + out_bias
    normed2 = low(layer_norm(hidden, ln2_gain, ln2_shift))
    upward = low_back(jnp.dot(normed2, up_weight, precision=highest) + up_bias)
    active = low(jax.nn.gelu(upward, approximate=True))
    return hidden + jnp.dot(active, down_weight, precision=highest) + down_bias

def reference(tokens, view_counts, ln1_gain, ln1_shift, qkv_weight, query_bias, value_bias, out_weight, out_bias, ln2_gain, ln2_shift, up_weight, up_bias, down_weight, down_bias, cotangent):
    params = tuple((member.astype(jnp.float32) for member in (ln1_gain, ln1_shift, qkv_weight, query_bias, value_bias, out_weight, out_bias, ln2_gain, ln2_shift, up_weight, up_bias, down_weight, down_bias)))

    def one_scene(running, inputs_now):
        scene_tokens, view_now, scene_cotangent = inputs_now
        usable = usable_keys(view_now, 0, SCENE_LEN)
        result, pullback = jax.vjp(lambda source, *weights: scene_forward(source, weights, usable), scene_tokens.astype(jnp.float32), *params)
        gradients = pullback(scene_cotangent.astype(jnp.float32))
        running = tuple((total + extra for total, extra in zip(running, gradients[1:])))
        return (running, (result.astype(jnp.bfloat16), gradients[0].astype(jnp.bfloat16)))
    initial = tuple((jnp.zeros_like(member) for member in params))
    totals, (outputs, input_grads) = lax.scan(one_scene, initial, (tokens, view_counts, cotangent))
    return (outputs, input_grads, totals[0], totals[1], totals[2], totals[3], totals[4], totals[5], totals[6], totals[7], totals[8], totals[9], totals[10], totals[11], totals[12])
```

```python
import itertools
import math

import jax
import jax.numpy as jnp
from jax import lax
from jax.experimental import pallas as pl
from jax.experimental.pallas import tpu as pltpu
from jax.sharding import Mesh
from jax.sharding import PartitionSpec as P

HEADS = 12
HEAD_DIM = 64
VIEW_TOK = 128
VIEWS_MAX = 8
D = 768
FF = 3072
BLK = 144
SLOTS = 4
ROWS = BLK * SLOTS
KEYS = 2 * ROWS
PAIRS = HEADS // 2
LANES = 128
FCHUNK = 768
NF = FF // FCHUNK

bf16 = jnp.bfloat16
f32 = jnp.float32
epsilon = 1e-05
masked_score = -1e30
GELU_C = math.sqrt(2.0 / math.pi)
GELU_A = 0.044715

AXES = ("y", "xl", "c", "z", "xh")
VMEM_LIMIT = 60 * 1024 * 1024


def mm(a, b):
    return lax.dot_general(a, b, (((1,), (0,)), ((), ())), preferred_element_type=f32)


def mm_nt(a, b):
    return lax.dot_general(a, b, (((1,), (1,)), ((), ())), preferred_element_type=f32)


def mm_tn(a, b):
    return lax.dot_general(a, b, (((0,), (0,)), ((), ())), preferred_element_type=f32)


def lane_row(at, first, last):
    lane = lax.broadcasted_iota(jnp.int32, (1, LANES), 1)
    return jnp.where((lane >= first) & (lane < last), 1.0, 0.0).astype(at)


def attention_forward_kernel(q_ref, ko_ref, vo_ref, ks_ref, vs_ref, mask_ref, p_ref, o_ref, linv_ref, att_ref):
    half = [lane_row(bf16, 0, 64), lane_row(bf16, 64, 128)]
    unit = [lane_row(bf16, 64, 65), lane_row(bf16, 0, 1)]
    q = q_ref[...]
    k = jnp.concatenate([ko_ref[...], ks_ref[...]], axis=0)
    v = jnp.concatenate([vo_ref[...], vs_ref[...]], axis=0)
    mask = mask_ref[...]
    lane = lax.broadcasted_iota(jnp.int32, (BLK, LANES), 1)
    q_now = [q * half[h] + unit[h] for h in range(2)]
    k_now = [k * half[h] + mask * unit[h] for h in range(2)]
    v_now = [v * half[h] + unit[h] for h in range(2)]
    for s in range(SLOTS):
        rows = slice(s * BLK, (s + 1) * BLK)
        outs, invs = [], []
        for h in range(2):
            scores = mm_nt(q_now[h][rows], k_now[h])
            top = jnp.max(scores, axis=1, keepdims=True)
            weights = jnp.exp((scores - top) * 0.125).astype(bf16)
            p_ref[h, rows, :] = weights
            out = mm(weights, v_now[h])
            total = out[:, 64:65] if h == 0 else out[:, 0:1]
            inv = 1.0 / total
            outs.append(out * inv)
            invs.append(jnp.broadcast_to(inv, (BLK, LANES)))
        out = jnp.where(lane < 64, outs[0], outs[1])
        o_ref[rows, :] = out
        att_ref[rows, :] = out.astype(bf16)
        linv_ref[rows, :] = jnp.where(lane < 64, invs[0], invs[1])


def attention_forward(joined, sibling, mask):
    col = lambda first: pl.BlockSpec((ROWS, LANES), lambda i, f=first: (0, f + i))
    return pl.pallas_call(
        attention_forward_kernel,
        grid=(PAIRS,),
        in_specs=[
            col(0), col(PAIRS), col(2 * PAIRS), col(0), col(PAIRS),
            pl.BlockSpec((KEYS, LANES), lambda i: (0, 0)),
        ],
        out_specs=[
            pl.BlockSpec((2, ROWS, KEYS), lambda i: (i, 0, 0)),
            col(0), col(0), col(0),
        ],
        out_shape=[
            jax.ShapeDtypeStruct((HEADS, ROWS, KEYS), bf16),
            jax.ShapeDtypeStruct((ROWS, D), f32),
            jax.ShapeDtypeStruct((ROWS, D), f32),
            jax.ShapeDtypeStruct((ROWS, D), bf16),
        ],
        compiler_params=pltpu.CompilerParams(vmem_limit_bytes=VMEM_LIMIT),
        cost_estimate=pl.CostEstimate(flops=16 * ROWS * KEYS * D, bytes_accessed=20_000_000, transcendentals=HEADS * ROWS * KEYS),
        name="attention_forward",
    )(joined, joined, joined, sibling, sibling, mask)


def attention_backward_kernel(
    q_ref, ko_ref, vo_ref, ks_ref, vs_ref, p_ref, o_ref, linv_ref, g_ref,
    gq_ref, gko_ref, gvo_ref, gks_ref, gvs_ref,
):
    half = [lane_row(bf16, 0, 64), lane_row(bf16, 64, 128)]
    two = [lane_row(bf16, 64, 66), lane_row(bf16, 0, 2)]
    q = q_ref[...]
    k = jnp.concatenate([ko_ref[...], ks_ref[...]], axis=0)
    v = jnp.concatenate([vo_ref[...], vs_ref[...]], axis=0)
    v_now = [v * half[h] + two[h] for h in range(2)]
    lane = lax.broadcasted_iota(jnp.int32, (ROWS, LANES), 1)
    gs = g_ref[...].astype(f32) * linv_ref[...]
    prod = gs * o_ref[...]
    gq, gk, gv = [], [], []
    for h in range(2):
        mine = (lane < 64) if h == 0 else (lane >= 64)
        base = 64 if h == 0 else 0
        delta = jnp.sum(jnp.where(mine, prod, 0.0), axis=1, keepdims=True)
        high = delta.astype(bf16).astype(f32)
        g_aug = jnp.where(
            mine, gs, jnp.where(lane == base, -high, jnp.where(lane == base + 1, high - delta, 0.0))
        ).astype(bf16)
        weights = p_ref[h]
        diff = mm_nt(g_aug, v_now[h])
        gscore = (weights.astype(f32) * diff).astype(bf16)
        gv.append(mm_tn(weights, g_aug))
        gk.append(mm_tn(gscore, q))
        gq.append(mm(gscore, k))
    gq_ref[...] = (jnp.where(lane < 64, gq[0], gq[1]) * 0.125).astype(bf16)
    lane_k = lax.broadcasted_iota(jnp.int32, (KEYS, LANES), 1)
    gk_all = jnp.where(lane_k < 64, gk[0], gk[1]) * 0.125
    gv_all = jnp.where(lane_k < 64, gv[0], gv[1])
    gko_ref[...] = gk_all[:ROWS]
    gvo_ref[...] = gv_all[:ROWS]
    gks_ref[...] = gk_all[ROWS:].astype(bf16)
    gvs_ref[...] = gv_all[ROWS:].astype(bf16)


def attention_backward(joined, sibling, weights, heads_out, linv, grad_att):
    col = lambda first: pl.BlockSpec((ROWS, LANES), lambda i, f=first: (0, f + i))
    return pl.pallas_call(
        attention_backward_kernel,
        grid=(PAIRS,),
        in_specs=[
            col(0), col(PAIRS), col(2 * PAIRS), col(0), col(PAIRS),
            pl.BlockSpec((2, ROWS, KEYS), lambda i: (i, 0, 0)),
            col(0), col(0), col(0),
        ],
        out_specs=[col(0), col(0), col(0), col(0), col(0)],
        out_shape=[
            jax.ShapeDtypeStruct((ROWS, D), bf16),
            jax.ShapeDtypeStruct((ROWS, D), f32),
            jax.ShapeDtypeStruct((ROWS, D), f32),
            jax.ShapeDtypeStruct((ROWS, D), bf16),
            jax.ShapeDtypeStruct((ROWS, D), bf16),
        ],
        compiler_params=pltpu.CompilerParams(vmem_limit_bytes=VMEM_LIMIT),
        cost_estimate=pl.CostEstimate(flops=32 * ROWS * KEYS * D, bytes_accessed=25_000_000, transcendentals=0),
        name="attention_backward",
    )(joined, joined, joined, sibling, sibling, weights, heads_out, linv, grad_att)


def feed_forward_kernel(
    att_ref, x_ref, g_ref, ow_ref, vec_ref, upb_ref, up_ref, down_ref,
    out_ref, gh_ref, gatt_ref, dout_ref, dup_ref, ddown_ref, vecg_ref, upbg_ref,
    hidden, xhat, rstd_s, normed2, y_acc, gn_acc,
):
    f = pl.program_id(0)
    out_bias, gain, shift, down_bias = (vec_ref[r : r + 1, :] for r in range(4))

    @pl.when(f == 0)
    def _():
        h = x_ref[...].astype(f32) + mm(att_ref[...], ow_ref[...]) + out_bias
        hidden[...] = h
        centred = h - jnp.mean(h, axis=1, keepdims=True)
        rstd = lax.rsqrt(jnp.mean(centred * centred, axis=1, keepdims=True) + epsilon)
        xh = centred * rstd
        xhat[...] = xh
        rstd_s[...] = jnp.broadcast_to(rstd, (ROWS, LANES))
        normed2[...] = (xh * gain + shift).astype(bf16)
        y_acc[...] = jnp.zeros_like(y_acc)
        gn_acc[...] = jnp.zeros_like(gn_acc)

    g = g_ref[...]
    n2 = normed2[...]
    u = mm(n2, up_ref[...]) + upb_ref[0]
    ga = mm_nt(g, down_ref[...])
    u2 = u * u
    t = jnp.tanh(u * (GELU_C + (GELU_C * GELU_A) * u2))
    hp = 0.5 + 0.5 * t
    active = (u * hp).astype(bf16)
    slope = hp + (0.5 * u) * (1.0 - t * t) * (GELU_C + (3.0 * GELU_C * GELU_A) * u2)
    gu = (ga * slope).astype(bf16)
    y_acc[...] += mm(active, down_ref[...])
    gn_acc[...] += mm_nt(gu, up_ref[...])
    ddown_ref[...] = mm_tn(active, g).astype(bf16)
    dup_ref[...] = mm_tn(n2, gu).astype(bf16)
    upbg_ref[0] = jnp.sum(gu.astype(f32), axis=0, keepdims=True)

    @pl.when(f == NF - 1)
    def _():
        out_ref[...] = (hidden[...] + y_acc[...] + down_bias).astype(bf16)
        gn = gn_acc[...]
        xh = xhat[...]
        gf = g_ref[...].astype(f32)
        vecg_ref[...] = jnp.zeros_like(vecg_ref)
        vecg_ref[1:2, :] = jnp.sum(gn * xh, axis=0, keepdims=True)
        vecg_ref[2:3, :] = jnp.sum(gn, axis=0, keepdims=True)
        vecg_ref[3:4, :] = jnp.sum(gf, axis=0, keepdims=True)
        gx = gn * gain
        mean1 = jnp.mean(gx, axis=1, keepdims=True)
        mean2 = jnp.mean(gx * xh, axis=1, keepdims=True)
        gh = gf + rstd_s[:, 0:1] * (gx - mean1 - xh * mean2)
        gh_ref[...] = gh
        vecg_ref[0:1, :] = jnp.sum(gh, axis=0, keepdims=True)
        gb = gh.astype(bf16)
        dout_ref[...] = mm_tn(att_ref[...], gb).astype(bf16)
        gatt_ref[...] = mm_nt(gb, ow_ref[...]).astype(bf16)


def feed_forward(attended, x, g, out_w, vecs, up_b, up_w, down_w):
    whole = lambda shape: pl.BlockSpec(shape, lambda f: (0,) * len(shape))
    return pl.pallas_call(
        feed_forward_kernel,
        grid=(NF,),
        in_specs=[
            whole((ROWS, D)), whole((ROWS, D)), whole((ROWS, D)), whole((D, D)), whole((8, D)),
            pl.BlockSpec((1, 1, FCHUNK), lambda f: (f, 0, 0)),
            pl.BlockSpec((D, FCHUNK), lambda f: (0, f)),
            pl.BlockSpec((FCHUNK, D), lambda f: (f, 0)),
        ],
        out_specs=[
            whole((ROWS, D)), whole((ROWS, D)), whole((ROWS, D)), whole((D, D)),
            pl.BlockSpec((D, FCHUNK), lambda f: (f, 0)),
            pl.BlockSpec((FCHUNK, D), lambda f: (f, 0)),
            whole((8, D)),
            pl.BlockSpec((1, 1, FCHUNK), lambda f: (f, 0, 0)),
        ],
        out_shape=[
            jax.ShapeDtypeStruct((ROWS, D), bf16),
            jax.ShapeDtypeStruct((ROWS, D), f32),
            jax.ShapeDtypeStruct((ROWS, D), bf16),
            jax.ShapeDtypeStruct((D, D), bf16),
            jax.ShapeDtypeStruct((NF * D, FCHUNK), bf16),
            jax.ShapeDtypeStruct((FF, D), bf16),
            jax.ShapeDtypeStruct((8, D), f32),
            jax.ShapeDtypeStruct((NF, 1, FCHUNK), f32),
        ],
        scratch_shapes=[
            pltpu.VMEM((ROWS, D), f32),
            pltpu.VMEM((ROWS, D), f32),
            pltpu.VMEM((ROWS, LANES), f32),
            pltpu.VMEM((ROWS, D), bf16),
            pltpu.VMEM((ROWS, D), f32),
            pltpu.VMEM((ROWS, D), f32),
        ],
        compiler_params=pltpu.CompilerParams(vmem_limit_bytes=VMEM_LIMIT),
        cost_estimate=pl.CostEstimate(flops=12 * ROWS * D * FF, bytes_accessed=30_000_000, transcendentals=ROWS * FF),
        name="feed_forward",
    )(attended, x, g, out_w, vecs, up_b, up_w, down_w)


def linear(y, xl, c, z, xh):
    return (((y * 2 + xl) * 2 + c) * 4 + z) * 2 + xh


def scene_pairs(slot):
    pairs = []
    for y in range(4):
        for xl in range(2):
            for z in range(4):
                for xh in range(2):
                    block = 2 * z + xh
                    scene = (slot - block) % 4
                    if scene < 3:
                        for c in range(2):
                            pairs.append((linear(y, xl, c, z, xh), linear(y, xl, block // 4, scene, c)))
    return pairs


def to_scene(values, block):
    pieces = []
    for slot in range(SLOTS):
        scene = jnp.minimum((slot - block) % 4, 2)
        pieces.append(lax.ppermute(lax.dynamic_index_in_dim(values, scene, 0, keepdims=False), AXES, scene_pairs(slot)))
    return jnp.concatenate(pieces, axis=0)


def from_scene(values, block):
    pieces = []
    for slot in range(SLOTS):
        back = [(target, source) for source, target in scene_pairs(slot)]
        pieces.append(lax.ppermute(values[slot * BLK : (slot + 1) * BLK], AXES, back))
    pieces = jnp.stack(pieces)
    return jnp.stack([lax.dynamic_index_in_dim(pieces, (m + block) % 4, 0, keepdims=False) for m in range(3)])


ORDERS = (("y", "z", "x"), ("z", "x", "y"), ("x", "y", "z"))
SWAP = ((0, 1), (1, 0))
STEPS = ((1, -1), (-1, 1), (2, 2))


def exchange(value, move):
    pairs = []
    for place in itertools.product(range(4), range(4), range(4), range(2)):
        ends = [linear(y, x % 2, c, z, x // 2) for x, y, z, c in (place, move(*place))]
        pairs.append(tuple(ends))
    return lax.ppermute(value, AXES, pairs)


def ring_exchange(value, axis, signs):
    def move(x, y, z, c):
        at = {"x": x, "y": y, "z": z}
        at[axis] = (at[axis] + signs[c]) % 4
        return at["x"], at["y"], at["z"], c

    return exchange(value, move)


def ring_place(axis):
    if axis == "x":
        return lax.axis_index("xh") * 2 + lax.axis_index("xl")
    return lax.axis_index(axis)


def reduce_stage(buffer, axis, core):
    place = ring_place(axis)
    blocks = buffer.reshape(4, buffer.shape[0] // 4, buffer.shape[1])
    total = lax.dynamic_index_in_dim(blocks, place, 0, keepdims=False).astype(f32)
    for signs in STEPS:
        step = jnp.where(core == 0, signs[0], signs[1])
        block = lax.dynamic_index_in_dim(blocks, (place + step) % 4, 0, keepdims=False)
        total = total + ring_exchange(block, axis, signs).astype(f32)
    return total.astype(bf16)


def gather_stage(block, axis, core):
    place = ring_place(axis)
    whole = jnp.zeros((4,) + block.shape, block.dtype)
    whole = lax.dynamic_update_index_in_dim(whole, block, place, 0)
    for signs in STEPS:
        step = jnp.where(core == 0, signs[0], signs[1])
        other = ring_exchange(block, axis, signs)
        whole = lax.dynamic_update_index_in_dim(whole, other, (place - step) % 4, 0)
    return whole.reshape(4 * block.shape[0], block.shape[1])


def sum_everywhere(grads, core):
    rows = grads.shape[0] // 3
    halves = grads.reshape(3, 2, rows // 2, grads.shape[1])
    parts = []
    for part in range(3):
        mine = lax.dynamic_index_in_dim(halves[part], core, 0, keepdims=False)
        other = lax.dynamic_index_in_dim(halves[part], 1 - core, 0, keepdims=False)
        parts.append((mine.astype(f32) + lax.ppermute(other, "c", SWAP).astype(f32)).astype(bf16))
    for stage in range(3):
        parts = [reduce_stage(parts[part], ORDERS[part][stage], core) for part in range(3)]
    for stage in (2, 1, 0):
        parts = [gather_stage(parts[part], ORDERS[part][stage], core) for part in range(3)]
    result = []
    for mine in parts:
        other = lax.ppermute(mine, "c", SWAP)
        result.append(jnp.where(core == 0, mine, other))
        result.append(jnp.where(core == 0, other, mine))
    return jnp.concatenate(result, axis=0)


def sum_small(values):
    values = values + lax.ppermute(values, "c", SWAP)
    for axis in "zyx":
        for bit in (1, 2):
            flip = lambda x, y, z, c: tuple(v ^ bit if n == axis else v for n, v in zip("xyz", (x, y, z))) + (c,)
            values = values + exchange(values, flip)
    return values


def body(
    tokens, view_counts, ln1_gain, ln1_shift, qkv_weight, query_bias, value_bias, out_weight, out_bias,
    ln2_gain, ln2_shift, up_weight, up_bias, down_weight, down_bias, cotangent,
):
    core, z, xh = lax.axis_index("c"), lax.axis_index("z"), lax.axis_index("xh")
    block = 2 * z + xh
    scene = jnp.minimum(z, 2)

    x = to_scene(tokens, block)
    views = view_counts.astype(f32)
    views_other = lax.ppermute(views, "c", SWAP)
    views = lax.dynamic_index_in_dim(jnp.where(core == xh, views, views_other), scene, 0, keepdims=False)
    g = to_scene(cotangent, block)

    slot = jnp.arange(ROWS, dtype=jnp.int32) // BLK
    inside = jnp.arange(ROWS, dtype=jnp.int32) % BLK
    offset = (slot - z) % 4 * BLK + inside
    place = jnp.concatenate([offset + core * ROWS, offset + (1 - core) * ROWS])
    usable = (place.astype(f32) < views * VIEW_TOK) | (place >= VIEWS_MAX * VIEW_TOK)
    mask = jnp.broadcast_to(jnp.where(usable, 0.0, masked_score).astype(bf16)[:, None], (KEYS, LANES))

    source = x.astype(f32)
    centred = source - jnp.mean(source, axis=1, keepdims=True)
    rstd = lax.rsqrt(jnp.mean(centred * centred, axis=1, keepdims=True) + epsilon)
    xhat = centred * rstd
    normed = (xhat * ln1_gain + ln1_shift).astype(bf16)
    qkv_bias = jnp.concatenate([query_bias, jnp.zeros((D,), f32), value_bias])
    joined = (jnp.dot(normed, qkv_weight, preferred_element_type=f32) + qkv_bias).astype(bf16)
    sibling = lax.ppermute(joined[:, D:], "c", SWAP)
    weights, heads_out, linv, attended = attention_forward(joined, sibling, mask)

    vecs = jnp.concatenate([jnp.stack([out_bias, ln2_gain, ln2_shift, down_bias]), jnp.zeros((4, D), f32)])
    output, grad_hidden, grad_att, d_out, d_up, d_down, vec_grads, up_b_grad = feed_forward(
        attended, x, g, out_weight, vecs, up_bias.reshape(NF, 1, FCHUNK), up_weight, down_weight
    )
    output = from_scene(output, block)
    ff_sum = sum_everywhere(jnp.concatenate([d_up, d_down], axis=0), core)

    grad_q, grad_k, grad_v, grad_k_other, grad_v_other = attention_backward(
        joined, sibling, weights, heads_out, linv, grad_att
    )
    swapped = lax.ppermute(jnp.concatenate([grad_k_other, grad_v_other], axis=1), "c", SWAP).astype(f32)
    grad_k = (grad_k + swapped[:, :D]).astype(bf16)
    grad_v = (grad_v + swapped[:, D:]).astype(bf16)

    d_qkv = [
        lax.dot_general(normed, part, (((0,), (0,)), ((), ())), preferred_element_type=f32).astype(bf16)
        for part in (grad_q, grad_k, grad_v)
    ]
    grad_joined = jnp.concatenate([grad_q, grad_k, grad_v], axis=1)
    grad_normed = lax.dot_general(grad_joined, qkv_weight, (((1,), (1,)), ((), ())), preferred_element_type=f32)
    gx = grad_normed * ln1_gain
    mean1 = jnp.mean(gx, axis=1, keepdims=True)
    mean2 = jnp.mean(gx * xhat, axis=1, keepdims=True)
    input_grad = (grad_hidden + rstd * (gx - mean1 - xhat * mean2)).astype(bf16)
    input_grad = from_scene(input_grad, block)
    small = jnp.concatenate(
        [
            vec_grads[0], vec_grads[1], vec_grads[2], vec_grads[3],
            jnp.sum(grad_normed * xhat, axis=0), jnp.sum(grad_normed, axis=0),
            jnp.sum(grad_q.astype(f32), axis=0), jnp.sum(grad_v.astype(f32), axis=0),
            up_b_grad.reshape(FF),
        ]
    ).reshape(-1, LANES)
    small = sum_small(small).reshape(-1)
    vector = lambda i: small[i * D : (i + 1) * D]
    qkvo_sum = sum_everywhere(jnp.concatenate(d_qkv + [d_out], axis=0), core)

    blocks = lambda a, n: jnp.concatenate([a[i * D : (i + 1) * D] for i in range(n)], axis=1).astype(f32)
    return (
        output, input_grad,
        vector(4), vector(5), blocks(qkvo_sum[: 3 * D], 3), vector(6), vector(7),
        qkvo_sum[3 * D :].astype(f32), vector(0), vector(1), vector(2),
        blocks(ff_sum[:FF], 4), small[8 * D :], ff_sum[FF:].astype(f32), vector(3),
    )


def solution(mesh):
    fine = Mesh(mesh.devices.reshape(4, 2, 2, 4, 2), AXES)
    rows = P(("y", "xl", "c"), ("z", "xh"), None)
    placed = (rows, P(("y", "xl", "c"))) + (P(),) * 13 + (rows,)
    return jax.shard_map(
        body, mesh=fine, in_specs=placed, out_specs=(rows, rows) + (P(),) * 13, check_vma=False
    )
```

```python
import itertools
import math

import jax
import jax.numpy as jnp
from jax import lax
from jax.experimental import pallas as pl
from jax.experimental.pallas import tpu as pltpu
from jax.sharding import Mesh
from jax.sharding import PartitionSpec as P

HEADS = 12
HEAD_DIM = 64
VIEW_TOK = 128
VIEWS_MAX = 8
D = 768
FF = 3072
BLK = 144
SLOTS = 4
ROWS = BLK * SLOTS
KEYS = 2 * ROWS
PAIRS = HEADS // 2
LANES = 128
FCHUNK = 768
NF = FF // FCHUNK

bf16 = jnp.bfloat16
f32 = jnp.float32
epsilon = 1e-05
masked_score = -1e30
GELU_C = math.sqrt(2.0 / math.pi)
GELU_A = 0.044715

AXES = ("y", "xl", "c", "z", "xh")
VMEM_LIMIT = 60 * 1024 * 1024


def mm(a, b):
    return lax.dot_general(a, b, (((1,), (0,)), ((), ())), preferred_element_type=f32)


def mm_nt(a, b):
    return lax.dot_general(a, b, (((1,), (1,)), ((), ())), preferred_element_type=f32)


def mm_tn(a, b):
    return lax.dot_general(a, b, (((0,), (0,)), ((), ())), preferred_element_type=f32)


def lane_row(at, first, last):
    lane = lax.broadcasted_iota(jnp.int32, (1, LANES), 1)
    return jnp.where((lane >= first) & (lane < last), 1.0, 0.0).astype(at)


def attention_forward_kernel(q_ref, ko_ref, vo_ref, ks_ref, vs_ref, mask_ref, p_ref, o_ref, linv_ref, att_ref):
    half = [lane_row(bf16, 0, 64), lane_row(bf16, 64, 128)]
    unit = [lane_row(bf16, 64, 65), lane_row(bf16, 0, 1)]
    q = q_ref[...]
    k = jnp.concatenate([ko_ref[...], ks_ref[...]], axis=0)
    v = jnp.concatenate([vo_ref[...], vs_ref[...]], axis=0)
    mask = mask_ref[...]
    lane = lax.broadcasted_iota(jnp.int32, (BLK, LANES), 1)
    q_now = [q * half[h] + unit[h] for h in range(2)]
    k_now = [k * half[h] + mask * unit[h] for h in range(2)]
    v_now = [v * half[h] + unit[h] for h in range(2)]
    for s in range(SLOTS):
        rows = slice(s * BLK, (s + 1) * BLK)
        outs, invs = [], []
        for h in range(2):
            scores = mm_nt(q_now[h][rows], k_now[h])
            top = jnp.max(scores, axis=1, keepdims=True)
            weights = jnp.exp((scores - top) * 0.125).astype(bf16)
            p_ref[h, rows, :] = weights
            out = mm(weights, v_now[h])
            total = out[:, 64:65] if h == 0 else out[:, 0:1]
            inv = 1.0 / total
            outs.append(out * inv)
            invs.append(jnp.broadcast_to(inv, (BLK, LANES)))
        out = jnp.where(lane < 64, outs[0], outs[1])
        o_ref[rows, :] = out
        att_ref[rows, :] = out.astype(bf16)
        linv_ref[rows, :] = jnp.where(lane < 64, invs[0], invs[1])


def attention_forward(joined, sibling, mask):
    col = lambda first: pl.BlockSpec((ROWS, LANES), lambda i, f=first: (0, f + i))
    return pl.pallas_call(
        attention_forward_kernel,
        grid=(PAIRS,),
        in_specs=[
            col(0), col(PAIRS), col(2 * PAIRS), col(0), col(PAIRS),
            pl.BlockSpec((KEYS, LANES), lambda i: (0, 0)),
        ],
        out_specs=[
            pl.BlockSpec((2, ROWS, KEYS), lambda i: (i, 0, 0)),
            col(0), col(0), col(0),
        ],
        out_shape=[
            jax.ShapeDtypeStruct((HEADS, ROWS, KEYS), bf16),
            jax.ShapeDtypeStruct((ROWS, D), f32),
            jax.ShapeDtypeStruct((ROWS, D), f32),
            jax.ShapeDtypeStruct((ROWS, D), bf16),
        ],
        compiler_params=pltpu.CompilerParams(vmem_limit_bytes=VMEM_LIMIT),
        cost_estimate=pl.CostEstimate(flops=16 * ROWS * KEYS * D, bytes_accessed=20_000_000, transcendentals=HEADS * ROWS * KEYS),
        name="attention_forward",
    )(joined, joined, joined, sibling, sibling, mask)


def attention_backward_kernel(
    q_ref, ko_ref, vo_ref, ks_ref, vs_ref, p_ref, o_ref, linv_ref, g_ref,
    gq_ref, gko_ref, gvo_ref, gks_ref, gvs_ref,
):
    half = [lane_row(bf16, 0, 64), lane_row(bf16, 64, 128)]
    two = [lane_row(bf16, 64, 66), lane_row(bf16, 0, 2)]
    q = q_ref[...]
    k = jnp.concatenate([ko_ref[...], ks_ref[...]], axis=0)
    v = jnp.concatenate([vo_ref[...], vs_ref[...]], axis=0)
    v_now = [v * half[h] + two[h] for h in range(2)]
    lane = lax.broadcasted_iota(jnp.int32, (ROWS, LANES), 1)
    gs = g_ref[...].astype(f32) * linv_ref[...]
    prod = gs * o_ref[...]
    gq, gk, gv = [], [], []
    for h in range(2):
        mine = (lane < 64) if h == 0 else (lane >= 64)
        base = 64 if h == 0 else 0
        delta = jnp.sum(jnp.where(mine, prod, 0.0), axis=1, keepdims=True)
        high = delta.astype(bf16).astype(f32)
        g_aug = jnp.where(
            mine, gs, jnp.where(lane == base, -high, jnp.where(lane == base + 1, high - delta, 0.0))
        ).astype(bf16)
        weights = p_ref[h]
        diff = mm_nt(g_aug, v_now[h])
        gscore = (weights.astype(f32) * diff).astype(bf16)
        gv.append(mm_tn(weights, g_aug))
        gk.append(mm_tn(gscore, q))
        gq.append(mm(gscore, k))
    gq_ref[...] = (jnp.where(lane < 64, gq[0], gq[1]) * 0.125).astype(bf16)
    lane_k = lax.broadcasted_iota(jnp.int32, (KEYS, LANES), 1)
    gk_all = jnp.where(lane_k < 64, gk[0], gk[1]) * 0.125
    gv_all = jnp.where(lane_k < 64, gv[0], gv[1])
    gko_ref[...] = gk_all[:ROWS]
    gvo_ref[...] = gv_all[:ROWS]
    gks_ref[...] = gk_all[ROWS:].astype(bf16)
    gvs_ref[...] = gv_all[ROWS:].astype(bf16)


def attention_backward(joined, sibling, weights, heads_out, linv, grad_att):
    col = lambda first: pl.BlockSpec((ROWS, LANES), lambda i, f=first: (0, f + i))
    return pl.pallas_call(
        attention_backward_kernel,
        grid=(PAIRS,),
        in_specs=[
            col(0), col(PAIRS), col(2 * PAIRS), col(0), col(PAIRS),
            pl.BlockSpec((2, ROWS, KEYS), lambda i: (i, 0, 0)),
            col(0), col(0), col(0),
        ],
        out_specs=[col(0), col(0), col(0), col(0), col(0)],
        out_shape=[
            jax.ShapeDtypeStruct((ROWS, D), bf16),
            jax.ShapeDtypeStruct((ROWS, D), f32),
            jax.ShapeDtypeStruct((ROWS, D), f32),
            jax.ShapeDtypeStruct((ROWS, D), bf16),
            jax.ShapeDtypeStruct((ROWS, D), bf16),
        ],
        compiler_params=pltpu.CompilerParams(vmem_limit_bytes=VMEM_LIMIT),
        cost_estimate=pl.CostEstimate(flops=32 * ROWS * KEYS * D, bytes_accessed=25_000_000, transcendentals=0),
        name="attention_backward",
    )(joined, joined, joined, sibling, sibling, weights, heads_out, linv, grad_att)


def feed_forward_kernel(
    att_ref, x_ref, g_ref, ow_ref, vec_ref, upb_ref, up_ref, down_ref,
    out_ref, gh_ref, gatt_ref, dout_ref, dup_ref, ddown_ref, vecg_ref, upbg_ref,
    hidden, xhat, rstd_s, normed2, y_acc, gn_acc,
):
    f = pl.program_id(0)
    out_bias, gain, shift, down_bias = (vec_ref[r : r + 1, :] for r in range(4))

    @pl.when(f == 0)
    def _():
        h = x_ref[...].astype(f32) + mm(att_ref[...], ow_ref[...]) + out_bias
        hidden[...] = h
        centred = h - jnp.mean(h, axis=1, keepdims=True)
        rstd = lax.rsqrt(jnp.mean(centred * centred, axis=1, keepdims=True) + epsilon)
        xh = centred * rstd
        xhat[...] = xh
        rstd_s[...] = jnp.broadcast_to(rstd, (ROWS, LANES))
        normed2[...] = (xh * gain + shift).astype(bf16)
        y_acc[...] = jnp.zeros_like(y_acc)
        gn_acc[...] = jnp.zeros_like(gn_acc)

    g = g_ref[...]
    n2 = normed2[...]
    u = mm(n2, up_ref[...]) + upb_ref[0]
    ga = mm_nt(g, down_ref[...])
    u2 = u * u
    t = jnp.tanh(u * (GELU_C + (GELU_C * GELU_A) * u2))
    hp = 0.5 + 0.5 * t
    active = (u * hp).astype(bf16)
    slope = hp + (0.5 * u) * (1.0 - t * t) * (GELU_C + (3.0 * GELU_C * GELU_A) * u2)
    gu = (ga * slope).astype(bf16)
    y_acc[...] += mm(active, down_ref[...])
    gn_acc[...] += mm_nt(gu, up_ref[...])
    ddown_ref[...] = mm_tn(active, g).astype(bf16)
    dup_ref[...] = mm_tn(n2, gu).astype(bf16)
    upbg_ref[0] = jnp.sum(gu.astype(f32), axis=0, keepdims=True)

    @pl.when(f == NF - 1)
    def _():
        out_ref[...] = (hidden[...] + y_acc[...] + down_bias).astype(bf16)
        gn = gn_acc[...]
        xh = xhat[...]
        gf = g_ref[...].astype(f32)
        vecg_ref[...] = jnp.zeros_like(vecg_ref)
        vecg_ref[1:2, :] = jnp.sum(gn * xh, axis=0, keepdims=True)
        vecg_ref[2:3, :] = jnp.sum(gn, axis=0, keepdims=True)
        vecg_ref[3:4, :] = jnp.sum(gf, axis=0, keepdims=True)
        gx = gn * gain
        mean1 = jnp.mean(gx, axis=1, keepdims=True)
        mean2 = jnp.mean(gx * xh, axis=1, keepdims=True)
        gh = gf + rstd_s[:, 0:1] * (gx - mean1 - xh * mean2)
        gh_ref[...] = gh
        vecg_ref[0:1, :] = jnp.sum(gh, axis=0, keepdims=True)
        gb = gh.astype(bf16)
        dout_ref[...] = mm_tn(att_ref[...], gb).astype(bf16)
        gatt_ref[...] = mm_nt(gb, ow_ref[...]).astype(bf16)


def feed_forward(attended, both, out_w, vecs, up_b, up_w, down_w):
    whole = lambda shape: pl.BlockSpec(shape, lambda f: (0,) * len(shape))
    return pl.pallas_call(
        feed_forward_kernel,
        grid=(NF,),
        in_specs=[
            whole((ROWS, D)),
            pl.BlockSpec((ROWS, D), lambda f: (0, 0)),
            pl.BlockSpec((ROWS, D), lambda f: (0, 1)),
            whole((D, D)), whole((8, D)),
            pl.BlockSpec((1, 1, FCHUNK), lambda f: (f, 0, 0)),
            pl.BlockSpec((D, FCHUNK), lambda f: (0, f)),
            pl.BlockSpec((FCHUNK, D), lambda f: (f, 0)),
        ],
        out_specs=[
            whole((ROWS, D)), whole((ROWS, D)), whole((ROWS, D)), whole((D, D)),
            pl.BlockSpec((D, FCHUNK), lambda f: (f, 0)),
            pl.BlockSpec((FCHUNK, D), lambda f: (f, 0)),
            whole((8, D)),
            pl.BlockSpec((1, 1, FCHUNK), lambda f: (f, 0, 0)),
        ],
        out_shape=[
            jax.ShapeDtypeStruct((ROWS, D), bf16),
            jax.ShapeDtypeStruct((ROWS, D), f32),
            jax.ShapeDtypeStruct((ROWS, D), bf16),
            jax.ShapeDtypeStruct((D, D), bf16),
            jax.ShapeDtypeStruct((NF * D, FCHUNK), bf16),
            jax.ShapeDtypeStruct((FF, D), bf16),
            jax.ShapeDtypeStruct((8, D), f32),
            jax.ShapeDtypeStruct((NF, 1, FCHUNK), f32),
        ],
        scratch_shapes=[
            pltpu.VMEM((ROWS, D), f32),
            pltpu.VMEM((ROWS, D), f32),
            pltpu.VMEM((ROWS, LANES), f32),
            pltpu.VMEM((ROWS, D), bf16),
            pltpu.VMEM((ROWS, D), f32),
            pltpu.VMEM((ROWS, D), f32),
        ],
        compiler_params=pltpu.CompilerParams(vmem_limit_bytes=VMEM_LIMIT),
        cost_estimate=pl.CostEstimate(flops=12 * ROWS * D * FF, bytes_accessed=30_000_000, transcendentals=ROWS * FF),
        name="feed_forward",
    )(attended, both, both, out_w, vecs, up_b, up_w, down_w)


def place_kernel(core_ref, mine_ref, other_ref, *out_refs):
    step = pl.program_id(0)
    lower = pl.num_programs(0) // 2
    from_mine = (step >= lower).astype(jnp.int32) == core_ref[0]
    for index, out_ref in enumerate(out_refs):
        count = pl.num_programs(0)
        first = 0 if index == 0 else count - 1
        last = count - 1 if index == len(out_refs) - 1 else count - 2

        @pl.when((step >= first) & (step <= last) & from_mine)
        def _():
            out_ref[...] = mine_ref[...].astype(f32)

        @pl.when((step >= first) & (step <= last) & jnp.logical_not(from_mine))
        def _():
            out_ref[...] = other_ref[...].astype(f32)


def place_rows(core, mine, other):
    half = mine.shape[0] // D
    source = pl.BlockSpec((D, D), lambda i, core_ref: (i % half, 0))
    return pl.pallas_call(
        place_kernel,
        grid_spec=pltpu.PrefetchScalarGridSpec(
            num_scalar_prefetch=1,
            grid=(2 * half,),
            in_specs=[source, source],
            out_specs=pl.BlockSpec((D, D), lambda i, core_ref: (i, 0)),
        ),
        out_shape=jax.ShapeDtypeStruct((2 * mine.shape[0], D), f32),
        compiler_params=pltpu.CompilerParams(vmem_limit_bytes=VMEM_LIMIT),
        name="place_rows",
    )(core, mine, other)


def place_columns(core, mine, other):
    half = mine.shape[0] // D
    source = pl.BlockSpec((D, D), lambda i, core_ref: (i % half, 0))
    return pl.pallas_call(
        place_kernel,
        grid_spec=pltpu.PrefetchScalarGridSpec(
            num_scalar_prefetch=1,
            grid=(2 * half,),
            in_specs=[source, source],
            out_specs=pl.BlockSpec((D, D), lambda i, core_ref: (0, i)),
        ),
        out_shape=jax.ShapeDtypeStruct((D, 2 * mine.shape[0]), f32),
        compiler_params=pltpu.CompilerParams(vmem_limit_bytes=VMEM_LIMIT),
        name="place_columns",
    )(core, mine, other)


def place_qkvo(core, mine, other):
    half = mine.shape[0] // D
    source = pl.BlockSpec((D, D), lambda i, core_ref: (i % half, 0))
    return pl.pallas_call(
        place_kernel,
        grid_spec=pltpu.PrefetchScalarGridSpec(
            num_scalar_prefetch=1,
            grid=(4,),
            in_specs=[source, source],
            out_specs=[
                pl.BlockSpec((D, D), lambda i, core_ref: (0, jnp.minimum(i, 2))),
                pl.BlockSpec((D, D), lambda i, core_ref: (0, 0)),
            ],
        ),
        out_shape=[jax.ShapeDtypeStruct((D, 3 * D), f32), jax.ShapeDtypeStruct((D, D), f32)],
        compiler_params=pltpu.CompilerParams(vmem_limit_bytes=VMEM_LIMIT),
        name="place_qkvo",
    )(core, mine, other)


def linear(y, xl, c, z, xh):
    return (((y * 2 + xl) * 2 + c) * 4 + z) * 2 + xh


def scene_pairs(slot):
    pairs = []
    for y, xl, z, xh in itertools.product(range(4), range(2), range(4), range(2)):
        block = 2 * z + xh
        scene = (slot - block) % 4
        if scene < 3:
            for c in range(2):
                pairs.append((linear(y, xl, c, z, xh), linear(y, xl, block // 4, scene, c)))
    return pairs


def to_scene(values, block):
    pieces = []
    for slot in range(SLOTS):
        scene = jnp.minimum((slot - block) % 4, 2)
        pieces.append(lax.ppermute(lax.dynamic_index_in_dim(values, scene, 0, keepdims=False), AXES, scene_pairs(slot)))
    return pieces


def from_scene(values, block):
    pieces = []
    for slot in range(SLOTS):
        back = [(target, source) for source, target in scene_pairs(slot)]
        pieces.append(lax.ppermute(values[slot * BLK : (slot + 1) * BLK], AXES, back))
    pieces = jnp.stack(pieces)
    return jnp.stack([lax.dynamic_index_in_dim(pieces, (m + block) % 4, 0, keepdims=False) for m in range(3)])


SWAP = ((0, 1), (1, 0))
CHIPS = ("y", "xh", "xl", "z")
MASKS = ((1, 3), (3, 1))


def exchange(value, move):
    pairs = []
    for place in itertools.product(range(4), range(4), range(4), range(2)):
        ends = [linear(y, x % 2, c, z, x // 2) for x, y, z, c in (place, move(*place))]
        pairs.append(tuple(ends))
    return lax.ppermute(value, AXES, pairs)


def ring_exchange(value, axis, step):
    def move(x, y, z, c):
        at = {"x": x, "y": y, "z": z}
        at[axis] = at[axis] ^ MASKS[c][step]
        return at["x"], at["y"], at["z"], c

    return exchange(value, move)


def ring_place(axis):
    if axis == "x":
        return lax.axis_index("xh") * 2 + lax.axis_index("xl")
    return lax.axis_index(axis)


def take(blocks, dim, index):
    return lax.dynamic_slice_in_dim(blocks, index, 1, dim)


def halve_stage(blocks, dim, axis, core):
    place = ring_place(axis)
    first = jnp.where(core == 0, 1, 3)
    second = 4 - first
    away = jnp.concatenate([take(blocks, dim, place ^ first), take(blocks, dim, place ^ 2)], axis=dim)
    keep = jnp.concatenate([take(blocks, dim, place), take(blocks, dim, place ^ second)], axis=dim)
    keep = keep + ring_exchange(away, axis, 0)
    return lax.slice_in_dim(keep, 0, 1, axis=dim) + ring_exchange(lax.slice_in_dim(keep, 1, 2, axis=dim), axis, 1)


def chip_gather(chunk):
    return lax.all_gather(chunk, CHIPS, axis=0, tiled=True)


def core_half(values, core):
    half = values.shape[0] // 2
    return lax.dynamic_slice_in_dim(values, core * half, half, 0)


def sum_ff(d_up, d_down, core):
    away = jnp.concatenate([core_half(d_up, 1 - core), core_half(d_down, 1 - core)], axis=0)
    other = lax.ppermute(away, "c", SWAP)
    half = FF // 2
    up = (core_half(d_up, core) + other[:half]).reshape(4, 4, 4, half // 64, D)
    down = (core_half(d_down, core) + other[half:]).reshape(4, 4, 4, half // 64, D)
    dims = {"y": 0, "x": 1, "z": 2}
    for axis_up, axis_down in zip("yxz", "zxy"):
        up = halve_stage(up, dims[axis_up], axis_up, core)
        down = halve_stage(down, dims[axis_down], axis_down, core)
    up = chip_gather(up.reshape(half // 64, D))
    down = chip_gather(down.reshape(half // 64, D))
    return up, down


def sum_qkvo(grads, core):
    rows = grads.shape[0] // 2
    mine = core_half(grads, core) + lax.ppermute(core_half(grads, 1 - core), "c", SWAP)
    terms = lax.all_to_all(mine.reshape(64, rows // 64, D), CHIPS, 0, 0)
    return chip_gather(jnp.sum(terms.astype(f32), axis=0).astype(bf16))


def sum_small(values):
    values = values + lax.ppermute(values, "c", SWAP)
    for axis in "zyx":
        for bit in (1, 2):
            flip = lambda x, y, z, c: tuple(v ^ bit if n == axis else v for n, v in zip("xyz", (x, y, z))) + (c,)
            values = values + exchange(values, flip)
    return values


def body(
    tokens, view_counts, ln1_gain, ln1_shift, qkv_weight, query_bias, value_bias, out_weight, out_bias,
    ln2_gain, ln2_shift, up_weight, up_bias, down_weight, down_bias, cotangent,
):
    core, z, xh = lax.axis_index("c"), lax.axis_index("z"), lax.axis_index("xh")
    block = 2 * z + xh
    scene = jnp.minimum(z, 2)

    views = jnp.broadcast_to(view_counts.astype(bf16)[:, None, None], (3, BLK, LANES))
    pieces = to_scene(jnp.concatenate([tokens, cotangent, views], axis=2), block)
    both = jnp.concatenate([piece[:, : 2 * D] for piece in pieces], axis=0)
    views = pieces[0][0, 2 * D].astype(f32)
    x = both[:, :D]

    slot = jnp.arange(ROWS, dtype=jnp.int32) // BLK
    inside = jnp.arange(ROWS, dtype=jnp.int32) % BLK
    offset = (slot - z) % 4 * BLK + inside
    place = jnp.concatenate([offset + core * ROWS, offset + (1 - core) * ROWS])
    usable = (place.astype(f32) < views * VIEW_TOK) | (place >= VIEWS_MAX * VIEW_TOK)
    mask = jnp.broadcast_to(jnp.where(usable, 0.0, masked_score).astype(bf16)[:, None], (KEYS, LANES))

    source = x.astype(f32)
    centred = source - jnp.mean(source, axis=1, keepdims=True)
    rstd = lax.rsqrt(jnp.mean(centred * centred, axis=1, keepdims=True) + epsilon)
    xhat = centred * rstd
    normed = (xhat * ln1_gain + ln1_shift).astype(bf16)
    qkv_bias = jnp.concatenate([query_bias, jnp.zeros((D,), f32), value_bias])
    joined = (jnp.dot(normed, qkv_weight, preferred_element_type=f32) + qkv_bias).astype(bf16)
    sibling = lax.ppermute(joined[:, D:], "c", SWAP)
    weights, heads_out, linv, attended = attention_forward(joined, sibling, mask)

    vecs = jnp.concatenate([jnp.stack([out_bias, ln2_gain, ln2_shift, down_bias]), jnp.zeros((4, D), f32)])
    output, grad_hidden, grad_att, d_out, d_up, d_down, vec_grads, up_b_grad = feed_forward(
        attended, both, out_weight, vecs, up_bias.reshape(NF, 1, FCHUNK), up_weight, down_weight
    )
    output = from_scene(output, block)
    up_sum, down_sum = sum_ff(d_up, d_down, core)

    grad_q, grad_k, grad_v, grad_k_other, grad_v_other = attention_backward(
        joined, sibling, weights, heads_out, linv, grad_att
    )
    swapped = lax.ppermute(jnp.concatenate([grad_k_other, grad_v_other], axis=1), "c", SWAP).astype(f32)
    grad_k = (grad_k + swapped[:, :D]).astype(bf16)
    grad_v = (grad_v + swapped[:, D:]).astype(bf16)

    d_qkv = [
        lax.dot_general(normed, part, (((0,), (0,)), ((), ())), preferred_element_type=f32).astype(bf16)
        for part in (grad_q, grad_k, grad_v)
    ]
    grad_joined = jnp.concatenate([grad_q, grad_k, grad_v], axis=1)
    grad_normed = lax.dot_general(grad_joined, qkv_weight, (((1,), (1,)), ((), ())), preferred_element_type=f32)
    gx = grad_normed * ln1_gain
    mean1 = jnp.mean(gx, axis=1, keepdims=True)
    mean2 = jnp.mean(gx * xhat, axis=1, keepdims=True)
    input_grad = (grad_hidden + rstd * (gx - mean1 - xhat * mean2)).astype(bf16)
    input_grad = from_scene(input_grad, block)
    small = jnp.concatenate(
        [
            vec_grads[0], vec_grads[1], vec_grads[2], vec_grads[3],
            jnp.sum(grad_normed * xhat, axis=0), jnp.sum(grad_normed, axis=0),
            jnp.sum(grad_q.astype(f32), axis=0), jnp.sum(grad_v.astype(f32), axis=0),
            up_b_grad.reshape(FF),
        ]
    ).reshape(-1, LANES)
    small = sum_small(small).reshape(-1)
    vector = lambda i: small[i * D : (i + 1) * D]
    qkvo_sum = sum_qkvo(jnp.concatenate(d_qkv + [d_out], axis=0), core)
    up_other, down_other, qkvo_other = (lax.ppermute(v, "c", SWAP) for v in (up_sum, down_sum, qkvo_sum))
    which = core.astype(jnp.int32).reshape(1)
    d_qkv, d_out = place_qkvo(which, qkvo_sum, qkvo_other)
    return (
        output, input_grad, vector(4), vector(5), d_qkv, vector(6), vector(7), d_out,
        vector(0), vector(1), vector(2), place_columns(which, up_sum, up_other), small[8 * D :],
        place_rows(which, down_sum, down_other), vector(3),
    )


def solution(mesh):
    fine = Mesh(mesh.devices.reshape(4, 2, 2, 4, 2), AXES)
    rows = P(("y", "xl", "c"), ("z", "xh"), None)
    placed = (rows, P(("y", "xl", "c"))) + (P(),) * 13 + (rows,)
    return jax.shard_map(
        body, mesh=fine, in_specs=placed, out_specs=(rows, rows) + (P(),) * 13, check_vma=False
    )
```

```python
import functools
import itertools
import math

import jax
import jax.numpy as jnp
from jax import lax
from jax.experimental import pallas as pl
from jax.experimental.pallas import tpu as pltpu
from jax.sharding import Mesh
from jax.sharding import PartitionSpec as P

HEADS = 12
HEAD_DIM = 64
VIEW_TOK = 128
VIEWS_MAX = 8
D = 768
FF = 3072
BLK = 144
SLOTS = 4
ROWS = BLK * SLOTS
KEYS = 2 * ROWS
PAIRS = HEADS // 2
LANES = 128
FCHUNK = 768
QUARTER = D // 4
NF = FF // FCHUNK

bf16 = jnp.bfloat16
f32 = jnp.float32
epsilon = 1e-05
masked_score = -1e30
GELU_C = math.sqrt(2.0 / math.pi)
GELU_A = 0.044715

AXES = ("y", "xl", "c", "z", "xh")
VMEM_LIMIT = 60 * 1024 * 1024


def mm(a, b):
    return lax.dot_general(a, b, (((1,), (0,)), ((), ())), preferred_element_type=f32)


def mm_nt(a, b):
    return lax.dot_general(a, b, (((1,), (1,)), ((), ())), preferred_element_type=f32)


def mm_tn(a, b):
    return lax.dot_general(a, b, (((0,), (0,)), ((), ())), preferred_element_type=f32)


def lane_row(at, first, last):
    lane = lax.broadcasted_iota(jnp.int32, (1, LANES), 1)
    return jnp.where((lane >= first) & (lane < last), 1.0, 0.0).astype(at)


def attention_forward_kernel(q_ref, ko_ref, vo_ref, ks_ref, vs_ref, mask_ref, p_ref, o_ref, linv_ref, att_ref):
    half = [lane_row(bf16, 0, 64), lane_row(bf16, 64, 128)]
    unit = [lane_row(bf16, 64, 65), lane_row(bf16, 0, 1)]
    q = q_ref[...]
    k = jnp.concatenate([ko_ref[...], ks_ref[...]], axis=0)
    v = jnp.concatenate([vo_ref[...], vs_ref[...]], axis=0)
    mask = mask_ref[...]
    lane = lax.broadcasted_iota(jnp.int32, (BLK, LANES), 1)
    q_now = [q * half[h] + unit[h] for h in range(2)]
    k_now = [k * half[h] + mask * unit[h] for h in range(2)]
    v_now = [v * half[h] + unit[h] for h in range(2)]
    for s in range(SLOTS):
        rows = slice(s * BLK, (s + 1) * BLK)
        outs, invs = [], []
        for h in range(2):
            scores = mm_nt(q_now[h][rows], k_now[h])
            top = jnp.max(scores, axis=1, keepdims=True)
            weights = jnp.exp((scores - top) * 0.125).astype(bf16)
            p_ref[h, rows, :] = weights
            out = mm(weights, v_now[h])
            total = out[:, 64:65] if h == 0 else out[:, 0:1]
            inv = 1.0 / total
            outs.append(out * inv)
            invs.append(jnp.broadcast_to(inv, (BLK, LANES)))
        out = jnp.where(lane < 64, outs[0], outs[1])
        o_ref[rows, :] = out
        att_ref[rows, :] = out.astype(bf16)
        linv_ref[rows, :] = jnp.where(lane < 64, invs[0], invs[1])


def attention_forward(joined, sibling, mask):
    col = lambda first: pl.BlockSpec((ROWS, LANES), lambda i, f=first: (0, f + i))
    return pl.pallas_call(
        attention_forward_kernel,
        grid=(PAIRS,),
        in_specs=[
            col(0), col(PAIRS), col(2 * PAIRS), col(0), col(PAIRS),
            pl.BlockSpec((KEYS, LANES), lambda i: (0, 0)),
        ],
        out_specs=[
            pl.BlockSpec((2, ROWS, KEYS), lambda i: (i, 0, 0)),
            col(0), col(0), col(0),
        ],
        out_shape=[
            jax.ShapeDtypeStruct((HEADS, ROWS, KEYS), bf16),
            jax.ShapeDtypeStruct((ROWS, D), f32),
            jax.ShapeDtypeStruct((ROWS, D), f32),
            jax.ShapeDtypeStruct((ROWS, D), bf16),
        ],
        compiler_params=pltpu.CompilerParams(vmem_limit_bytes=VMEM_LIMIT),
        cost_estimate=pl.CostEstimate(flops=16 * ROWS * KEYS * D, bytes_accessed=20_000_000, transcendentals=HEADS * ROWS * KEYS),
        name="attention_forward",
    )(joined, joined, joined, sibling, sibling, mask)


def attention_backward_kernel(
    q_ref, ko_ref, vo_ref, ks_ref, vs_ref, p_ref, o_ref, linv_ref, g_ref,
    gq_ref, gko_ref, gvo_ref, gks_ref, gvs_ref,
):
    half = [lane_row(bf16, 0, 64), lane_row(bf16, 64, 128)]
    two = [lane_row(bf16, 64, 66), lane_row(bf16, 0, 2)]
    q = q_ref[...]
    k = jnp.concatenate([ko_ref[...], ks_ref[...]], axis=0)
    v = jnp.concatenate([vo_ref[...], vs_ref[...]], axis=0)
    v_now = [v * half[h] + two[h] for h in range(2)]
    lane = lax.broadcasted_iota(jnp.int32, (ROWS, LANES), 1)
    gs = g_ref[...].astype(f32) * linv_ref[...]
    prod = gs * o_ref[...]
    gq, gk, gv = [], [], []
    for h in range(2):
        mine = (lane < 64) if h == 0 else (lane >= 64)
        base = 64 if h == 0 else 0
        delta = jnp.sum(jnp.where(mine, prod, 0.0), axis=1, keepdims=True)
        high = delta.astype(bf16).astype(f32)
        g_aug = jnp.where(
            mine, gs, jnp.where(lane == base, -high, jnp.where(lane == base + 1, high - delta, 0.0))
        ).astype(bf16)
        weights = p_ref[h]
        diff = mm_nt(g_aug, v_now[h])
        gscore = (weights.astype(f32) * diff).astype(bf16)
        gv.append(mm_tn(weights, g_aug))
        gk.append(mm_tn(gscore, q))
        gq.append(mm(gscore, k))
    gq_ref[...] = (jnp.where(lane < 64, gq[0], gq[1]) * 0.125).astype(bf16)
    lane_k = lax.broadcasted_iota(jnp.int32, (KEYS, LANES), 1)
    gk_all = jnp.where(lane_k < 64, gk[0], gk[1]) * 0.125
    gv_all = jnp.where(lane_k < 64, gv[0], gv[1])
    gko_ref[...] = gk_all[:ROWS]
    gvo_ref[...] = gv_all[:ROWS]
    gks_ref[...] = gk_all[ROWS:].astype(bf16)
    gvs_ref[...] = gv_all[ROWS:].astype(bf16)


def attention_backward(joined, sibling, weights, heads_out, linv, grad_att, first, count):
    col = lambda base: pl.BlockSpec((ROWS, LANES), lambda i, f=base + first: (0, f + i))
    own = pl.BlockSpec((ROWS, LANES), lambda i: (0, i))
    width = count * LANES
    return pl.pallas_call(
        attention_backward_kernel,
        grid=(count,),
        in_specs=[
            col(0), col(PAIRS), col(2 * PAIRS), col(0), col(PAIRS),
            pl.BlockSpec((2, ROWS, KEYS), lambda i: (first + i, 0, 0)),
            col(0), col(0), col(0),
        ],
        out_specs=[own] * 5,
        out_shape=[
            jax.ShapeDtypeStruct((ROWS, width), bf16),
            jax.ShapeDtypeStruct((ROWS, width), f32),
            jax.ShapeDtypeStruct((ROWS, width), f32),
            jax.ShapeDtypeStruct((ROWS, width), bf16),
            jax.ShapeDtypeStruct((ROWS, width), bf16),
        ],
        compiler_params=pltpu.CompilerParams(vmem_limit_bytes=VMEM_LIMIT),
        cost_estimate=pl.CostEstimate(flops=32 * ROWS * KEYS * width, bytes_accessed=12_000_000, transcendentals=0),
        name="attention_backward",
    )(joined, joined, joined, sibling, sibling, weights, heads_out, linv, grad_att)


def chunk_both_ways(g, n2, up, down, up_b):
    u = mm(n2, up) + up_b
    ga = mm_nt(g, down)
    u2 = u * u
    t = jnp.tanh(u * (GELU_C + (GELU_C * GELU_A) * u2))
    hp = 0.5 + 0.5 * t
    active = (u * hp).astype(bf16)
    slope = hp + (0.5 * u) * (1.0 - t * t) * (GELU_C + (3.0 * GELU_C * GELU_A) * u2)
    gu = (ga * slope).astype(bf16)
    return active, gu


def ff_first_kernel(
    at_ref, att_ref, x_ref, g_ref, ow_ref, vec_ref, upb_ref, up_ref, down_ref,
    y_ref, xhat_ref, rstd_ref, n2_ref, gn_ref, dup_ref, ddown_ref, upbg_ref,
):
    step = pl.program_id(0)
    out_bias, gain, shift, down_bias = (vec_ref[r : r + 1, :] for r in range(4))

    @pl.when(step == 0)
    def _():
        h = x_ref[...].astype(f32) + mm(att_ref[...], ow_ref[...]) + out_bias
        centred = h - jnp.mean(h, axis=1, keepdims=True)
        rstd = lax.rsqrt(jnp.mean(centred * centred, axis=1, keepdims=True) + epsilon)
        xh = centred * rstd
        xhat_ref[...] = xh
        rstd_ref[...] = jnp.broadcast_to(rstd, (ROWS, LANES))
        n2_ref[...] = (xh * gain + shift).astype(bf16)
        y_ref[...] = h + down_bias
        gn_ref[...] = jnp.zeros_like(gn_ref)

    g = g_ref[...]
    n2 = n2_ref[...]
    active, gu = chunk_both_ways(g, n2, up_ref[...], down_ref[...], upb_ref[0])
    ddown_ref[...] = mm_tn(active, g).astype(bf16)
    dup_ref[...] = mm_tn(n2, gu).astype(bf16)
    y_ref[...] += mm(active, down_ref[...])
    gn_ref[...] += mm_nt(gu, up_ref[...])
    upbg_ref[0] = jnp.sum(gu.astype(f32), axis=0, keepdims=True)


def quarters(buffer, place, core, keep_ref, away_ref):
    first = 1 + 2 * core
    for ref, index, block in (
        (keep_ref, 0, place), (keep_ref, 1, place ^ (4 - first)), (away_ref, 0, place ^ first), (away_ref, 1, place ^ 2),
    ):
        ref[index, 0] = buffer[pl.ds(pl.multiple_of(block * QUARTER, QUARTER), QUARTER), :]


def ff_second_kernel(
    at_ref, g_ref, ow_ref, vec_ref, upb_ref, up_ref, down_ref,
    y_ref, xhat_ref, rstd_ref, n2_ref, gn_in_ref,
    out_ref, gh_ref, gb_ref, gatt_ref, active_ref, gu_ref, vecg_ref, upbg_ref,
    y_acc, gn_acc,
):
    step = pl.program_id(0)
    gain = vec_ref[1:2, :]
    g = g_ref[...]
    active, gu = chunk_both_ways(g, n2_ref[...], up_ref[...], down_ref[...], upb_ref[0])
    active_ref[...] = active
    gu_ref[...] = gu
    upbg_ref[0] = jnp.sum(gu.astype(f32), axis=0, keepdims=True)
    y = mm(active, down_ref[...])
    gn = mm_nt(gu, up_ref[...])

    @pl.when(step == 0)
    def _():
        y_acc[...] = y + y_ref[...]
        gn_acc[...] = gn + gn_in_ref[...]

    @pl.when(step == 1)
    def _():
        out_ref[...] = (y_acc[...] + y).astype(bf16)
        gn_all = gn_acc[...] + gn
        xh = xhat_ref[...]
        gf = g.astype(f32)
        vecg_ref[...] = jnp.zeros_like(vecg_ref)
        vecg_ref[1:2, :] = jnp.sum(gn_all * xh, axis=0, keepdims=True)
        vecg_ref[2:3, :] = jnp.sum(gn_all, axis=0, keepdims=True)
        vecg_ref[3:4, :] = jnp.sum(gf, axis=0, keepdims=True)
        gx = gn_all * gain
        mean1 = jnp.mean(gx, axis=1, keepdims=True)
        mean2 = jnp.mean(gx * xh, axis=1, keepdims=True)
        gh = gf + rstd_ref[:, 0:1] * (gx - mean1 - xh * mean2)
        gh_ref[...] = gh
        vecg_ref[0:1, :] = jnp.sum(gh, axis=0, keepdims=True)
        gb = gh.astype(bf16)
        gb_ref[...] = gb
        gatt_ref[...] = mm_nt(gb, ow_ref[...]).astype(bf16)


def ff_grads_kernel(
    at_ref, active_ref, gu_ref, g_ref, n2_ref, dup_in_ref, ddown_in_ref,
    up_keep_ref, up_away_ref, down_keep_ref, down_away_ref, up_buf, down_buf,
):
    up_buf[...] = (mm_tn(n2_ref[...], gu_ref[...]) + dup_in_ref[...].astype(f32)).astype(bf16)
    quarters(up_buf, at_ref[1], at_ref[0], up_keep_ref, up_away_ref)
    down_buf[...] = (mm_tn(active_ref[...], g_ref[...]) + ddown_in_ref[...].astype(f32)).astype(bf16)
    quarters(down_buf, at_ref[2], at_ref[0], down_keep_ref, down_away_ref)


def whole(*shape):
    return pl.BlockSpec(shape, lambda s, at: (0,) * len(shape))


def ff_specs(chunk):
    return [
        pl.BlockSpec((1, 1, FCHUNK), lambda s, at: (chunk(s, at), 0, 0)),
        pl.BlockSpec((D, FCHUNK), lambda s, at: (0, chunk(s, at))),
        pl.BlockSpec((FCHUNK, D), lambda s, at: (chunk(s, at), 0)),
    ]


TOKEN_SPEC = pl.BlockSpec((ROWS, D), lambda s, at: (0, 0))
COTANGENT_SPEC = pl.BlockSpec((ROWS, D), lambda s, at: (0, 1))
STEP_ROWS = pl.BlockSpec((FCHUNK, D), lambda s, at: (s, 0))
QUARTERS = pl.BlockSpec((2, 1, QUARTER, D), lambda s, at: (0, s, 0, 0))
FF_COST = pl.CostEstimate(flops=6 * ROWS * D * FF, bytes_accessed=15_000_000, transcendentals=ROWS * FF // 2)


def ff_first(at, attended, both, out_w, vecs, up_b, up_w, down_w):
    shape = jax.ShapeDtypeStruct
    return pl.pallas_call(
        ff_first_kernel,
        grid_spec=pltpu.PrefetchScalarGridSpec(
            num_scalar_prefetch=1,
            grid=(NF // 2,),
            in_specs=[whole(ROWS, D), TOKEN_SPEC, COTANGENT_SPEC, whole(D, D), whole(8, D)]
            + ff_specs(lambda s, at: 2 * (1 - at[0]) + s),
            out_specs=[
                whole(ROWS, D), whole(ROWS, D), whole(ROWS, LANES), whole(ROWS, D), whole(ROWS, D),
                STEP_ROWS, STEP_ROWS, pl.BlockSpec((1, 1, FCHUNK), lambda s, at: (s, 0, 0)),
            ],
        ),
        out_shape=[
            shape((ROWS, D), f32), shape((ROWS, D), f32), shape((ROWS, LANES), f32), shape((ROWS, D), bf16),
            shape((ROWS, D), f32), shape((FF // 2, D), bf16), shape((FF // 2, D), bf16),
            shape((NF // 2, 1, FCHUNK), f32),
        ],
        compiler_params=pltpu.CompilerParams(vmem_limit_bytes=VMEM_LIMIT),
        cost_estimate=FF_COST,
        name="ff_first",
    )(at, attended, both, both, out_w, vecs, up_b, up_w, down_w)


def ff_second(at, both, out_w, vecs, up_b, up_w, down_w, kept):
    shape = jax.ShapeDtypeStruct
    step_columns = pl.BlockSpec((ROWS, FCHUNK), lambda s, at: (0, s))
    return pl.pallas_call(
        ff_second_kernel,
        grid_spec=pltpu.PrefetchScalarGridSpec(
            num_scalar_prefetch=1,
            grid=(NF // 2,),
            in_specs=[COTANGENT_SPEC, whole(D, D), whole(8, D)]
            + ff_specs(lambda s, at: 2 * at[0] + s)
            + [whole(ROWS, D), whole(ROWS, D), whole(ROWS, LANES), whole(ROWS, D), whole(ROWS, D)],
            out_specs=[whole(ROWS, D)] * 4
            + [step_columns, step_columns, whole(8, D), pl.BlockSpec((1, 1, FCHUNK), lambda s, at: (s, 0, 0))],
            scratch_shapes=[pltpu.VMEM((ROWS, D), f32), pltpu.VMEM((ROWS, D), f32)],
        ),
        out_shape=[
            shape((ROWS, D), bf16), shape((ROWS, D), f32), shape((ROWS, D), bf16), shape((ROWS, D), bf16),
            shape((ROWS, FF // 2), bf16), shape((ROWS, FF // 2), bf16),
            shape((8, D), f32), shape((NF // 2, 1, FCHUNK), f32),
        ],
        compiler_params=pltpu.CompilerParams(vmem_limit_bytes=VMEM_LIMIT),
        cost_estimate=FF_COST,
        name="ff_second",
    )(at, both, out_w, vecs, up_b, up_w, down_w, *kept)


def ff_grads(at, active, gu, both, n2, arrived):
    quarter_shape = jax.ShapeDtypeStruct((2, NF // 2, QUARTER, D), bf16)
    step_columns = pl.BlockSpec((ROWS, FCHUNK), lambda s, at: (0, s))
    return pl.pallas_call(
        ff_grads_kernel,
        grid_spec=pltpu.PrefetchScalarGridSpec(
            num_scalar_prefetch=1,
            grid=(NF // 2,),
            in_specs=[step_columns, step_columns, COTANGENT_SPEC, whole(ROWS, D), STEP_ROWS, STEP_ROWS],
            out_specs=[QUARTERS] * 4,
            scratch_shapes=[pltpu.VMEM((D, FCHUNK), bf16), pltpu.VMEM((FCHUNK, D), bf16)],
        ),
        out_shape=[quarter_shape] * 4,
        compiler_params=pltpu.CompilerParams(vmem_limit_bytes=VMEM_LIMIT),
        cost_estimate=pl.CostEstimate(flops=4 * ROWS * D * FF // 2, bytes_accessed=15_000_000, transcendentals=0),
        name="ff_grads",
    )(at, active, gu, both, n2, *arrived)


def square_kernel(at_ref, left_ref, right_ref, out_ref):
    out_ref[...] = mm_tn(left_ref[...], right_ref[...]).astype(bf16)


def square_sum_kernel(
    at_ref, left_ref, right_ref, other_ref, keep0_ref, away0_ref, keep1_ref, away1_ref, buf
):
    buf[...] = (mm_tn(left_ref[...], right_ref[...]) + other_ref[...].astype(f32)).astype(bf16)

    @pl.when(pl.program_id(0) == 0)
    def _():
        quarters(buf, at_ref[1], at_ref[0], keep0_ref, away0_ref)

    @pl.when(pl.program_id(0) == 1)
    def _():
        quarters(buf, at_ref[2], at_ref[0], keep1_ref, away1_ref)


def square_specs(mine):
    def number(s, at):
        return 2 * (at[0] if mine else 1 - at[0]) + s

    return [
        pl.BlockSpec((ROWS, D), lambda s, at: (0, jnp.maximum(number(s, at) - 2, 0))),
        pl.BlockSpec((ROWS, D), lambda s, at: (0, number(s, at))),
    ]


SQUARE_COST = pl.CostEstimate(flops=4 * ROWS * D * D, bytes_accessed=6_000_000, transcendentals=0)


def square_away(at, left, right):
    return pl.pallas_call(
        square_kernel,
        grid_spec=pltpu.PrefetchScalarGridSpec(
            num_scalar_prefetch=1, grid=(2,), in_specs=square_specs(False),
            out_specs=pl.BlockSpec((D, D), lambda s, at: (s, 0)),
        ),
        out_shape=jax.ShapeDtypeStruct((2 * D, D), bf16),
        compiler_params=pltpu.CompilerParams(vmem_limit_bytes=VMEM_LIMIT),
        cost_estimate=SQUARE_COST,
        name="square_away",
    )(at, left, right)


def square_mine(at, left, right, other):
    quarter_shape = jax.ShapeDtypeStruct((2, 1, QUARTER, D), bf16)
    return pl.pallas_call(
        square_sum_kernel,
        grid_spec=pltpu.PrefetchScalarGridSpec(
            num_scalar_prefetch=1, grid=(2,),
            in_specs=square_specs(True) + [pl.BlockSpec((D, D), lambda s, at: (s, 0))],
            out_specs=[whole(2, 1, QUARTER, D)] * 4,
            scratch_shapes=[pltpu.VMEM((D, D), bf16)],
        ),
        out_shape=[quarter_shape] * 4,
        compiler_params=pltpu.CompilerParams(vmem_limit_bytes=VMEM_LIMIT),
        cost_estimate=SQUARE_COST,
        name="square_mine",
    )(at, left, right, other)


def put_quarters(out_ref, place, core, own_ref, got_ref):
    first = 1 + 2 * core
    for ref, index, block in (
        (own_ref, 0, place), (own_ref, 1, place ^ (4 - first)), (got_ref, 0, place ^ first), (got_ref, 1, place ^ 2),
    ):
        out_ref[pl.ds(pl.multiple_of(block * QUARTER, QUARTER), QUARTER), :] = ref[index, 0].astype(f32)


def put_from(out_ref, at_ref, part, half, own, got, own_other, got_other):
    core, place = at_ref[0], at_ref[1 + part]

    @pl.when(core == half)
    def _():
        put_quarters(out_ref, place, core, own, got)

    @pl.when(core != half)
    def _():
        put_quarters(out_ref, place, 1 - core, own_other, got_other)


def place_ff_kernel(at_ref, *refs):
    half = pl.program_id(0) // 2
    put_from(refs[8], at_ref, 0, half, *refs[:4])
    put_from(refs[9], at_ref, 1, half, *refs[4:8])


def place_ff(at, first, second):
    source = pl.BlockSpec((2, 1, QUARTER, D), lambda s, at: (0, s % 2, 0, 0))
    return pl.pallas_call(
        place_ff_kernel,
        grid_spec=pltpu.PrefetchScalarGridSpec(
            num_scalar_prefetch=1, grid=(NF,), in_specs=[source] * 8,
            out_specs=[pl.BlockSpec((D, FCHUNK), lambda s, at: (0, s)), pl.BlockSpec((FCHUNK, D), lambda s, at: (s, 0))],
        ),
        out_shape=[jax.ShapeDtypeStruct((D, FF), f32), jax.ShapeDtypeStruct((FF, D), f32)],
        compiler_params=pltpu.CompilerParams(vmem_limit_bytes=VMEM_LIMIT),
        cost_estimate=pl.CostEstimate(flops=0, bytes_accessed=40_000_000, transcendentals=0),
        name="place_ff",
    )(at, *first, *second)


def place_squares_kernel(at_ref, *refs):
    for block in range(4):
        out_ref = refs[8] if block < 3 else refs[9]
        part = block % 2

        @pl.when(pl.program_id(0) == block)
        def _():
            put_from(out_ref, at_ref, part, block // 2, *refs[4 * part : 4 * part + 4])


def place_squares(at, first, second):
    return pl.pallas_call(
        place_squares_kernel,
        grid_spec=pltpu.PrefetchScalarGridSpec(
            num_scalar_prefetch=1, grid=(4,), in_specs=[whole(2, 1, QUARTER, D)] * 8,
            out_specs=[pl.BlockSpec((D, D), lambda s, at: (0, jnp.minimum(s, 2))), whole(D, D)],
        ),
        out_shape=[jax.ShapeDtypeStruct((D, 3 * D), f32), jax.ShapeDtypeStruct((D, D), f32)],
        compiler_params=pltpu.CompilerParams(vmem_limit_bytes=VMEM_LIMIT),
        cost_estimate=pl.CostEstimate(flops=0, bytes_accessed=20_000_000, transcendentals=0),
        name="place_squares",
    )(at, *first, *second)


def linear(y, xl, c, z, xh):
    return (((y * 2 + xl) * 2 + c) * 4 + z) * 2 + xh


def scene_pairs(slot):
    pairs = []
    for y, xl, z, xh in itertools.product(range(4), range(2), range(4), range(2)):
        block = 2 * z + xh
        scene = (slot - block) % 4
        if scene < 3:
            for c in range(2):
                pairs.append((linear(y, xl, c, z, xh), linear(y, xl, block // 4, scene, c)))
    return pairs


def to_scene(values, block):
    pieces = []
    for slot in range(SLOTS):
        scene = jnp.minimum((slot - block) % 4, 2)
        pieces.append(lax.ppermute(lax.dynamic_index_in_dim(values, scene, 0, keepdims=False), AXES, scene_pairs(slot)))
    return pieces


def send_from_scene(values):
    pieces = []
    for slot in range(SLOTS):
        back = [(target, source) for source, target in scene_pairs(slot)]
        pieces.append(lax.ppermute(values[slot * BLK : (slot + 1) * BLK], AXES, back))
    return pieces


def take_from_scene(pieces, block):
    pieces = jnp.stack(pieces)
    return jnp.stack([lax.dynamic_index_in_dim(pieces, (m + block) % 4, 0, keepdims=False) for m in range(3)])


SWAP = ((0, 1), (1, 0))
STEPS = ((1, -1), (-1, 1), (2, 2))
MASKS = ((1, 3), (3, 1))


def exchange(value, move):
    pairs = []
    for place in itertools.product(range(4), range(4), range(4), range(2)):
        ends = [linear(y, x % 2, c, z, x // 2) for x, y, z, c in (place, move(*place))]
        pairs.append(tuple(ends))
    return lax.ppermute(value, AXES, pairs)


def shift(value, axis, signs):
    def move(x, y, z, c):
        at = {"x": x, "y": y, "z": z}
        at[axis] = (at[axis] + signs[c]) % 4
        return at["x"], at["y"], at["z"], c

    return exchange(value, move)


def meet(value, axis, step):
    def move(x, y, z, c):
        at = {"x": x, "y": y, "z": z}
        at[axis] = at[axis] ^ MASKS[c][step]
        return at["x"], at["y"], at["z"], c

    return exchange(value, move)


def swap(value):
    return lax.ppermute(value, "c", SWAP)


class Sum:
    def __init__(self, core, x_place, keep, away):
        self.core, self.x_place = core, x_place
        self.keep, self.away = keep, away

    def send_half(self):
        return [meet(self.away[0], "y", 0), meet(self.away[1], "z", 0)]

    def take_half(self, arrived):
        self.keep = [k + a for k, a in zip(self.keep, arrived)]

    def send_quarter(self):
        return [meet(self.keep[0][1], "y", 1), meet(self.keep[1][1], "z", 1)]

    def take_quarter(self, arrived):
        total = jnp.stack([k[0] + a for k, a in zip(self.keep, arrived)])
        self.blocks = total.reshape(total.shape[:2] + (4, QUARTER // 4, D))

    def block(self, step):
        return lax.dynamic_index_in_dim(self.blocks, (self.x_place + step) % 4, 2, keepdims=False)

    def steps(self):
        return [jnp.where(self.core == 0, a, b) for a, b in STEPS]

    def send_x(self):
        return [shift(self.block(step), "x", signs) for step, signs in zip(self.steps(), STEPS)]

    def take_x(self, arrived):
        total = self.block(0).astype(f32)
        for term in arrived:
            total = total + term.astype(f32)
        self.ends = total.astype(bf16)

    def send_last(self, step):
        return [meet(self.ends[0], "z", step), meet(self.ends[1], "y", step)]

    def take_last(self, arrived):
        self.ends = self.ends + jnp.stack(arrived)

    def send_x_back(self):
        return [shift(self.ends, "x", signs) for signs in STEPS]

    def take_x_back(self, arrived):
        whole_x = jnp.zeros_like(self.blocks)
        for step, piece in zip([0] + self.steps(), [self.ends] + arrived):
            whole_x = lax.dynamic_update_index_in_dim(whole_x, piece, (self.x_place - step) % 4, 2)
        whole_x = whole_x.reshape(self.blocks.shape[:2] + (QUARTER, D))
        self.own = [whole_x[0], whole_x[1]]

    def send_quarter_back(self):
        return [meet(self.own[0], "y", 1), meet(self.own[1], "z", 1)]

    def take_quarter_back(self, arrived):
        self.own = [jnp.stack([o, a]) for o, a in zip(self.own, arrived)]

    def send_half_back(self):
        return [meet(self.own[0], "y", 0), meet(self.own[1], "z", 0)]

    def send_own(self):
        return [swap(self.own[0]), swap(self.own[1])]

    def pieces(self, got, own_other, got_other):
        return [[self.own[p], got[p], own_other[p], got_other[p]] for p in range(2)]


BITS = tuple((axis, bit) for axis in "czyx" for bit in ((1,) if axis == "c" else (1, 2)))


def send_small(values, number):
    axis, bit = BITS[number]
    flip = lambda x, y, z, c: tuple(v ^ bit if n == axis else v for n, v in zip("xyzc", (x, y, z, c)))
    return [exchange(values, flip)]


def hold(*values):
    return lax.optimization_barrier(values)


def body(
    tokens, view_counts, ln1_gain, ln1_shift, qkv_weight, query_bias, value_bias, out_weight, out_bias,
    ln2_gain, ln2_shift, up_weight, up_bias, down_weight, down_bias, cotangent,
):
    core, z, xh = lax.axis_index("c"), lax.axis_index("z"), lax.axis_index("xh")
    block = 2 * z + xh
    scene = jnp.minimum(z, 2)

    views = jnp.broadcast_to(view_counts.astype(bf16)[:, None, None], (3, BLK, LANES))
    pieces = to_scene(jnp.concatenate([tokens, cotangent, views], axis=2), block)
    both = jnp.concatenate([piece[:, : 2 * D] for piece in pieces], axis=0)
    views = pieces[0][0, 2 * D].astype(f32)
    x = both[:, :D]

    slot = jnp.arange(ROWS, dtype=jnp.int32) // BLK
    inside = jnp.arange(ROWS, dtype=jnp.int32) % BLK
    offset = (slot - z) % 4 * BLK + inside
    place = jnp.concatenate([offset + core * ROWS, offset + (1 - core) * ROWS])
    usable = (place.astype(f32) < views * VIEW_TOK) | (place >= VIEWS_MAX * VIEW_TOK)
    mask = jnp.broadcast_to(jnp.where(usable, 0.0, masked_score).astype(bf16)[:, None], (KEYS, LANES))

    source = x.astype(f32)
    centred = source - jnp.mean(source, axis=1, keepdims=True)
    rstd = lax.rsqrt(jnp.mean(centred * centred, axis=1, keepdims=True) + epsilon)
    xhat = centred * rstd
    normed = (xhat * ln1_gain + ln1_shift).astype(bf16)
    qkv_bias = jnp.concatenate([query_bias, jnp.zeros((D,), f32), value_bias])
    joined = (jnp.dot(normed, qkv_weight, preferred_element_type=f32) + qkv_bias).astype(bf16)
    sibling = lax.ppermute(joined[:, D:], "c", SWAP)
    weights, heads_out, linv, attended = attention_forward(joined, sibling, mask)

    vecs = jnp.concatenate([jnp.stack([out_bias, ln2_gain, ln2_shift, down_bias]), jnp.zeros((4, D), f32)])
    up_b = up_bias.reshape(NF, 1, FCHUNK)
    y = lax.axis_index("y")
    x_place = lax.axis_index("xh") * 2 + lax.axis_index("xl")
    at = jnp.stack([core, y, z]).astype(jnp.int32)
    *kept, up_away, down_away, up_b_first = ff_first(at, attended, both, out_weight, vecs, up_b, up_weight, down_weight)
    moving = [swap(up_away), swap(down_away)]
    output, grad_hidden, grad_branch, grad_att, active, grad_up, vec_grads, up_b_second = ff_second(
        at, both, out_weight, vecs, up_b, up_weight, down_weight, kept
    )

    moving, active = hold(moving, active)
    up_keep, up_away, down_keep, down_away = ff_grads(at, active, grad_up, both, kept[3], moving)
    ff = Sum(core, x_place, [up_keep, down_keep], [up_away, down_away])
    ff.away, grad_att = hold(ff.away, grad_att)
    moving = ff.send_half()
    one = attention_backward(joined, sibling, weights, heads_out, linv, grad_att, 0, PAIRS // 2)

    moving, one = hold(moving, one)
    ff.take_half(moving)
    ff.keep, grad_att = hold(ff.keep, grad_att)
    moving = ff.send_quarter()
    two = attention_backward(joined, sibling, weights, heads_out, linv, grad_att, PAIRS // 2, PAIRS // 2)

    grads = [jnp.concatenate([a, b], axis=1) for a, b in zip(one, two)]
    others = jnp.concatenate(grads[3:], axis=1)
    moving, others = hold(moving, others)
    swapped = swap(others)
    ff.take_quarter(moving)
    moving = ff.send_x()
    grad_q = grads[0]

    moving, swapped = hold(moving, swapped)
    swapped = swapped.astype(f32)
    grad_k = (grads[1] + swapped[:, :D]).astype(bf16)
    grad_v = (grads[2] + swapped[:, D:]).astype(bf16)
    right = jnp.concatenate([grad_q, grad_k, grad_v, grad_branch], axis=1)
    left = jnp.concatenate([normed, attended], axis=1)
    away = square_away(at, left, right)
    ff.take_x(moving)
    ff.ends, away = hold(ff.ends, away)
    moving2 = [swap(away)]
    moving = ff.send_last(0)
    grad_normed = lax.dot_general(
        right[:, : 3 * D], qkv_weight, (((1,), (1,)), ((), ())), preferred_element_type=f32
    )

    moving, moving2, grad_normed = hold(moving, moving2, grad_normed)
    ff.take_last(moving)
    ff.ends, moving2 = hold(ff.ends, moving2)
    moving = ff.send_last(1)
    keep0, away0, keep1, away1 = square_mine(at, left, right, moving2[0])
    squares = Sum(core, x_place, [keep0, keep1], [away0, away1])

    moving, squares.away, grad_normed = hold(moving, squares.away, grad_normed)
    ff.take_last(moving)
    moving2 = squares.send_half()
    moving = ff.send_x_back()
    gx = grad_normed * ln1_gain
    mean1 = jnp.mean(gx, axis=1, keepdims=True)
    mean2 = jnp.mean(gx * xhat, axis=1, keepdims=True)
    input_grad = (grad_hidden + rstd * (gx - mean1 - xhat * mean2)).astype(bf16)
    up_b_grad = jnp.where(
        core == 0, jnp.concatenate([up_b_second, up_b_first]), jnp.concatenate([up_b_first, up_b_second])
    )
    small = jnp.concatenate(
        [
            vec_grads[0], vec_grads[1], vec_grads[2], vec_grads[3],
            jnp.sum(grad_normed * xhat, axis=0), jnp.sum(grad_normed, axis=0),
            jnp.sum(grad_q.astype(f32), axis=0), jnp.sum(grad_v.astype(f32), axis=0),
            up_b_grad.reshape(FF),
        ]
    ).reshape(-1, LANES)

    moving, moving2, small, input_grad = hold(moving, moving2, small, input_grad)
    squares.take_half(moving2)
    ff.take_x_back(moving)
    squares.keep, ff.own, small = hold(squares.keep, ff.own, small)
    moving2 = squares.send_quarter()
    moving = ff.send_quarter_back()
    moving3 = send_small(small, 0)

    moving, moving2, moving3 = hold(moving, moving2, moving3)
    squares.take_quarter(moving2)
    ff.take_quarter_back(moving)
    small = small + moving3[0]
    squares.blocks, ff.own, small = hold(squares.blocks, ff.own, small)
    moving2 = squares.send_x()
    moving = ff.send_half_back()

    moving2, small = hold(moving2, small)
    squares.take_x(moving2)
    squares.ends, small, ff.own = hold(squares.ends, small, ff.own)
    moving2 = squares.send_last(0)
    moving3 = send_small(small, 1)
    own_other = ff.send_own()

    moving2, moving3 = hold(moving2, moving3)
    squares.take_last(moving2)
    small = small + moving3[0]
    squares.ends, small = hold(squares.ends, small)
    moving2 = squares.send_last(1)
    moving3 = send_small(small, 2)

    moving, moving2, moving3, own_other = hold(moving, moving2, moving3, own_other)
    squares.take_last(moving2)
    small = small + moving3[0]
    got = moving
    squares.ends, small, got, output = hold(squares.ends, small, got, output)
    moving2 = squares.send_x_back()
    got_other = [swap(v) for v in got]

    moving2, got_other, output = hold(moving2, got_other, output)
    squares.take_x_back(moving2)
    squares.own, small, output = hold(squares.own, small, output)
    moving2 = squares.send_quarter_back()
    moving3 = send_small(small, 3)
    d_up, d_down = place_ff(at, *ff.pieces(got, own_other, got_other))

    moving2, moving3, d_up, d_down = hold(moving2, moving3, d_up, d_down)
    squares.take_quarter_back(moving2)
    small = small + moving3[0]
    squares.own, small, output = hold(squares.own, small, output)
    moving2 = squares.send_half_back()
    own_other = squares.send_own()
    moving3 = send_small(small, 4)

    moving2, moving3, own_other, output, input_grad = hold(moving2, moving3, own_other, output, input_grad)
    small = small + moving3[0]
    got_other = [swap(v) for v in moving2]
    returned = send_from_scene(jnp.concatenate([output, input_grad], axis=1))
    got_other, small = hold(got_other, small)
    moving3 = send_small(small, 5)
    d_qkv, d_out = place_squares(at, *squares.pieces(moving2, own_other, got_other))
    small = small + moving3[0]
    small, returned = hold(small, returned)
    moving3 = send_small(small, 6)
    returned = take_from_scene(returned, block)
    output, input_grad = returned[:, :, :D], returned[:, :, D:]
    small = (small + moving3[0]).reshape(-1)
    vector = lambda i: small[i * D : (i + 1) * D]
    return (
        output, input_grad, vector(4), vector(5), d_qkv, vector(6), vector(7), d_out,
        vector(0), vector(1), vector(2), d_up, small[8 * D :], d_down, vector(3),
    )


def solution(mesh):
    fine = Mesh(mesh.devices.reshape(4, 2, 2, 4, 2), AXES)
    rows = P(("y", "xl", "c"), ("z", "xh"), None)
    placed = (rows, P(("y", "xl", "c"))) + (P(),) * 13 + (rows,)
    return jax.shard_map(
        body, mesh=fine, in_specs=placed, out_specs=(rows, rows) + (P(),) * 13, check_vma=False
    )
```

```python
import functools
import itertools
import math

import jax
import jax.numpy as jnp
from jax import lax
from jax.experimental import pallas as pl
from jax.experimental.pallas import tpu as pltpu
from jax.sharding import Mesh
from jax.sharding import PartitionSpec as P

HEADS = 12
HEAD_DIM = 64
VIEW_TOK = 128
VIEWS_MAX = 8
D = 768
FF = 3072
BLK = 144
SLOTS = 4
ROWS = BLK * SLOTS
KEYS = 2 * ROWS
PAIRS = HEADS // 2
LANES = 128
FCHUNK = 768
QROWS = 288
QUARTER = D // 4
NF = FF // FCHUNK

bf16 = jnp.bfloat16
f32 = jnp.float32
epsilon = 1e-05
masked_score = -1e30
GELU_C = math.sqrt(2.0 / math.pi)
GELU_A = 0.044715

AXES = ("y", "xl", "c", "z", "xh")
VMEM_LIMIT = 60 * 1024 * 1024


def mm(a, b):
    return lax.dot_general(a, b, (((1,), (0,)), ((), ())), preferred_element_type=f32)


def mm_nt(a, b):
    return lax.dot_general(a, b, (((1,), (1,)), ((), ())), preferred_element_type=f32)


def mm_tn(a, b):
    return lax.dot_general(a, b, (((0,), (0,)), ((), ())), preferred_element_type=f32)


def lane_row(at, first, last):
    lane = lax.broadcasted_iota(jnp.int32, (1, LANES), 1)
    return jnp.where((lane >= first) & (lane < last), 1.0, 0.0).astype(at)


def attention_forward_kernel(q_ref, ko_ref, vo_ref, ks_ref, vs_ref, mask_ref, p_ref, o_ref, linv_ref, att_ref):
    half = [lane_row(bf16, 0, 64), lane_row(bf16, 64, 128)]
    unit = [lane_row(bf16, 64, 65), lane_row(bf16, 0, 1)]
    q = q_ref[...]
    k = jnp.concatenate([ko_ref[...], ks_ref[...]], axis=0)
    v = jnp.concatenate([vo_ref[...], vs_ref[...]], axis=0)
    mask = mask_ref[...]
    lane = lax.broadcasted_iota(jnp.int32, (QROWS, LANES), 1)
    q_now = [q * half[h] + unit[h] for h in range(2)]
    k_now = [k * half[h] + mask * unit[h] for h in range(2)]
    v_now = [v * half[h] + unit[h] for h in range(2)]
    items = [(slice(s * QROWS, (s + 1) * QROWS), h) for s in range(ROWS // QROWS) for h in range(2)]
    done = {}

    def product(number, weights):
        rows, h = items[number]
        out = mm(weights, v_now[h])
        inv = 1.0 / (out[:, 64:65] if h == 0 else out[:, 0:1])
        done[h] = (out * inv, jnp.broadcast_to(inv, (QROWS, LANES)))
        if h == 1:
            out = jnp.where(lane < 64, done[0][0], done[1][0])
            o_ref[rows, :] = out
            att_ref[rows, :] = out.astype(bf16)
            linv_ref[rows, :] = jnp.where(lane < 64, done[0][1], done[1][1])

    scores = mm_nt(q_now[0][items[0][0]], k_now[0])
    before = None
    for number, (rows, h) in enumerate(items):
        following = None
        if number + 1 < len(items):
            next_rows, next_h = items[number + 1]
            following = mm_nt(q_now[next_h][next_rows], k_now[next_h])
        top = jnp.max(scores, axis=1, keepdims=True)
        weights = jnp.exp((scores - top) * 0.125).astype(bf16)
        p_ref[h, rows, :] = weights
        if before is not None:
            product(number - 1, before)
        before, scores = weights, following
    product(len(items) - 1, before)


def head_columns(base):
    return pl.BlockSpec((ROWS, LANES), lambda i, f=base: (0, f + i))


def attention_forward(queries, own, sibling, mask):
    col = head_columns
    return pl.pallas_call(
        attention_forward_kernel,
        grid=(PAIRS,),
        in_specs=[col(0), col(0), col(PAIRS), col(0), col(PAIRS), pl.BlockSpec((KEYS, LANES), lambda i: (0, 0))],
        out_specs=[pl.BlockSpec((2, ROWS, KEYS), lambda i: (i, 0, 0)), col(0), col(0), col(0)],
        out_shape=[
            jax.ShapeDtypeStruct((HEADS, ROWS, KEYS), bf16),
            jax.ShapeDtypeStruct((ROWS, D), f32),
            jax.ShapeDtypeStruct((ROWS, D), f32),
            jax.ShapeDtypeStruct((ROWS, D), bf16),
        ],
        compiler_params=pltpu.CompilerParams(vmem_limit_bytes=VMEM_LIMIT),
        cost_estimate=pl.CostEstimate(flops=16 * ROWS * KEYS * D, bytes_accessed=20_000_000, transcendentals=HEADS * ROWS * KEYS),
        name="attention_forward",
    )(queries, own, own, sibling, sibling, mask)


def attention_backward_kernel(
    at_ref, q_ref, ko_ref, vo_ref, ks_ref, vs_ref, p_ref, o_ref, linv_ref, g_ref, gq_ref, gown_ref, sent_ref
):
    half = [lane_row(bf16, 0, 64), lane_row(bf16, 64, 128)]
    two = [lane_row(bf16, 64, 66), lane_row(bf16, 0, 2)]
    lane = lax.broadcasted_iota(jnp.int32, (ROWS, LANES), 1)
    k = jnp.concatenate([ko_ref[...], ks_ref[...]], axis=0)
    v = jnp.concatenate([vo_ref[...], vs_ref[...]], axis=0)
    gs = g_ref[...].astype(f32) * linv_ref[...]
    prod = gs * o_ref[...]
    g_now, v_now = [], []
    for h in range(2):
        mine = (lane < 64) if h == 0 else (lane >= 64)
        base = 64 if h == 0 else 0
        delta = jnp.sum(jnp.where(mine, prod, 0.0), axis=1, keepdims=True)
        high = delta.astype(bf16).astype(f32)
        columns = jnp.where(lane == base, -high, jnp.where(lane == base + 1, high - delta, 0.0))
        g_now.append(jnp.where(mine, gs, columns).astype(bf16))
        v_now.append(v * half[h] + two[h])
    g_turned, q_turned = gs.astype(bf16).T, q_ref[...].T
    head = lambda turned, h: turned[64 * h : 64 * h + 64]
    grad_score = lambda h, diff: (p_ref[h].astype(f32) * diff).astype(bf16)
    diff = mm_nt(g_now[0], v_now[0])
    gv0 = mm(head(g_turned, 0), p_ref[0])
    gs0 = grad_score(0, diff)
    diff = mm_nt(g_now[1], v_now[1])
    gv1 = mm(head(g_turned, 1), p_ref[1])
    gs1 = grad_score(1, diff)
    gk0, gq0 = mm(head(q_turned, 0), gs0), mm(gs0, k)
    gk1, gq1 = mm(head(q_turned, 1), gs1), mm(gs1, k)
    gq = (jnp.where(lane < 64, gq0, gq1) * 0.125).astype(bf16)
    gk = (jnp.concatenate([gk0, gk1], axis=0) * 0.125).T.astype(bf16)
    gv = jnp.concatenate([gv0, gv1], axis=0).T.astype(bf16)
    gq_ref[...] = gq
    gown_ref[0], gown_ref[1] = gk[:ROWS], gv[:ROWS]
    sent_ref[0], sent_ref[1] = gk[ROWS:], gv[ROWS:]
    sent_ref[2] = jnp.where(at_ref[0] == 0, gv[:ROWS], gk[:ROWS])
    sent_ref[3] = gq


def attention_backward(at, queries, own, sibling, weights, heads_out, linv, grad_att):
    col = lambda base: pl.BlockSpec((ROWS, LANES), lambda i, at: (0, base + i))
    several = lambda count: pl.BlockSpec((count, ROWS, LANES), lambda i, at: (0, 0, i))
    return pl.pallas_call(
        attention_backward_kernel,
        grid_spec=pltpu.PrefetchScalarGridSpec(
            num_scalar_prefetch=1, grid=(PAIRS,),
            in_specs=[
                col(0), col(0), col(PAIRS), col(0), col(PAIRS),
                pl.BlockSpec((2, ROWS, KEYS), lambda i, at: (i, 0, 0)),
                col(0), col(0), col(0),
            ],
            out_specs=[col(0), several(2), several(4)],
        ),
        out_shape=[jax.ShapeDtypeStruct(shape, bf16) for shape in ((ROWS, D), (2, ROWS, D), (4, ROWS, D))],
        compiler_params=pltpu.CompilerParams(vmem_limit_bytes=VMEM_LIMIT),
        cost_estimate=pl.CostEstimate(flops=32 * ROWS * KEYS * D, bytes_accessed=25_000_000, transcendentals=0),
        name="attention_backward",
    )(at, queries, own, own, sibling, sibling, weights, heads_out, linv, grad_att)


def quarter_blocks(place, core):
    first = 1 + 2 * core
    return place, place ^ (4 - first), place ^ first, place ^ 2


def quarter_rows(block):
    return pl.ds(pl.multiple_of(block * QUARTER, QUARTER), QUARTER)


def put_quarters(ref, buffer, place, core):
    for index, block in enumerate(quarter_blocks(place, core)):
        ref[index, 0] = buffer[quarter_rows(block), :]


def feed_forward_kernel(
    at_ref, att_ref, x_ref, g_ref, ow_ref, vec_ref, upb_ref, up_ref, down_ref,
    out_ref, gh_ref, gb_ref, gatt_ref, up_other_ref, up_mine_ref, down_other_ref, down_mine_ref, vecg_ref, upbg_ref,
    hidden, xhat, rstd_s, normed2, y_acc, gn_acc, buffer,
):
    step = pl.program_id(0)
    out_bias, gain, shift, down_bias = (vec_ref[r : r + 1, :] for r in range(4))

    @pl.when(step == 0)
    def _():
        h = x_ref[...].astype(f32) + mm(att_ref[...], ow_ref[...]) + out_bias
        hidden[...] = h
        centred = h - jnp.mean(h, axis=1, keepdims=True)
        rstd = lax.rsqrt(jnp.mean(centred * centred, axis=1, keepdims=True) + epsilon)
        xh = centred * rstd
        xhat[...] = xh
        rstd_s[...] = jnp.broadcast_to(rstd, (ROWS, LANES))
        normed2[...] = (xh * gain + shift).astype(bf16)
        y_acc[...] = jnp.zeros_like(y_acc)
        gn_acc[...] = jnp.zeros_like(gn_acc)

    g = g_ref[...]
    n2 = normed2[...]
    u = mm(n2, up_ref[...]) + upb_ref[0]
    ga = mm_nt(g, down_ref[...])
    u2 = u * u
    t = jnp.tanh(u * (GELU_C + (GELU_C * GELU_A) * u2))
    hp = 0.5 + 0.5 * t
    active = (u * hp).astype(bf16)
    slope = hp + (0.5 * u) * (1.0 - t * t) * (GELU_C + (3.0 * GELU_C * GELU_A) * u2)
    gu = (ga * slope).astype(bf16)
    y_acc[...] += mm(active, down_ref[...])
    gn_acc[...] += mm_nt(gu, up_ref[...])
    upbg_ref[0] = jnp.sum(gu.astype(f32), axis=0, keepdims=True)
    for part, value, other_ref, mine_ref in (
        (0, mm_tn(n2, gu), up_other_ref, up_mine_ref), (1, mm_tn(active, g), down_other_ref, down_mine_ref),
    ):
        buffer[...] = value.astype(bf16)

        @pl.when(step < NF // 2)
        def _():
            put_quarters(other_ref, buffer, at_ref[1 + part], 1 - at_ref[0])

        @pl.when(step >= NF // 2)
        def _():
            put_quarters(mine_ref, buffer, at_ref[1 + part], at_ref[0])

    @pl.when(step == NF - 1)
    def _():
        out_ref[...] = (hidden[...] + y_acc[...] + down_bias).astype(bf16)
        gn = gn_acc[...]
        xh = xhat[...]
        gf = g_ref[...].astype(f32)
        vecg_ref[...] = jnp.zeros_like(vecg_ref)
        vecg_ref[1:2, :] = jnp.sum(gn * xh, axis=0, keepdims=True)
        vecg_ref[2:3, :] = jnp.sum(gn, axis=0, keepdims=True)
        vecg_ref[3:4, :] = jnp.sum(gf, axis=0, keepdims=True)
        gx = gn * gain
        mean1 = jnp.mean(gx, axis=1, keepdims=True)
        mean2 = jnp.mean(gx * xh, axis=1, keepdims=True)
        gh = gf + rstd_s[:, 0:1] * (gx - mean1 - xh * mean2)
        gh_ref[...] = gh
        vecg_ref[0:1, :] = jnp.sum(gh, axis=0, keepdims=True)
        gb = gh.astype(bf16)
        gb_ref[...] = gb
        gatt_ref[...] = mm_nt(gb, ow_ref[...]).astype(bf16)


def whole(*shape):
    return pl.BlockSpec(shape, lambda s, at: (0,) * len(shape))


TOKEN_SPEC = pl.BlockSpec((ROWS, D), lambda s, at: (0, 0))
COTANGENT_SPEC = pl.BlockSpec((ROWS, D), lambda s, at: (0, 1))


def feed_forward(at, attended, both, out_w, vecs, up_b, up_w, down_w):
    shape = jax.ShapeDtypeStruct
    chunk = lambda s, at: (2 * (1 - at[0]) + s) % NF
    other = pl.BlockSpec((4, 1, QUARTER, D), lambda s, at: (0, jnp.minimum(s, NF // 2 - 1), 0, 0))
    mine = pl.BlockSpec((4, 1, QUARTER, D), lambda s, at: (0, jnp.maximum(s - NF // 2, 0), 0, 0))
    return pl.pallas_call(
        feed_forward_kernel,
        grid_spec=pltpu.PrefetchScalarGridSpec(
            num_scalar_prefetch=1,
            grid=(NF,),
            in_specs=[
                whole(ROWS, D), TOKEN_SPEC, COTANGENT_SPEC, whole(D, D), whole(8, D),
                pl.BlockSpec((1, 1, FCHUNK), lambda s, at: (chunk(s, at), 0, 0)),
                pl.BlockSpec((D, FCHUNK), lambda s, at: (0, chunk(s, at))),
                pl.BlockSpec((FCHUNK, D), lambda s, at: (chunk(s, at), 0)),
            ],
            out_specs=[whole(ROWS, D)] * 4
            + [other, mine, other, mine, whole(8, D), pl.BlockSpec((1, 1, FCHUNK), lambda s, at: (chunk(s, at), 0, 0))],
            scratch_shapes=[
                pltpu.VMEM((ROWS, D), f32), pltpu.VMEM((ROWS, D), f32), pltpu.VMEM((ROWS, LANES), f32),
                pltpu.VMEM((ROWS, D), bf16), pltpu.VMEM((ROWS, D), f32), pltpu.VMEM((ROWS, D), f32),
                pltpu.VMEM((D, D), bf16),
            ],
        ),
        out_shape=[
            shape((ROWS, D), bf16), shape((ROWS, D), f32), shape((ROWS, D), bf16), shape((ROWS, D), bf16),
        ]
        + [shape((4, NF // 2, QUARTER, D), bf16)] * 4
        + [shape((8, D), f32), shape((NF, 1, FCHUNK), f32)],
        compiler_params=pltpu.CompilerParams(vmem_limit_bytes=VMEM_LIMIT),
        cost_estimate=pl.CostEstimate(flops=12 * ROWS * D * FF, bytes_accessed=30_000_000, transcendentals=ROWS * FF),
        name="feed_forward",
    )(at, attended, both, both, out_w, vecs, up_b, up_w, down_w)


def squares_kernel(
    at_ref, gq_ref, own_ref, other_ref, arrived_ref, arrived_own_ref, arrived_gq_ref, gb_ref, gb_other_ref,
    normed_ref, normed_other_ref, att_ref, att_other_ref, keep0_ref, away0_ref, keep1_ref, away1_ref,
    joined, joined_other, buffer,
):
    core = at_ref[0]

    def product(part, left, left_other, right, right_other):
        buffer[...] = (mm_tn(left[...], right[...]) + mm_tn(left_other[...], right_other[...])).astype(bf16)
        keep_ref, away_ref = ((keep0_ref, away0_ref), (keep1_ref, away1_ref))[part]
        for index, block in enumerate(quarter_blocks(at_ref[1 + part], core)):
            (keep_ref if index < 2 else away_ref)[index % 2, 0] = buffer[quarter_rows(block), :]

    joined[...] = own_ref[0] + arrived_ref[0]
    joined_other[...] = arrived_own_ref[0] + other_ref[0]

    @pl.when(core == 0)
    def _():
        product(0, normed_ref, normed_other_ref, gq_ref, arrived_gq_ref.at[0])
        product(1, normed_ref, normed_other_ref, joined, joined_other)

    @pl.when(core != 0)
    def _():
        product(0, normed_ref, normed_other_ref, joined, joined_other)
        product(1, att_ref, att_other_ref, gb_ref, gb_other_ref)


def squares(at, gq, own, sent, arrived, *pairs):
    rows = whole(ROWS, D)
    pick = pl.BlockSpec((1, ROWS, D), lambda s, at: (at[0], 0, 0))
    number = lambda n: pl.BlockSpec((1, ROWS, D), lambda s, at: (n, 0, 0))
    return pl.pallas_call(
        squares_kernel,
        grid_spec=pltpu.PrefetchScalarGridSpec(
            num_scalar_prefetch=1, grid=(1,),
            in_specs=[rows, pick, pick, pick, number(2), number(3)] + [rows] * 6,
            out_specs=[whole(2, 1, QUARTER, D)] * 4,
            scratch_shapes=[pltpu.VMEM((ROWS, D), bf16), pltpu.VMEM((ROWS, D), bf16), pltpu.VMEM((D, D), bf16)],
        ),
        out_shape=[jax.ShapeDtypeStruct((2, 1, QUARTER, D), bf16)] * 4,
        compiler_params=pltpu.CompilerParams(vmem_limit_bytes=VMEM_LIMIT),
        cost_estimate=pl.CostEstimate(flops=8 * ROWS * D * D, bytes_accessed=13_000_000, transcendentals=0),
        name="squares",
    )(at, gq, own, sent, arrived, arrived, arrived, *pairs)


def input_grad_kernel(
    gq_ref, own_ref, swapped_ref, w_ref, x_ref, gh_ref, gain_ref, vecg_ref, upbg_ref, out_ref, small_ref, right
):
    step = pl.program_id(0)
    right[:, :D] = gq_ref[...]
    right[:, D : 2 * D] = own_ref[0] + swapped_ref[0]
    right[:, 2 * D :] = own_ref[1] + swapped_ref[1]
    grad_normed = mm_nt(right[...], w_ref[...])
    source = x_ref[...].astype(f32)
    centred = source - jnp.mean(source, axis=1, keepdims=True)
    rstd = lax.rsqrt(jnp.mean(centred * centred, axis=1, keepdims=True) + epsilon)
    xhat = centred * rstd
    gx = grad_normed * gain_ref[0:1, :]
    mean1 = jnp.mean(gx, axis=1, keepdims=True)
    mean2 = jnp.mean(gx * xhat, axis=1, keepdims=True)
    out_ref[...] = (gh_ref[...] + rstd * (gx - mean1 - xhat * mean2)).astype(bf16)

    @pl.when(step == 0)
    def _():
        small_ref[...] = jnp.zeros_like(small_ref)
        small_ref[0:4, :] = vecg_ref[0:4, :]
        for f in range(NF):
            small_ref[8 + f : 9 + f, :] = upbg_ref[f]

    small_ref[4:5, :] += jnp.sum(grad_normed * xhat, axis=0, keepdims=True)
    small_ref[5:6, :] += jnp.sum(grad_normed, axis=0, keepdims=True)
    small_ref[6:7, :] += jnp.sum(right[:, :D].astype(f32), axis=0, keepdims=True)
    small_ref[7:8, :] += jnp.sum(right[:, 2 * D :].astype(f32), axis=0, keepdims=True)


def input_gradient(gq, own, swapped, qkv_w, both, grad_hidden, gain, vec_grads, up_b_grad):
    steps = 3
    length = ROWS // steps
    rows = pl.BlockSpec((length, D), lambda s: (s, 0))
    pair = pl.BlockSpec((2, length, D), lambda s: (0, s, 0))
    fixed = lambda *shape: pl.BlockSpec(shape, lambda s: (0,) * len(shape))
    return pl.pallas_call(
        input_grad_kernel,
        grid=(steps,),
        in_specs=[rows, pair, pair, fixed(D, 3 * D), rows, rows, fixed(8, D), fixed(8, D), fixed(NF, 1, FCHUNK)],
        out_specs=[rows, fixed(16, D)],
        out_shape=[jax.ShapeDtypeStruct((ROWS, D), bf16), jax.ShapeDtypeStruct((16, D), f32)],
        scratch_shapes=[pltpu.VMEM((length, 3 * D), bf16)],
        compiler_params=pltpu.CompilerParams(vmem_limit_bytes=VMEM_LIMIT),
        cost_estimate=pl.CostEstimate(flops=6 * ROWS * D * D, bytes_accessed=10_000_000, transcendentals=0),
        name="input_gradient",
    )(gq, own, swapped, qkv_w, both, grad_hidden, gain, vec_grads, up_b_grad)


def place_kernel(mine, late, at_ref, source0_ref, source1_ref, *refs):
    up_ref, down_ref, qkv_ref, out_ref, tiles, sems = refs[-6:]
    half = at_ref[0] if mine else 1 - at_ref[0]
    sources = (source0_ref, source1_ref)
    copies = []

    def send(source, target, condition=None):
        number = len(copies)
        copies.append(None)
        tiles[number] = source.astype(f32)

        def start(to):
            copy = pltpu.make_async_copy(tiles.at[number], to, sems.at[number])
            copy.start()

        if condition is None:
            start(target[0])
        else:
            pl.when(condition)(lambda: start(target[0]))
            pl.when(jnp.logical_not(condition))(lambda: start(target[1]))

    for j in range(2):
        block = 2 * half + j
        columns = pl.ds(pl.multiple_of(block * D, D), D)
        for s in range(2):
            rows = [
                quarter_rows(quarter_blocks(at_ref[1 + part], half)[s + (2 if late else 0)]) for part in range(2)
            ]
            send(sources[0][s, j], [up_ref.at[rows[0], columns]])
            down_rows = pl.ds(pl.multiple_of(block * D + rows[1].start, QUARTER), QUARTER)
            send(sources[1][s, j], [down_ref.at[down_rows, :]])
            if j == 0:
                send(sources[j][s, 2], [qkv_ref.at[rows[j], columns]])
            else:
                columns_qkv = pl.ds(pl.multiple_of(D, D), D)
                send(sources[j][s, 2], [qkv_ref.at[rows[j], columns_qkv], out_ref.at[rows[j], :]], half == 0)
    for number in range(len(copies)):
        pltpu.make_async_copy(tiles.at[number], up_ref.at[pl.ds(0, QUARTER), pl.ds(0, D)], sems.at[number]).wait()


def place(at, pieces, mine, late, before=()):
    shape = jax.ShapeDtypeStruct
    anywhere = pl.BlockSpec(memory_space=pl.ANY)
    return pl.pallas_call(
        functools.partial(place_kernel, mine, late),
        grid_spec=pltpu.PrefetchScalarGridSpec(
            num_scalar_prefetch=1, grid=(1,),
            in_specs=[whole(2, NF // 2 + 1, QUARTER, D)] * 2 + [anywhere] * len(before),
            out_specs=[anywhere] * 4,
            scratch_shapes=[pltpu.VMEM((12, QUARTER, D), f32), pltpu.SemaphoreType.DMA((12,))],
        ),
        out_shape=[shape((D, FF), f32), shape((FF, D), f32), shape((D, 3 * D), f32), shape((D, D), f32)],
        input_output_aliases={3 + index: index for index in range(len(before))},
        compiler_params=pltpu.CompilerParams(vmem_limit_bytes=VMEM_LIMIT),
        cost_estimate=pl.CostEstimate(flops=0, bytes_accessed=11_000_000, transcendentals=0),
        name="place_late" if late else "place_early",
    )(at, *pieces, *before)


def linear(y, xl, c, z, xh):
    return (((y * 2 + xl) * 2 + c) * 4 + z) * 2 + xh


def scene_pairs(slot):
    pairs = []
    for y, xl, z, xh in itertools.product(range(4), range(2), range(4), range(2)):
        block = 2 * z + xh
        scene = (slot - block) % 4
        if scene < 3:
            for c in range(2):
                pairs.append((linear(y, xl, c, z, xh), linear(y, xl, block // 4, scene, c)))
    return pairs


def to_scene(values, block):
    pieces = []
    for slot in range(SLOTS):
        scene = jnp.minimum((slot - block) % 4, 2)
        pieces.append(lax.ppermute(lax.dynamic_index_in_dim(values, scene, 0, keepdims=False), AXES, scene_pairs(slot)))
    return pieces


def send_from_scene(values):
    pieces = []
    for slot in range(SLOTS):
        back = [(target, source) for source, target in scene_pairs(slot)]
        pieces.append(lax.ppermute(values[slot * BLK : (slot + 1) * BLK], AXES, back))
    return pieces


def take_from_scene(pieces, block):
    pieces = jnp.stack(pieces)
    return jnp.stack([lax.dynamic_index_in_dim(pieces, (m + block) % 4, 0, keepdims=False) for m in range(3)])


SWAP = ((0, 1), (1, 0))
MASKS = ((1, 3), (3, 1))


def exchange(value, move):
    pairs = []
    for place in itertools.product(range(4), range(4), range(4), range(2)):
        ends = [linear(y, x % 2, c, z, x // 2) for x, y, z, c in (place, move(*place))]
        pairs.append(tuple(ends))
    return lax.ppermute(value, AXES, pairs)


def meet(value, axis, step):
    def move(x, y, z, c):
        at = {"x": x, "y": y, "z": z}
        at[axis] = at[axis] ^ MASKS[c][step]
        return at["x"], at["y"], at["z"], c

    return exchange(value, move)


def swap(value):
    return lax.ppermute(value, "c", SWAP)


ORDERS = ("yxz", "zyx")


def meet_parts(values, stage, step):
    return [meet(value, ORDERS[part][stage], step) for part, value in enumerate(values)]


def add(*terms):
    return functools.reduce(jnp.add, [term.astype(f32) for term in terms]).astype(bf16)


def block_of(blocks, index):
    return lax.dynamic_index_in_dim(blocks, index, 1, keepdims=False)


def put_block(blocks, value, index):
    return lax.dynamic_update_index_in_dim(blocks, value, index, 1)


SMALL = 16


def meet_with(value, small, axis, step):
    high = lax.reduce_precision(small, 8, 7)
    low = lax.reduce_precision(small - high, 8, 7)
    rows = value.reshape(-1, D)
    message = jnp.concatenate([rows, high.astype(bf16), low.astype(bf16)], axis=0)
    arrived = meet(message, axis, step)
    count = rows.shape[0]
    other = arrived[count : count + SMALL].astype(f32) + arrived[count + SMALL :].astype(f32)
    return arrived[:count].reshape(value.shape), (high + low) + other


def hold(*values):
    return lax.optimization_barrier(values)


def body(
    tokens, view_counts, ln1_gain, ln1_shift, qkv_weight, query_bias, value_bias, out_weight, out_bias,
    ln2_gain, ln2_shift, up_weight, up_bias, down_weight, down_bias, cotangent,
):
    core, z, xh = lax.axis_index("c"), lax.axis_index("z"), lax.axis_index("xh")

    block = 2 * z + xh
    views = jnp.broadcast_to(view_counts.astype(bf16)[:, None, None], (3, BLK, LANES))
    pieces = to_scene(jnp.concatenate([tokens, cotangent, views], axis=2), block)
    both = jnp.concatenate([piece[:, : 2 * D] for piece in pieces], axis=0)
    views = pieces[0][0, 2 * D].astype(f32)
    x = both[:, :D]

    row = jnp.arange(ROWS, dtype=jnp.int32)
    offset = (row // BLK - z) % 4 * BLK + row % BLK
    position = jnp.concatenate([offset + core * ROWS, offset + (1 - core) * ROWS])
    usable = (position.astype(f32) < views * VIEW_TOK) | (position >= VIEWS_MAX * VIEW_TOK)
    mask = jnp.broadcast_to(jnp.where(usable, 0.0, masked_score).astype(bf16)[:, None], (KEYS, LANES))

    source = x.astype(f32)
    centred = source - jnp.mean(source, axis=1, keepdims=True)
    rstd = lax.rsqrt(jnp.mean(centred * centred, axis=1, keepdims=True) + epsilon)
    normed = (centred * rstd * ln1_gain + ln1_shift).astype(bf16)
    product = lambda weight: jnp.dot(normed, weight, preferred_element_type=f32)
    kv_bias = jnp.concatenate([jnp.zeros((D,), f32), value_bias])
    own = (product(qkv_weight[:, D:]) + kv_bias).astype(bf16)
    sibling = swap(own)
    normed_other = swap(normed)
    queries = (product(qkv_weight[:, :D]) + query_bias).astype(bf16)
    weights, heads_out, linv, attended = attention_forward(queries, own, sibling, mask)

    vecs = jnp.concatenate([jnp.stack([out_bias, ln2_gain, ln2_shift, down_bias]), jnp.zeros((4, D), f32)])
    up_b = up_bias.reshape(NF, 1, FCHUNK)
    y = lax.axis_index("y")
    x_place = lax.axis_index("xh") * 2 + lax.axis_index("xl")
    at = jnp.stack([core, y, z]).astype(jnp.int32)
    output, grad_hidden, grad_branch, grad_att, up_other, up_mine, down_other, down_mine, vec_grads, up_b_grad = (
        feed_forward(at, attended, both, out_weight, vecs, up_b, up_weight, down_weight)
    )

    moving = [swap(up_other), swap(down_other)]
    attended_other, branch_other = swap(attended), swap(grad_branch)
    grad_q, grad_own, sent = attention_backward(at, queries, own, sibling, weights, heads_out, linv, grad_att)

    moving, attended_other, branch_other, sent = hold(moving, attended_other, branch_other, sent)
    arrived = swap(sent)
    pieces = [(up_mine, moving[0]), (down_mine, moving[1])]
    away = [add(mine[2:], other[2:]) for mine, other in pieces]
    arrived, away = hold(arrived, away)
    halved = meet_parts(away, 0, 0)
    keep0, away0, keep1, away1 = squares(
        at, grad_q, grad_own, sent, arrived, grad_branch, branch_other, normed, normed_other, attended, attended_other
    )

    away, grad_hidden = hold([away0, away1], grad_hidden)
    square_halved = meet_parts(away, 0, 0)
    gains = jnp.broadcast_to(ln1_gain[None, :], (8, D))
    input_grad, small = input_gradient(
        grad_q, grad_own, arrived, qkv_weight, both, grad_hidden, gains, vec_grads, up_b_grad
    )

    halved, square_halved, small, input_grad = hold(halved, square_halved, small, input_grad)
    away = [add(mine[1], other[1], half[1]) for (mine, other), half in zip(pieces, halved)]
    square_away = [add(keep[1], half[1]) for keep, half in zip((keep0, keep1), square_halved)]
    square_quartered = meet_parts(square_away, 0, 1)
    quartered = meet_parts(away, 0, 1)

    def ring_sum(pieces, halved, quartered):
        return [
            add(mine[0], other[0], half[0], quarter)
            for (mine, other), half, quarter in zip(pieces, halved, quartered)
        ]

    ff_own = ring_sum(pieces, halved, quartered)
    square_quartered, ff_own, small = hold(square_quartered, ff_own, small)
    owns = [add(k[0], h[0], q) for k, h, q in zip((keep0, keep1), square_halved, square_quartered)]
    blocks = [
        jnp.concatenate([f, o], axis=0).reshape(NF // 2 + 1, 4, QUARTER // 4, D) for f, o in zip(ff_own, owns)
    ]
    places = [x_place, y]
    first = 1 + 2 * core
    keep = [(block_of(b, p), block_of(b, p ^ (4 - first))) for b, p in zip(blocks, places)]
    away = [jnp.stack([block_of(b, p ^ first), block_of(b, p ^ 2)]) for b, p in zip(blocks, places)]
    keep, away, small = hold(keep, away, small)
    one_way = meet(away[0], "x", 0)
    other_way, small = meet_with(away[1], small, "y", 0)

    one_way, other_way, small = hold(one_way, other_way, small)
    halved = [one_way, other_way]
    away, small = hold([add(k[1], h[1]) for k, h in zip(keep, halved)], small)
    one_way = meet(away[0], "x", 1)
    other_way, small = meet_with(away[1], small, "y", 1)

    one_way, other_way, small = hold(one_way, other_way, small)
    quartered = [one_way, other_way]
    ends = [add(k[0], h[0], q) for k, h, q in zip(keep, halved, quartered)]
    for step in range(2):
        ends, small = hold(ends, small)
        one_way, small = meet_with(ends[0], small, "z", step)
        other_way = meet(ends[1], "x", step)
        one_way, other_way, small = hold(one_way, other_way, small)
        ends = [ends[0] + one_way, ends[1] + other_way]

    ends, small, output, input_grad = hold(ends, small, output, input_grad)
    one_way, small = meet_with(ends[0], small, "x", 1)
    other_way = meet(ends[1], "y", 1)

    one_way, other_way, small = hold(one_way, other_way, small)
    pairs = [jnp.stack([ends[0], one_way]), jnp.stack([ends[1], other_way])]
    pairs, small = hold(pairs, small)
    one_way, small = meet_with(pairs[0], small, "x", 0)
    other_way = meet(pairs[1], "y", 0)

    one_way, other_way, small = hold(one_way, other_way, small)
    owns = []
    for pair, more, p, empty in zip(pairs, (one_way, other_way), places, blocks):
        full = jnp.zeros_like(empty)
        for value, index in ((pair[0], p), (pair[1], p ^ (4 - first)), (more[0], p ^ first), (more[1], p ^ 2)):
            full = put_block(full, value, index)
        owns.append(full.reshape(NF // 2 + 1, QUARTER, D))
    owns, small, output, input_grad = hold(owns, small, output, input_grad)
    arrived = meet_parts(owns, 0, 1)
    returned = send_from_scene(jnp.concatenate([output, input_grad], axis=1))

    arrived, returned = hold(arrived, returned)
    pairs = [jnp.stack([o, a]) for o, a in zip(owns, arrived)]
    pairs, small = hold(pairs, small)
    got = meet_parts(pairs, 0, 0)
    own_other = [swap(v) for v in pairs]
    small_other = swap(small)
    placed = place(at, pairs, True, False)
    returned = take_from_scene(returned, block)

    own_other, small_other, placed = hold(own_other, small_other, placed)
    small = small + small_other
    placed = place(at, own_other, False, False, placed)
    got, placed, returned = hold(got, placed, returned)
    got_other = [swap(v) for v in got]
    placed = place(at, got, True, True, placed)
    d_up, d_down, d_qkv, d_out = place(at, got_other, False, True, placed)
    return (
        returned[:, :, :D], returned[:, :, D:], small[4], small[5], d_qkv, small[6], small[7], d_out,
        small[0], small[1], small[2], d_up, small[8:12].reshape(FF), d_down, small[3],
    )


def solution(mesh):
    fine = Mesh(mesh.devices.reshape(4, 2, 2, 4, 2), AXES)
    rows = P(("y", "xl", "c"), ("z", "xh"), None)
    placed = (rows, P(("y", "xl", "c"))) + (P(),) * 13 + (rows,)
    return jax.shard_map(
        body, mesh=fine, in_specs=placed, out_specs=(rows, rows) + (P(),) * 13, check_vma=False
    )
```

```python
import functools
import itertools
import math

import jax
import jax.numpy as jnp
from jax import lax
from jax.experimental import pallas as pl
from jax.experimental.pallas import tpu as pltpu
from jax.sharding import Mesh
from jax.sharding import PartitionSpec as P

HEADS = 12
HEAD_DIM = 64
VIEW_TOK = 128
VIEWS_MAX = 8
D = 768
FF = 3072
BLK = 144
SLOTS = 4
ROWS = BLK * SLOTS
KEYS = 2 * ROWS
PAIRS = HEADS // 2
LANES = 128
FCHUNK = 768
QROWS = 288
QUARTER = D // 4
NF = FF // FCHUNK

bf16 = jnp.bfloat16
f32 = jnp.float32
epsilon = 1e-05
masked_score = -1e30
GELU_C = math.sqrt(2.0 / math.pi)
GELU_A = 0.044715

AXES = ("y", "xl", "c", "z", "xh")
VMEM_LIMIT = 60 * 1024 * 1024


def mm(a, b):
    return lax.dot_general(a, b, (((1,), (0,)), ((), ())), preferred_element_type=f32)


def mm_nt(a, b):
    return lax.dot_general(a, b, (((1,), (1,)), ((), ())), preferred_element_type=f32)


def mm_tn(a, b):
    return lax.dot_general(a, b, (((0,), (0,)), ((), ())), preferred_element_type=f32)


def lane_row(at, first, last):
    lane = lax.broadcasted_iota(jnp.int32, (1, LANES), 1)
    return jnp.where((lane >= first) & (lane < last), 1.0, 0.0).astype(at)


def attention_forward_kernel(q_ref, ko_ref, vo_ref, ks_ref, vs_ref, mask_ref, p_ref, o_ref, linv_ref, att_ref):
    half = [lane_row(bf16, 0, 64), lane_row(bf16, 64, 128)]
    unit = [lane_row(bf16, 64, 65), lane_row(bf16, 0, 1)]
    q = q_ref[...]
    k = jnp.concatenate([ko_ref[...], ks_ref[...]], axis=0)
    v = jnp.concatenate([vo_ref[...], vs_ref[...]], axis=0)
    mask = mask_ref[...]
    lane = lax.broadcasted_iota(jnp.int32, (QROWS, LANES), 1)
    q_now = [q * half[h] + unit[h] for h in range(2)]
    k_now = [k * half[h] + mask * unit[h] for h in range(2)]
    v_now = [v * half[h] + unit[h] for h in range(2)]
    items = [(slice(s * QROWS, (s + 1) * QROWS), h) for s in range(ROWS // QROWS) for h in range(2)]
    done = {}

    def product(number, weights):
        rows, h = items[number]
        out = mm(weights, v_now[h])
        inv = 1.0 / (out[:, 64:65] if h == 0 else out[:, 0:1])
        done[h] = (out * inv, jnp.broadcast_to(inv, (QROWS, LANES)))
        if h == 1:
            out = jnp.where(lane < 64, done[0][0], done[1][0])
            o_ref[rows, :] = out
            att_ref[rows, :] = out.astype(bf16)
            linv_ref[rows, :] = jnp.where(lane < 64, done[0][1], done[1][1])

    scores = mm_nt(q_now[0][items[0][0]], k_now[0])
    before = None
    for number, (rows, h) in enumerate(items):
        following = None
        if number + 1 < len(items):
            next_rows, next_h = items[number + 1]
            following = mm_nt(q_now[next_h][next_rows], k_now[next_h])
        top = jnp.max(scores, axis=1, keepdims=True)
        weights = jnp.exp((scores - top) * 0.125).astype(bf16)
        p_ref[h, rows, :] = weights
        if before is not None:
            product(number - 1, before)
        before, scores = weights, following
    product(len(items) - 1, before)


def head_columns(base):
    return pl.BlockSpec((ROWS, LANES), lambda i, f=base: (0, f + i))


def attention_forward(queries, own, sibling, mask):
    col = head_columns
    return pl.pallas_call(
        attention_forward_kernel,
        grid=(PAIRS,),
        in_specs=[col(0), col(0), col(PAIRS), col(0), col(PAIRS), pl.BlockSpec((KEYS, LANES), lambda i: (0, 0))],
        out_specs=[pl.BlockSpec((2, ROWS, KEYS), lambda i: (i, 0, 0)), col(0), col(0), col(0)],
        out_shape=[
            jax.ShapeDtypeStruct((HEADS, ROWS, KEYS), bf16),
            jax.ShapeDtypeStruct((ROWS, D), f32),
            jax.ShapeDtypeStruct((ROWS, D), f32),
            jax.ShapeDtypeStruct((ROWS, D), bf16),
        ],
        compiler_params=pltpu.CompilerParams(vmem_limit_bytes=VMEM_LIMIT),
        cost_estimate=pl.CostEstimate(flops=16 * ROWS * KEYS * D, bytes_accessed=20_000_000, transcendentals=HEADS * ROWS * KEYS),
        name="attention_forward",
    )(queries, own, own, sibling, sibling, mask)


def attention_backward_kernel(
    at_ref, q_ref, ko_ref, vo_ref, ks_ref, vs_ref, p_ref, o_ref, linv_ref, g_ref, gq_ref, gown_ref, sent_ref
):
    half = [lane_row(bf16, 0, 64), lane_row(bf16, 64, 128)]
    two = [lane_row(bf16, 64, 66), lane_row(bf16, 0, 2)]
    lane = lax.broadcasted_iota(jnp.int32, (ROWS, LANES), 1)
    k = jnp.concatenate([ko_ref[...], ks_ref[...]], axis=0)
    v = jnp.concatenate([vo_ref[...], vs_ref[...]], axis=0)
    gs = g_ref[...].astype(f32) * linv_ref[...]
    prod = gs * o_ref[...]
    g_now, v_now = [], []
    for h in range(2):
        mine = (lane < 64) if h == 0 else (lane >= 64)
        base = 64 if h == 0 else 0
        delta = jnp.sum(jnp.where(mine, prod, 0.0), axis=1, keepdims=True)
        high = delta.astype(bf16).astype(f32)
        columns = jnp.where(lane == base, -high, jnp.where(lane == base + 1, high - delta, 0.0))
        g_now.append(jnp.where(mine, gs, columns).astype(bf16))
        v_now.append(v * half[h] + two[h])
    g_turned, q_turned = gs.astype(bf16).T, q_ref[...].T
    head = lambda turned, h: turned[64 * h : 64 * h + 64]
    grad_score = lambda h, diff: (p_ref[h].astype(f32) * diff).astype(bf16)
    diff = mm_nt(g_now[0], v_now[0])
    gv0 = mm(head(g_turned, 0), p_ref[0])
    gs0 = grad_score(0, diff)
    diff = mm_nt(g_now[1], v_now[1])
    gv1 = mm(head(g_turned, 1), p_ref[1])
    gs1 = grad_score(1, diff)
    gk0, gq0 = mm(head(q_turned, 0), gs0), mm(gs0, k)
    gk1, gq1 = mm(head(q_turned, 1), gs1), mm(gs1, k)
    gq = (jnp.where(lane < 64, gq0, gq1) * 0.125).astype(bf16)
    gk = (jnp.concatenate([gk0, gk1], axis=0) * 0.125).T.astype(bf16)
    gv = jnp.concatenate([gv0, gv1], axis=0).T.astype(bf16)
    gq_ref[...] = gq
    gown_ref[0], gown_ref[1] = gk[:ROWS], gv[:ROWS]
    sent_ref[0], sent_ref[1] = gk[ROWS:], gv[ROWS:]
    sent_ref[2] = jnp.where(at_ref[0] == 0, gv[:ROWS], gk[:ROWS])
    sent_ref[3] = gq


def attention_backward(at, queries, own, sibling, weights, heads_out, linv, grad_att):
    col = lambda base: pl.BlockSpec((ROWS, LANES), lambda i, at: (0, base + i))
    several = lambda count: pl.BlockSpec((count, ROWS, LANES), lambda i, at: (0, 0, i))
    return pl.pallas_call(
        attention_backward_kernel,
        grid_spec=pltpu.PrefetchScalarGridSpec(
            num_scalar_prefetch=1, grid=(PAIRS,),
            in_specs=[
                col(0), col(0), col(PAIRS), col(0), col(PAIRS),
                pl.BlockSpec((2, ROWS, KEYS), lambda i, at: (i, 0, 0)),
                col(0), col(0), col(0),
            ],
            out_specs=[col(0), several(2), several(4)],
        ),
        out_shape=[jax.ShapeDtypeStruct(shape, bf16) for shape in ((ROWS, D), (2, ROWS, D), (4, ROWS, D))],
        compiler_params=pltpu.CompilerParams(vmem_limit_bytes=VMEM_LIMIT),
        cost_estimate=pl.CostEstimate(flops=32 * ROWS * KEYS * D, bytes_accessed=25_000_000, transcendentals=0),
        name="attention_backward",
    )(at, queries, own, own, sibling, sibling, weights, heads_out, linv, grad_att)


def quarter_blocks(place, core):
    first = 1 + 2 * core
    return place, place ^ (4 - first), place ^ first, place ^ 2


def quarter_rows(block):
    return pl.ds(pl.multiple_of(block * QUARTER, QUARTER), QUARTER)


def put_quarters(ref, buffer, place, core):
    for index, block in enumerate(quarter_blocks(place, core)):
        ref[index, 0] = buffer[quarter_rows(block), :]


def feed_forward_kernel(
    at_ref, att_ref, x_ref, g_ref, ow_ref, vec_ref, upb_ref, up_ref, down_ref,
    out_ref, gh_ref, gb_ref, gatt_ref, up_other_ref, up_mine_ref, down_other_ref, down_mine_ref, vecg_ref, upbg_ref,
    hidden, xhat, rstd_s, normed2, y_acc, gn_acc, buffer,
):
    step = pl.program_id(0)
    out_bias, gain, shift, down_bias = (vec_ref[r : r + 1, :] for r in range(4))

    @pl.when(step == 0)
    def _():
        h = x_ref[...].astype(f32) + mm(att_ref[...], ow_ref[...]) + out_bias
        hidden[...] = h
        centred = h - jnp.mean(h, axis=1, keepdims=True)
        rstd = lax.rsqrt(jnp.mean(centred * centred, axis=1, keepdims=True) + epsilon)
        xh = centred * rstd
        xhat[...] = xh
        rstd_s[...] = jnp.broadcast_to(rstd, (ROWS, LANES))
        normed2[...] = (xh * gain + shift).astype(bf16)
        y_acc[...] = jnp.zeros_like(y_acc)
        gn_acc[...] = jnp.zeros_like(gn_acc)

    g = g_ref[...]
    n2 = normed2[...]
    u = mm(n2, up_ref[...]) + upb_ref[0]
    ga = mm_nt(g, down_ref[...])
    u2 = u * u
    t = jnp.tanh(u * (GELU_C + (GELU_C * GELU_A) * u2))
    hp = 0.5 + 0.5 * t
    active = (u * hp).astype(bf16)
    slope = hp + (0.5 * u) * (1.0 - t * t) * (GELU_C + (3.0 * GELU_C * GELU_A) * u2)
    gu = (ga * slope).astype(bf16)
    y_acc[...] += mm(active, down_ref[...])
    gn_acc[...] += mm_nt(gu, up_ref[...])
    upbg_ref[0] = jnp.sum(gu.astype(f32), axis=0, keepdims=True)
    for part, value, other_ref, mine_ref in (
        (0, mm_tn(n2, gu), up_other_ref, up_mine_ref), (1, mm_tn(active, g), down_other_ref, down_mine_ref),
    ):
        buffer[...] = value.astype(bf16)

        @pl.when(step < NF // 2)
        def _():
            put_quarters(other_ref, buffer, at_ref[1 + part], 1 - at_ref[0])

        @pl.when(step >= NF // 2)
        def _():
            put_quarters(mine_ref, buffer, at_ref[1 + part], at_ref[0])

    @pl.when(step == NF - 1)
    def _():
        out_ref[...] = (hidden[...] + y_acc[...] + down_bias).astype(bf16)
        gn = gn_acc[...]
        xh = xhat[...]
        gf = g_ref[...].astype(f32)
        vecg_ref[...] = jnp.zeros_like(vecg_ref)
        vecg_ref[1:2, :] = jnp.sum(gn * xh, axis=0, keepdims=True)
        vecg_ref[2:3, :] = jnp.sum(gn, axis=0, keepdims=True)
        vecg_ref[3:4, :] = jnp.sum(gf, axis=0, keepdims=True)
        gx = gn * gain
        mean1 = jnp.mean(gx, axis=1, keepdims=True)
        mean2 = jnp.mean(gx * xh, axis=1, keepdims=True)
        gh = gf + rstd_s[:, 0:1] * (gx - mean1 - xh * mean2)
        gh_ref[...] = gh
        vecg_ref[0:1, :] = jnp.sum(gh, axis=0, keepdims=True)
        gb = gh.astype(bf16)
        gb_ref[...] = gb
        gatt_ref[...] = mm_nt(gb, ow_ref[...]).astype(bf16)


def whole(*shape):
    return pl.BlockSpec(shape, lambda s, at: (0,) * len(shape))


TOKEN_SPEC = pl.BlockSpec((ROWS, D), lambda s, at: (0, 0))
COTANGENT_SPEC = pl.BlockSpec((ROWS, D), lambda s, at: (0, 1))


def feed_forward(at, attended, both, out_w, vecs, up_b, up_w, down_w):
    shape = jax.ShapeDtypeStruct
    chunk = lambda s, at: (2 * (1 - at[0]) + s) % NF
    other = pl.BlockSpec((4, 1, QUARTER, D), lambda s, at: (0, jnp.minimum(s, NF // 2 - 1), 0, 0))
    mine = pl.BlockSpec((4, 1, QUARTER, D), lambda s, at: (0, jnp.maximum(s - NF // 2, 0), 0, 0))
    return pl.pallas_call(
        feed_forward_kernel,
        grid_spec=pltpu.PrefetchScalarGridSpec(
            num_scalar_prefetch=1,
            grid=(NF,),
            in_specs=[
                whole(ROWS, D), TOKEN_SPEC, COTANGENT_SPEC, whole(D, D), whole(8, D),
                pl.BlockSpec((1, 1, FCHUNK), lambda s, at: (chunk(s, at), 0, 0)),
                pl.BlockSpec((D, FCHUNK), lambda s, at: (0, chunk(s, at))),
                pl.BlockSpec((FCHUNK, D), lambda s, at: (chunk(s, at), 0)),
            ],
            out_specs=[whole(ROWS, D)] * 4
            + [other, mine, other, mine, whole(8, D), pl.BlockSpec((1, 1, FCHUNK), lambda s, at: (chunk(s, at), 0, 0))],
            scratch_shapes=[
                pltpu.VMEM((ROWS, D), f32), pltpu.VMEM((ROWS, D), f32), pltpu.VMEM((ROWS, LANES), f32),
                pltpu.VMEM((ROWS, D), bf16), pltpu.VMEM((ROWS, D), f32), pltpu.VMEM((ROWS, D), f32),
                pltpu.VMEM((D, D), bf16),
            ],
        ),
        out_shape=[
            shape((ROWS, D), bf16), shape((ROWS, D), f32), shape((ROWS, D), bf16), shape((ROWS, D), bf16),
        ]
        + [shape((4, NF // 2, QUARTER, D), bf16)] * 4
        + [shape((8, D), f32), shape((NF, 1, FCHUNK), f32)],
        compiler_params=pltpu.CompilerParams(vmem_limit_bytes=VMEM_LIMIT),
        cost_estimate=pl.CostEstimate(flops=12 * ROWS * D * FF, bytes_accessed=30_000_000, transcendentals=ROWS * FF),
        name="feed_forward",
    )(at, attended, both, both, out_w, vecs, up_b, up_w, down_w)


def squares_kernel(
    at_ref, gq_ref, own_ref, other_ref, arrived_ref, arrived_own_ref, arrived_gq_ref, gb_ref, gb_other_ref,
    normed_ref, normed_other_ref, att_ref, att_other_ref, keep0_ref, away0_ref, keep1_ref, away1_ref,
    joined, joined_other, buffer,
):
    core = at_ref[0]

    def product(part, left, left_other, right, right_other):
        buffer[...] = (mm_tn(left[...], right[...]) + mm_tn(left_other[...], right_other[...])).astype(bf16)
        keep_ref, away_ref = ((keep0_ref, away0_ref), (keep1_ref, away1_ref))[part]
        for index, block in enumerate(quarter_blocks(at_ref[1 + part], core)):
            (keep_ref if index < 2 else away_ref)[index % 2, 0] = buffer[quarter_rows(block), :]

    joined[...] = own_ref[0] + arrived_ref[0]
    joined_other[...] = arrived_own_ref[0] + other_ref[0]

    @pl.when(core == 0)
    def _():
        product(0, normed_ref, normed_other_ref, gq_ref, arrived_gq_ref.at[0])
        product(1, normed_ref, normed_other_ref, joined, joined_other)

    @pl.when(core != 0)
    def _():
        product(0, normed_ref, normed_other_ref, joined, joined_other)
        product(1, att_ref, att_other_ref, gb_ref, gb_other_ref)


def squares(at, gq, own, sent, arrived, *pairs):
    rows = whole(ROWS, D)
    pick = pl.BlockSpec((1, ROWS, D), lambda s, at: (at[0], 0, 0))
    number = lambda n: pl.BlockSpec((1, ROWS, D), lambda s, at: (n, 0, 0))
    return pl.pallas_call(
        squares_kernel,
        grid_spec=pltpu.PrefetchScalarGridSpec(
            num_scalar_prefetch=1, grid=(1,),
            in_specs=[rows, pick, pick, pick, number(2), number(3)] + [rows] * 6,
            out_specs=[whole(2, 1, QUARTER, D)] * 4,
            scratch_shapes=[pltpu.VMEM((ROWS, D), bf16), pltpu.VMEM((ROWS, D), bf16), pltpu.VMEM((D, D), bf16)],
        ),
        out_shape=[jax.ShapeDtypeStruct((2, 1, QUARTER, D), bf16)] * 4,
        compiler_params=pltpu.CompilerParams(vmem_limit_bytes=VMEM_LIMIT),
        cost_estimate=pl.CostEstimate(flops=8 * ROWS * D * D, bytes_accessed=13_000_000, transcendentals=0),
        name="squares",
    )(at, gq, own, sent, arrived, arrived, arrived, *pairs)


def input_grad_kernel(
    gq_ref, own_ref, swapped_ref, w_ref, x_ref, gh_ref, gain_ref, vecg_ref, upbg_ref, out_ref, small_ref, right
):
    step = pl.program_id(0)
    right[:, :D] = gq_ref[...]
    right[:, D : 2 * D] = own_ref[0] + swapped_ref[0]
    right[:, 2 * D :] = own_ref[1] + swapped_ref[1]
    grad_normed = mm_nt(right[...], w_ref[...])
    source = x_ref[...].astype(f32)
    centred = source - jnp.mean(source, axis=1, keepdims=True)
    rstd = lax.rsqrt(jnp.mean(centred * centred, axis=1, keepdims=True) + epsilon)
    xhat = centred * rstd
    gx = grad_normed * gain_ref[0:1, :]
    mean1 = jnp.mean(gx, axis=1, keepdims=True)
    mean2 = jnp.mean(gx * xhat, axis=1, keepdims=True)
    out_ref[...] = (gh_ref[...] + rstd * (gx - mean1 - xhat * mean2)).astype(bf16)

    @pl.when(step == 0)
    def _():
        small_ref[...] = jnp.zeros_like(small_ref)
        small_ref[0:4, :] = vecg_ref[0:4, :]
        for f in range(NF):
            small_ref[8 + f : 9 + f, :] = upbg_ref[f]

    small_ref[4:5, :] += jnp.sum(grad_normed * xhat, axis=0, keepdims=True)
    small_ref[5:6, :] += jnp.sum(grad_normed, axis=0, keepdims=True)
    small_ref[6:7, :] += jnp.sum(right[:, :D].astype(f32), axis=0, keepdims=True)
    small_ref[7:8, :] += jnp.sum(right[:, 2 * D :].astype(f32), axis=0, keepdims=True)


def input_gradient(gq, own, swapped, qkv_w, both, grad_hidden, gain, vec_grads, up_b_grad):
    steps = 3
    length = ROWS // steps
    rows = pl.BlockSpec((length, D), lambda s: (s, 0))
    pair = pl.BlockSpec((2, length, D), lambda s: (0, s, 0))
    fixed = lambda *shape: pl.BlockSpec(shape, lambda s: (0,) * len(shape))
    return pl.pallas_call(
        input_grad_kernel,
        grid=(steps,),
        in_specs=[rows, pair, pair, fixed(D, 3 * D), rows, rows, fixed(8, D), fixed(8, D), fixed(NF, 1, FCHUNK)],
        out_specs=[rows, fixed(16, D)],
        out_shape=[jax.ShapeDtypeStruct((ROWS, D), bf16), jax.ShapeDtypeStruct((16, D), f32)],
        scratch_shapes=[pltpu.VMEM((length, 3 * D), bf16)],
        compiler_params=pltpu.CompilerParams(vmem_limit_bytes=VMEM_LIMIT),
        cost_estimate=pl.CostEstimate(flops=6 * ROWS * D * D, bytes_accessed=10_000_000, transcendentals=0),
        name="input_gradient",
    )(gq, own, swapped, qkv_w, both, grad_hidden, gain, vec_grads, up_b_grad)


def place_kernel(mine, late, at_ref, source0_ref, source1_ref, *refs):
    up_ref, down_ref, qkv_ref, out_ref, pieces, tiles, in_sems, out_sems = refs[-8:]
    half = at_ref[0] if mine else 1 - at_ref[0]
    sources = (source0_ref, source1_ref)
    plan = []
    for j in range(2):
        block = 2 * half + j
        columns = pl.ds(pl.multiple_of(block * D, D), D)
        for s in range(2):
            rows = [
                quarter_rows(quarter_blocks(at_ref[1 + part], half)[s + (2 if late else 0)]) for part in range(2)
            ]
            down_rows = pl.ds(pl.multiple_of(block * D + rows[1].start, QUARTER), QUARTER)
            plan.append((sources[0].at[s, j], up_ref.at[rows[0], columns], None))
            plan.append((sources[1].at[s, j], down_ref.at[down_rows, :], None))
            last = out_ref.at[rows[j], :] if j == 1 else None
            square_columns = columns if j == 0 else pl.ds(D, D)
            plan.append((sources[j].at[s, 2], qkv_ref.at[rows[j], square_columns], last))
    loads = []
    for number, (source, _, _) in enumerate(plan):
        loads.append(pltpu.make_async_copy(source, pieces.at[number], in_sems.at[number]))
        loads[-1].start()
    for number, (_, target, last) in enumerate(plan):
        loads[number].wait()
        tiles[number] = pieces[number].astype(f32)

        def start(to, number=number):
            pltpu.make_async_copy(tiles.at[number], to, out_sems.at[number]).start()

        if last is None:
            start(target)
        else:
            pl.when(half == 0)(lambda: start(target))
            pl.when(half != 0)(lambda: start(last))
    for number, (_, target, _) in enumerate(plan):
        pltpu.make_async_copy(tiles.at[number], target, out_sems.at[number]).wait()


def place(at, pieces, mine, late, before=()):
    shape = jax.ShapeDtypeStruct
    anywhere = pl.BlockSpec(memory_space=pl.ANY)
    return pl.pallas_call(
        functools.partial(place_kernel, mine, late),
        grid_spec=pltpu.PrefetchScalarGridSpec(
            num_scalar_prefetch=1, grid=(1,),
            in_specs=[anywhere] * (2 + len(before)),
            out_specs=[anywhere] * 4,
            scratch_shapes=[
                pltpu.VMEM((12, QUARTER, D), bf16), pltpu.VMEM((12, QUARTER, D), f32),
                pltpu.SemaphoreType.DMA((12,)), pltpu.SemaphoreType.DMA((12,)),
            ],
        ),
        out_shape=[shape((D, FF), f32), shape((FF, D), f32), shape((D, 3 * D), f32), shape((D, D), f32)],
        input_output_aliases={3 + index: index for index in range(len(before))},
        compiler_params=pltpu.CompilerParams(vmem_limit_bytes=VMEM_LIMIT),
        cost_estimate=pl.CostEstimate(flops=0, bytes_accessed=11_000_000, transcendentals=0),
        name="place_late" if late else "place_early",
    )(at, *pieces, *before)


def linear(y, xl, c, z, xh):
    return (((y * 2 + xl) * 2 + c) * 4 + z) * 2 + xh


def scene_pairs(slot):
    pairs = []
    for y, xl, z, xh in itertools.product(range(4), range(2), range(4), range(2)):
        block = 2 * z + xh
        scene = (slot - block) % 4
        if scene < 3:
            for c in range(2):
                pairs.append((linear(y, xl, c, z, xh), linear(y, xl, block // 4, scene, c)))
    return pairs


def to_scene(values, block):
    pieces = []
    for slot in range(SLOTS):
        scene = jnp.minimum((slot - block) % 4, 2)
        pieces.append(lax.ppermute(lax.dynamic_index_in_dim(values, scene, 0, keepdims=False), AXES, scene_pairs(slot)))
    return pieces


def send_from_scene(values):
    pieces = []
    for slot in range(SLOTS):
        back = [(target, source) for source, target in scene_pairs(slot)]
        pieces.append(lax.ppermute(values[slot * BLK : (slot + 1) * BLK], AXES, back))
    return pieces


def take_from_scene(pieces, block):
    pieces = jnp.stack(pieces)
    return jnp.stack([lax.dynamic_index_in_dim(pieces, (m + block) % 4, 0, keepdims=False) for m in range(3)])


SWAP = ((0, 1), (1, 0))
MASKS = ((1, 3), (3, 1))


def exchange(value, move):
    pairs = []
    for place in itertools.product(range(4), range(4), range(4), range(2)):
        ends = [linear(y, x % 2, c, z, x // 2) for x, y, z, c in (place, move(*place))]
        pairs.append(tuple(ends))
    return lax.ppermute(value, AXES, pairs)


def meet(value, axis, step):
    def move(x, y, z, c):
        at = {"x": x, "y": y, "z": z}
        at[axis] = at[axis] ^ MASKS[c][step]
        return at["x"], at["y"], at["z"], c

    return exchange(value, move)


def swap(value):
    return lax.ppermute(value, "c", SWAP)


ORDERS = ("yxz", "zyx")


def meet_parts(values, stage, step):
    return [meet(value, ORDERS[part][stage], step) for part, value in enumerate(values)]


def add(*terms):
    return functools.reduce(jnp.add, [term.astype(f32) for term in terms]).astype(bf16)


def block_of(blocks, index):
    return lax.dynamic_index_in_dim(blocks, index, 1, keepdims=False)


def put_block(blocks, value, index):
    return lax.dynamic_update_index_in_dim(blocks, value, index, 1)


SMALL = 16


def meet_with(value, small, axis, step):
    high = lax.reduce_precision(small, 8, 7)
    low = lax.reduce_precision(small - high, 8, 7)
    rows = value.reshape(-1, D)
    message = jnp.concatenate([rows, high.astype(bf16), low.astype(bf16)], axis=0)
    arrived = meet(message, axis, step)
    count = rows.shape[0]
    other = arrived[count : count + SMALL].astype(f32) + arrived[count + SMALL :].astype(f32)
    return arrived[:count].reshape(value.shape), (high + low) + other


def hold(*values):
    return lax.optimization_barrier(values)


def body(
    tokens, view_counts, ln1_gain, ln1_shift, qkv_weight, query_bias, value_bias, out_weight, out_bias,
    ln2_gain, ln2_shift, up_weight, up_bias, down_weight, down_bias, cotangent,
):
    core, z, xh = lax.axis_index("c"), lax.axis_index("z"), lax.axis_index("xh")

    block = 2 * z + xh
    views = jnp.broadcast_to(view_counts.astype(bf16)[:, None, None], (3, BLK, LANES))
    pieces = to_scene(jnp.concatenate([tokens, cotangent, views], axis=2), block)
    vecs = jnp.concatenate([jnp.stack([out_bias, ln2_gain, ln2_shift, down_bias]), jnp.zeros((4, D), f32)])
    gains = jnp.broadcast_to(ln1_gain[None, :], (8, D))
    weight_q, weight_kv = qkv_weight[:, :D], qkv_weight[:, D:]
    pieces, vecs, gains, weight_q, weight_kv = hold(pieces, vecs, gains, weight_q, weight_kv)
    both = jnp.concatenate([piece[:, : 2 * D] for piece in pieces], axis=0)
    views = pieces[0][0, 2 * D].astype(f32)
    x = both[:, :D]

    row = jnp.arange(ROWS, dtype=jnp.int32)
    offset = (row // BLK - z) % 4 * BLK + row % BLK
    position = jnp.concatenate([offset + core * ROWS, offset + (1 - core) * ROWS])
    usable = (position.astype(f32) < views * VIEW_TOK) | (position >= VIEWS_MAX * VIEW_TOK)
    mask = jnp.broadcast_to(jnp.where(usable, 0.0, masked_score).astype(bf16)[:, None], (KEYS, LANES))

    source = x.astype(f32)
    centred = source - jnp.mean(source, axis=1, keepdims=True)
    rstd = lax.rsqrt(jnp.mean(centred * centred, axis=1, keepdims=True) + epsilon)
    normed = (centred * rstd * ln1_gain + ln1_shift).astype(bf16)
    product = lambda weight: jnp.dot(normed, weight, preferred_element_type=f32)
    kv_bias = jnp.concatenate([jnp.zeros((D,), f32), value_bias])
    own = (product(weight_kv) + kv_bias).astype(bf16)
    sibling = swap(own)
    normed_other = swap(normed)
    queries = (product(weight_q) + query_bias).astype(bf16)
    weights, heads_out, linv, attended = attention_forward(queries, own, sibling, mask)

    up_b = up_bias.reshape(NF, 1, FCHUNK)
    y = lax.axis_index("y")
    x_place = lax.axis_index("xh") * 2 + lax.axis_index("xl")
    at = jnp.stack([core, y, z]).astype(jnp.int32)
    output, grad_hidden, grad_branch, grad_att, up_other, up_mine, down_other, down_mine, vec_grads, up_b_grad = (
        feed_forward(at, attended, both, out_weight, vecs, up_b, up_weight, down_weight)
    )

    moving = [swap(up_other), swap(down_other)]
    attended_other, branch_other = swap(attended), swap(grad_branch)
    grad_q, grad_own, sent = attention_backward(at, queries, own, sibling, weights, heads_out, linv, grad_att)

    moving, attended_other, branch_other, sent = hold(moving, attended_other, branch_other, sent)
    arrived = swap(sent)
    pieces = [(up_mine, moving[0]), (down_mine, moving[1])]
    away = [add(mine[2:], other[2:]) for mine, other in pieces]
    halved = meet_parts(away, 0, 0)
    arrived, away = hold(arrived, away)
    keep0, away0, keep1, away1 = squares(
        at, grad_q, grad_own, sent, arrived, grad_branch, branch_other, normed, normed_other, attended, attended_other
    )

    away, grad_hidden = hold([away0, away1], grad_hidden)
    square_halved = meet_parts(away, 0, 0)
    input_grad, small = input_gradient(
        grad_q, grad_own, arrived, qkv_weight, both, grad_hidden, gains, vec_grads, up_b_grad
    )

    halved, square_halved, small, input_grad = hold(halved, square_halved, small, input_grad)
    away = [add(mine[1], other[1], half[1]) for (mine, other), half in zip(pieces, halved)]
    square_away = [add(keep[1], half[1]) for keep, half in zip((keep0, keep1), square_halved)]
    square_quartered = meet_parts(square_away, 0, 1)
    quartered = meet_parts(away, 0, 1)

    def ring_sum(pieces, halved, quartered):
        return [
            add(mine[0], other[0], half[0], quarter)
            for (mine, other), half, quarter in zip(pieces, halved, quartered)
        ]

    ff_own = ring_sum(pieces, halved, quartered)
    square_quartered, ff_own, small = hold(square_quartered, ff_own, small)
    owns = [add(k[0], h[0], q) for k, h, q in zip((keep0, keep1), square_halved, square_quartered)]
    blocks = [
        jnp.concatenate([f, o], axis=0).reshape(NF // 2 + 1, 4, QUARTER // 4, D) for f, o in zip(ff_own, owns)
    ]
    places = [x_place, y]
    first = 1 + 2 * core
    keep = [(block_of(b, p), block_of(b, p ^ (4 - first))) for b, p in zip(blocks, places)]
    away = [jnp.stack([block_of(b, p ^ first), block_of(b, p ^ 2)]) for b, p in zip(blocks, places)]
    keep, away, small = hold(keep, away, small)
    one_way = meet(away[0], "x", 0)
    other_way, small = meet_with(away[1], small, "y", 0)

    one_way, other_way, small = hold(one_way, other_way, small)
    halved = [one_way, other_way]
    away, small = hold([add(k[1], h[1]) for k, h in zip(keep, halved)], small)
    one_way = meet(away[0], "x", 1)
    other_way, small = meet_with(away[1], small, "y", 1)

    one_way, other_way, small = hold(one_way, other_way, small)
    quartered = [one_way, other_way]
    ends = [add(k[0], h[0], q) for k, h, q in zip(keep, halved, quartered)]
    for step in range(2):
        ends, small = hold(ends, small)
        one_way, small = meet_with(ends[0], small, "z", step)
        other_way = meet(ends[1], "x", step)
        one_way, other_way, small = hold(one_way, other_way, small)
        ends = [ends[0] + one_way, ends[1] + other_way]

    ends, small, output, input_grad = hold(ends, small, output, input_grad)
    one_way, small = meet_with(ends[0], small, "x", 1)
    other_way = meet(ends[1], "y", 1)

    one_way, other_way, small = hold(one_way, other_way, small)
    pairs = [jnp.stack([ends[0], one_way]), jnp.stack([ends[1], other_way])]
    pairs, small = hold(pairs, small)
    one_way, small = meet_with(pairs[0], small, "x", 0)
    other_way = meet(pairs[1], "y", 0)

    one_way, other_way, small = hold(one_way, other_way, small)
    owns = []
    for pair, more, p, empty in zip(pairs, (one_way, other_way), places, blocks):
        full = jnp.zeros_like(empty)
        for value, index in ((pair[0], p), (pair[1], p ^ (4 - first)), (more[0], p ^ first), (more[1], p ^ 2)):
            full = put_block(full, value, index)
        owns.append(full.reshape(NF // 2 + 1, QUARTER, D))
    owns, small, output, input_grad = hold(owns, small, output, input_grad)
    arrived = meet_parts(owns, 0, 1)
    returned = send_from_scene(jnp.concatenate([output, input_grad], axis=1))

    arrived, returned = hold(arrived, returned)
    pairs = [jnp.stack([o, a]) for o, a in zip(owns, arrived)]
    pairs, small = hold(pairs, small)
    got = meet_parts(pairs, 0, 0)
    own_other = [swap(v) for v in pairs]
    small_other = swap(small)
    placed = place(at, pairs, True, False)
    returned = take_from_scene(returned, block)
    output, input_grad = returned[:, :, :D], returned[:, :, D:]

    own_other, small_other, placed, output, input_grad = hold(own_other, small_other, placed, output, input_grad)
    small = small + small_other
    placed = place(at, own_other, False, False, placed)
    got, placed = hold(got, placed)
    got_other = [swap(v) for v in got]
    placed = place(at, got, True, True, placed)
    d_up, d_down, d_qkv, d_out = place(at, got_other, False, True, placed)
    return (
        output, input_grad, small[4], small[5], d_qkv, small[6], small[7], d_out,
        small[0], small[1], small[2], d_up, small[8:12].reshape(FF), d_down, small[3],
    )


def solution(mesh):
    fine = Mesh(mesh.devices.reshape(4, 2, 2, 4, 2), AXES)
    rows = P(("y", "xl", "c"), ("z", "xh"), None)
    placed = (rows, P(("y", "xl", "c"))) + (P(),) * 13 + (rows,)
    return jax.shard_map(
        body, mesh=fine, in_specs=placed, out_specs=(rows, rows) + (P(),) * 13, check_vma=False
    )
```

```python
import functools
import itertools
import math

import jax
import jax.numpy as jnp
from jax import lax
from jax.experimental import pallas as pl
from jax.experimental.pallas import tpu as pltpu
from jax.sharding import Mesh
from jax.sharding import PartitionSpec as P

HEADS = 12
HEAD_DIM = 64
VIEW_TOK = 128
VIEWS_MAX = 8
D = 768
FF = 3072
BLK = 144
SLOTS = 4
ROWS = BLK * SLOTS
KEYS = 2 * ROWS
PAIRS = HEADS // 2
LANES = 128
FCHUNK = 768
QROWS = 288
QUARTER = D // 4
NF = FF // FCHUNK

bf16 = jnp.bfloat16
f32 = jnp.float32
epsilon = 1e-05
masked_score = -1e30
GELU_C = math.sqrt(2.0 / math.pi)
GELU_A = 0.044715

AXES = ("y", "xl", "c", "z", "xh")
MIB = 1024 * 1024


def mm(a, b):
    return lax.dot_general(a, b, (((1,), (0,)), ((), ())), preferred_element_type=f32)


def mm_nt(a, b):
    return lax.dot_general(a, b, (((1,), (1,)), ((), ())), preferred_element_type=f32)


def mm_tn(a, b):
    return lax.dot_general(a, b, (((0,), (0,)), ((), ())), preferred_element_type=f32)


def lane_row(at, first, last):
    lane = lax.broadcasted_iota(jnp.int32, (1, LANES), 1)
    return jnp.where((lane >= first) & (lane < last), 1.0, 0.0).astype(at)


def attention_forward_kernel(q_ref, ko_ref, vo_ref, ks_ref, vs_ref, mask_ref, p_ref, o_ref, linv_ref, att_ref):
    half = [lane_row(bf16, 0, 64), lane_row(bf16, 64, 128)]
    unit = [lane_row(bf16, 64, 65), lane_row(bf16, 0, 1)]
    q = q_ref[...]
    k = jnp.concatenate([ko_ref[...], ks_ref[...]], axis=0)
    v = jnp.concatenate([vo_ref[...], vs_ref[...]], axis=0)
    mask = mask_ref[...]
    lane = lax.broadcasted_iota(jnp.int32, (QROWS, LANES), 1)
    q_now = [q * half[h] + unit[h] for h in range(2)]
    k_now = [k * half[h] + mask * unit[h] for h in range(2)]
    v_now = [v * half[h] + unit[h] for h in range(2)]
    items = [(slice(s * QROWS, (s + 1) * QROWS), h) for s in range(ROWS // QROWS) for h in range(2)]
    done = {}

    def product(number, weights):
        rows, h = items[number]
        out = mm(weights, v_now[h])
        inv = 1.0 / (out[:, 64:65] if h == 0 else out[:, 0:1])
        done[h] = (out * inv, jnp.broadcast_to(inv, (QROWS, LANES)))
        if h == 1:
            out = jnp.where(lane < 64, done[0][0], done[1][0])
            o_ref[rows, :] = out
            att_ref[rows, :] = out.astype(bf16)
            linv_ref[rows, :] = jnp.where(lane < 64, done[0][1], done[1][1])

    scores = mm_nt(q_now[0][items[0][0]], k_now[0])
    before = None
    for number, (rows, h) in enumerate(items):
        following = None
        if number + 1 < len(items):
            next_rows, next_h = items[number + 1]
            following = mm_nt(q_now[next_h][next_rows], k_now[next_h])
        top = jnp.max(scores, axis=1, keepdims=True)
        weights = jnp.exp((scores - top) * 0.125).astype(bf16)
        p_ref[h, rows, :] = weights
        if before is not None:
            product(number - 1, before)
        before, scores = weights, following
    product(len(items) - 1, before)


def head_columns(base):
    return pl.BlockSpec((ROWS, LANES), lambda i, f=base: (0, f + i))


def attention_forward(queries, own, sibling, mask):
    col = head_columns
    return pl.pallas_call(
        attention_forward_kernel,
        grid=(PAIRS,),
        in_specs=[col(0), col(0), col(PAIRS), col(0), col(PAIRS), pl.BlockSpec((KEYS, LANES), lambda i: (0, 0))],
        out_specs=[pl.BlockSpec((2, ROWS, KEYS), lambda i: (i, 0, 0)), col(0), col(0), col(0)],
        out_shape=[
            jax.ShapeDtypeStruct((HEADS, ROWS, KEYS), bf16),
            jax.ShapeDtypeStruct((ROWS, D), f32),
            jax.ShapeDtypeStruct((ROWS, D), f32),
            jax.ShapeDtypeStruct((ROWS, D), bf16),
        ],
        compiler_params=pltpu.CompilerParams(vmem_limit_bytes=60 * MIB),
        cost_estimate=pl.CostEstimate(flops=16 * ROWS * KEYS * D, bytes_accessed=20_000_000, transcendentals=HEADS * ROWS * KEYS),
        name="attention_forward",
    )(queries, own, own, sibling, sibling, mask)


def attention_backward_kernel(
    at_ref, q_ref, ko_ref, vo_ref, ks_ref, vs_ref, p_ref, o_ref, linv_ref, g_ref, gq_ref, gown_ref, sent_ref
):
    half = [lane_row(bf16, 0, 64), lane_row(bf16, 64, 128)]
    two = [lane_row(bf16, 64, 66), lane_row(bf16, 0, 2)]
    lane = lax.broadcasted_iota(jnp.int32, (ROWS, LANES), 1)
    k = jnp.concatenate([ko_ref[...], ks_ref[...]], axis=0)
    v = jnp.concatenate([vo_ref[...], vs_ref[...]], axis=0)
    gs = g_ref[...].astype(f32) * linv_ref[...]
    prod = gs * o_ref[...]
    g_now, v_now = [], []
    for h in range(2):
        mine = (lane < 64) if h == 0 else (lane >= 64)
        base = 64 if h == 0 else 0
        delta = jnp.sum(jnp.where(mine, prod, 0.0), axis=1, keepdims=True)
        high = delta.astype(bf16).astype(f32)
        columns = jnp.where(lane == base, -high, jnp.where(lane == base + 1, high - delta, 0.0))
        g_now.append(jnp.where(mine, gs, columns).astype(bf16))
        v_now.append(v * half[h] + two[h])
    g_turned, q_turned = gs.astype(bf16).T, q_ref[...].T
    head = lambda turned, h: turned[64 * h : 64 * h + 64]
    grad_score = lambda h, diff: (p_ref[h].astype(f32) * diff).astype(bf16)
    diff = mm_nt(g_now[0], v_now[0])
    gv0 = mm(head(g_turned, 0), p_ref[0])
    gs0 = grad_score(0, diff)
    diff = mm_nt(g_now[1], v_now[1])
    gv1 = mm(head(g_turned, 1), p_ref[1])
    gs1 = grad_score(1, diff)
    gk0, gq0 = mm(head(q_turned, 0), gs0), mm(gs0, k)
    gk1, gq1 = mm(head(q_turned, 1), gs1), mm(gs1, k)
    gq = (jnp.where(lane < 64, gq0, gq1) * 0.125).astype(bf16)
    gk = (jnp.concatenate([gk0, gk1], axis=0) * 0.125).T.astype(bf16)
    gv = jnp.concatenate([gv0, gv1], axis=0).T.astype(bf16)
    gq_ref[...] = gq
    gown_ref[0], gown_ref[1] = gk[:ROWS], gv[:ROWS]
    sent_ref[0], sent_ref[1] = gk[ROWS:], gv[ROWS:]
    sent_ref[2] = jnp.where(at_ref[0] == 0, gv[:ROWS], gk[:ROWS])
    sent_ref[3] = gq


def attention_backward(at, queries, own, sibling, weights, heads_out, linv, grad_att):
    col = lambda base: pl.BlockSpec((ROWS, LANES), lambda i, at: (0, base + i))
    several = lambda count: pl.BlockSpec((count, ROWS, LANES), lambda i, at: (0, 0, i))
    return pl.pallas_call(
        attention_backward_kernel,
        grid_spec=pltpu.PrefetchScalarGridSpec(
            num_scalar_prefetch=1, grid=(PAIRS,),
            in_specs=[
                col(0), col(0), col(PAIRS), col(0), col(PAIRS),
                pl.BlockSpec((2, ROWS, KEYS), lambda i, at: (i, 0, 0)),
                col(0), col(0), col(0),
            ],
            out_specs=[col(0), several(2), several(4)],
        ),
        out_shape=[jax.ShapeDtypeStruct(shape, bf16) for shape in ((ROWS, D), (2, ROWS, D), (4, ROWS, D))],
        compiler_params=pltpu.CompilerParams(vmem_limit_bytes=60 * MIB),
        cost_estimate=pl.CostEstimate(flops=32 * ROWS * KEYS * D, bytes_accessed=25_000_000, transcendentals=0),
        name="attention_backward",
    )(at, queries, own, own, sibling, sibling, weights, heads_out, linv, grad_att)


def quarter_blocks(place, core):
    first = 1 + 2 * core
    return place, place ^ (4 - first), place ^ first, place ^ 2


def quarter_rows(block):
    return pl.ds(pl.multiple_of(block * QUARTER, QUARTER), QUARTER)


def put_quarters(ref, buffer, place, core):
    for index, block in enumerate(quarter_blocks(place, core)):
        ref[index, 0] = buffer[quarter_rows(block), :]


def feed_forward_kernel(
    at_ref, att_ref, x_ref, g_ref, ow_ref, vec_ref, upb_ref, up_ref, down_ref,
    out_ref, gh_ref, gb_ref, gatt_ref, up_other_ref, up_mine_ref, down_other_ref, down_mine_ref, vecg_ref, upbg_ref,
    hidden, xhat, rstd_s, normed2, y_acc, gn_acc, buffer,
):
    step = pl.program_id(0)
    out_bias, gain, shift, down_bias = (vec_ref[r : r + 1, :] for r in range(4))

    @pl.when(step == 0)
    def _():
        h = x_ref[...].astype(f32) + mm(att_ref[...], ow_ref[...]) + out_bias
        hidden[...] = h
        centred = h - jnp.mean(h, axis=1, keepdims=True)
        rstd = lax.rsqrt(jnp.mean(centred * centred, axis=1, keepdims=True) + epsilon)
        xh = centred * rstd
        xhat[...] = xh
        rstd_s[...] = jnp.broadcast_to(rstd, (ROWS, LANES))
        normed2[...] = (xh * gain + shift).astype(bf16)
        y_acc[...] = jnp.zeros_like(y_acc)
        gn_acc[...] = jnp.zeros_like(gn_acc)

    g = g_ref[...]
    n2 = normed2[...]
    u = mm(n2, up_ref[...]) + upb_ref[0]
    ga = mm_nt(g, down_ref[...])
    u2 = u * u
    t = jnp.tanh(u * (GELU_C + (GELU_C * GELU_A) * u2))
    hp = 0.5 + 0.5 * t
    active = (u * hp).astype(bf16)
    slope = hp + (0.5 * u) * (1.0 - t * t) * (GELU_C + (3.0 * GELU_C * GELU_A) * u2)
    gu = (ga * slope).astype(bf16)
    y_acc[...] += mm(active, down_ref[...])
    gn_acc[...] += mm_nt(gu, up_ref[...])
    upbg_ref[0] = jnp.sum(gu.astype(f32), axis=0, keepdims=True)
    for part, value, other_ref, mine_ref in (
        (0, mm_tn(n2, gu), up_other_ref, up_mine_ref), (1, mm_tn(active, g), down_other_ref, down_mine_ref),
    ):
        buffer[...] = value.astype(bf16)

        @pl.when(step < NF // 2)
        def _():
            put_quarters(other_ref, buffer, at_ref[1 + part], 1 - at_ref[0])

        @pl.when(step >= NF // 2)
        def _():
            put_quarters(mine_ref, buffer, at_ref[1 + part], at_ref[0])

    @pl.when(step == NF - 1)
    def _():
        out_ref[...] = (hidden[...] + y_acc[...] + down_bias).astype(bf16)
        gn = gn_acc[...]
        xh = xhat[...]
        gf = g_ref[...].astype(f32)
        vecg_ref[...] = jnp.zeros_like(vecg_ref)
        vecg_ref[1:2, :] = jnp.sum(gn * xh, axis=0, keepdims=True)
        vecg_ref[2:3, :] = jnp.sum(gn, axis=0, keepdims=True)
        vecg_ref[3:4, :] = jnp.sum(gf, axis=0, keepdims=True)
        gx = gn * gain
        mean1 = jnp.mean(gx, axis=1, keepdims=True)
        mean2 = jnp.mean(gx * xh, axis=1, keepdims=True)
        gh = gf + rstd_s[:, 0:1] * (gx - mean1 - xh * mean2)
        gh_ref[...] = gh
        vecg_ref[0:1, :] = jnp.sum(gh, axis=0, keepdims=True)
        gb = gh.astype(bf16)
        gb_ref[...] = gb
        gatt_ref[...] = mm_nt(gb, ow_ref[...]).astype(bf16)


def whole(*shape):
    return pl.BlockSpec(shape, lambda s, at: (0,) * len(shape))


TOKEN_SPEC = pl.BlockSpec((ROWS, D), lambda s, at: (0, 0))
COTANGENT_SPEC = pl.BlockSpec((ROWS, D), lambda s, at: (0, 1))


def feed_forward(at, attended, both, out_w, vecs, up_b, up_w, down_w):
    shape = jax.ShapeDtypeStruct
    chunk = lambda s, at: (2 * (1 - at[0]) + s) % NF
    other = pl.BlockSpec((4, 1, QUARTER, D), lambda s, at: (0, jnp.minimum(s, NF // 2 - 1), 0, 0))
    mine = pl.BlockSpec((4, 1, QUARTER, D), lambda s, at: (0, jnp.maximum(s - NF // 2, 0), 0, 0))
    return pl.pallas_call(
        feed_forward_kernel,
        grid_spec=pltpu.PrefetchScalarGridSpec(
            num_scalar_prefetch=1,
            grid=(NF,),
            in_specs=[
                whole(ROWS, D), TOKEN_SPEC, COTANGENT_SPEC, whole(D, D), whole(8, D),
                pl.BlockSpec((1, 1, FCHUNK), lambda s, at: (chunk(s, at), 0, 0)),
                pl.BlockSpec((D, FCHUNK), lambda s, at: (0, chunk(s, at))),
                pl.BlockSpec((FCHUNK, D), lambda s, at: (chunk(s, at), 0)),
            ],
            out_specs=[whole(ROWS, D)] * 4
            + [other, mine, other, mine, whole(8, D), pl.BlockSpec((1, 1, FCHUNK), lambda s, at: (chunk(s, at), 0, 0))],
            scratch_shapes=[
                pltpu.VMEM((ROWS, D), f32), pltpu.VMEM((ROWS, D), f32), pltpu.VMEM((ROWS, LANES), f32),
                pltpu.VMEM((ROWS, D), bf16), pltpu.VMEM((ROWS, D), f32), pltpu.VMEM((ROWS, D), f32),
                pltpu.VMEM((D, D), bf16),
            ],
        ),
        out_shape=[
            shape((ROWS, D), bf16), shape((ROWS, D), f32), shape((ROWS, D), bf16), shape((ROWS, D), bf16),
        ]
        + [shape((4, NF // 2, QUARTER, D), bf16)] * 4
        + [shape((8, D), f32), shape((NF, 1, FCHUNK), f32)],
        compiler_params=pltpu.CompilerParams(vmem_limit_bytes=60 * MIB),
        cost_estimate=pl.CostEstimate(flops=12 * ROWS * D * FF, bytes_accessed=30_000_000, transcendentals=ROWS * FF),
        name="feed_forward",
    )(at, attended, both, both, out_w, vecs, up_b, up_w, down_w)


def squares_kernel(
    at_ref, gq_ref, own_ref, other_ref, arrived_ref, arrived_own_ref, arrived_gq_ref, gb_ref, gb_other_ref,
    normed_ref, normed_other_ref, att_ref, att_other_ref, keep0_ref, away0_ref, keep1_ref, away1_ref,
    joined, joined_other, buffer,
):
    core = at_ref[0]

    def product(part, left, left_other, right, right_other):
        buffer[...] = (mm_tn(left[...], right[...]) + mm_tn(left_other[...], right_other[...])).astype(bf16)
        keep_ref, away_ref = ((keep0_ref, away0_ref), (keep1_ref, away1_ref))[part]
        for index, block in enumerate(quarter_blocks(at_ref[1 + part], core)):
            (keep_ref if index < 2 else away_ref)[index % 2, 0] = buffer[quarter_rows(block), :]

    joined[...] = own_ref[0] + arrived_ref[0]
    joined_other[...] = arrived_own_ref[0] + other_ref[0]

    @pl.when(core == 0)
    def _():
        product(0, normed_ref, normed_other_ref, gq_ref, arrived_gq_ref.at[0])
        product(1, normed_ref, normed_other_ref, joined, joined_other)

    @pl.when(core != 0)
    def _():
        product(0, normed_ref, normed_other_ref, joined, joined_other)
        product(1, att_ref, att_other_ref, gb_ref, gb_other_ref)


def squares(at, gq, own, sent, arrived, *pairs):
    rows = whole(ROWS, D)
    pick = pl.BlockSpec((1, ROWS, D), lambda s, at: (at[0], 0, 0))
    number = lambda n: pl.BlockSpec((1, ROWS, D), lambda s, at: (n, 0, 0))
    return pl.pallas_call(
        squares_kernel,
        grid_spec=pltpu.PrefetchScalarGridSpec(
            num_scalar_prefetch=1, grid=(1,),
            in_specs=[rows, pick, pick, pick, number(2), number(3)] + [rows] * 6,
            out_specs=[whole(2, 1, QUARTER, D)] * 4,
            scratch_shapes=[pltpu.VMEM((ROWS, D), bf16), pltpu.VMEM((ROWS, D), bf16), pltpu.VMEM((D, D), bf16)],
        ),
        out_shape=[jax.ShapeDtypeStruct((2, 1, QUARTER, D), bf16)] * 4,
        compiler_params=pltpu.CompilerParams(vmem_limit_bytes=44 * MIB),
        cost_estimate=pl.CostEstimate(flops=8 * ROWS * D * D, bytes_accessed=13_000_000, transcendentals=0),
        name="squares",
    )(at, gq, own, sent, arrived, arrived, arrived, *pairs)


def input_grad_kernel(
    gq_ref, own_ref, swapped_ref, w_ref, x_ref, gh_ref, gain_ref, vecg_ref, upbg_ref, out_ref, small_ref, right
):
    step = pl.program_id(0)
    right[:, :D] = gq_ref[...]
    right[:, D : 2 * D] = own_ref[0] + swapped_ref[0]
    right[:, 2 * D :] = own_ref[1] + swapped_ref[1]
    grad_normed = mm_nt(right[...], w_ref[...])
    source = x_ref[...].astype(f32)
    centred = source - jnp.mean(source, axis=1, keepdims=True)
    rstd = lax.rsqrt(jnp.mean(centred * centred, axis=1, keepdims=True) + epsilon)
    xhat = centred * rstd
    gx = grad_normed * gain_ref[0:1, :]
    mean1 = jnp.mean(gx, axis=1, keepdims=True)
    mean2 = jnp.mean(gx * xhat, axis=1, keepdims=True)
    out_ref[...] = (gh_ref[...] + rstd * (gx - mean1 - xhat * mean2)).astype(bf16)

    @pl.when(step == 0)
    def _():
        small_ref[...] = jnp.zeros_like(small_ref)
        small_ref[0:4, :] = vecg_ref[0:4, :]
        for f in range(NF):
            small_ref[8 + f : 9 + f, :] = upbg_ref[f]

    small_ref[4:5, :] += jnp.sum(grad_normed * xhat, axis=0, keepdims=True)
    small_ref[5:6, :] += jnp.sum(grad_normed, axis=0, keepdims=True)
    small_ref[6:7, :] += jnp.sum(right[:, :D].astype(f32), axis=0, keepdims=True)
    small_ref[7:8, :] += jnp.sum(right[:, 2 * D :].astype(f32), axis=0, keepdims=True)


def input_gradient(gq, own, swapped, qkv_w, both, grad_hidden, gain, vec_grads, up_b_grad):
    steps = 3
    length = ROWS // steps
    rows = pl.BlockSpec((length, D), lambda s: (s, 0))
    pair = pl.BlockSpec((2, length, D), lambda s: (0, s, 0))
    fixed = lambda *shape: pl.BlockSpec(shape, lambda s: (0,) * len(shape))
    return pl.pallas_call(
        input_grad_kernel,
        grid=(steps,),
        in_specs=[rows, pair, pair, fixed(D, 3 * D), rows, rows, fixed(8, D), fixed(8, D), fixed(NF, 1, FCHUNK)],
        out_specs=[rows, fixed(16, D)],
        out_shape=[jax.ShapeDtypeStruct((ROWS, D), bf16), jax.ShapeDtypeStruct((16, D), f32)],
        scratch_shapes=[pltpu.VMEM((length, 3 * D), bf16)],
        compiler_params=pltpu.CompilerParams(vmem_limit_bytes=60 * MIB),
        cost_estimate=pl.CostEstimate(flops=6 * ROWS * D * D, bytes_accessed=10_000_000, transcendentals=0),
        name="input_gradient",
    )(gq, own, swapped, qkv_w, both, grad_hidden, gain, vec_grads, up_b_grad)


def place_kernel(mine, late, at_ref, source0_ref, source1_ref, *refs):
    up_ref, down_ref, qkv_ref, out_ref, pieces, tiles, in_sems, out_sems = refs[-8:]
    half = at_ref[0] if mine else 1 - at_ref[0]
    sources = (source0_ref, source1_ref)
    plan = []
    for j in range(2):
        block = 2 * half + j
        columns = pl.ds(pl.multiple_of(block * D, D), D)
        for s in range(2):
            rows = [
                quarter_rows(quarter_blocks(at_ref[1 + part], half)[s + (2 if late else 0)]) for part in range(2)
            ]
            down_rows = pl.ds(pl.multiple_of(block * D + rows[1].start, QUARTER), QUARTER)
            plan.append((sources[0].at[s, j], up_ref.at[rows[0], columns], None))
            plan.append((sources[1].at[s, j], down_ref.at[down_rows, :], None))
            last = out_ref.at[rows[j], :] if j == 1 else None
            square_columns = columns if j == 0 else pl.ds(D, D)
            plan.append((sources[j].at[s, 2], qkv_ref.at[rows[j], square_columns], last))
    loads = []
    for number, (source, _, _) in enumerate(plan):
        loads.append(pltpu.make_async_copy(source, pieces.at[number], in_sems.at[number]))
        loads[-1].start()
    for number, (_, target, last) in enumerate(plan):
        loads[number].wait()
        tiles[number] = pieces[number].astype(f32)

        def start(to, number=number):
            pltpu.make_async_copy(tiles.at[number], to, out_sems.at[number]).start()

        if last is None:
            start(target)
        else:
            pl.when(half == 0)(lambda: start(target))
            pl.when(half != 0)(lambda: start(last))
    for number, (_, target, _) in enumerate(plan):
        pltpu.make_async_copy(tiles.at[number], target, out_sems.at[number]).wait()


def place(at, pieces, mine, late, before=()):
    shape = jax.ShapeDtypeStruct
    anywhere = pl.BlockSpec(memory_space=pl.ANY)
    return pl.pallas_call(
        functools.partial(place_kernel, mine, late),
        grid_spec=pltpu.PrefetchScalarGridSpec(
            num_scalar_prefetch=1, grid=(1,),
            in_specs=[anywhere] * (2 + len(before)),
            out_specs=[anywhere] * 4,
            scratch_shapes=[
                pltpu.VMEM((12, QUARTER, D), bf16), pltpu.VMEM((12, QUARTER, D), f32),
                pltpu.SemaphoreType.DMA((12,)), pltpu.SemaphoreType.DMA((12,)),
            ],
        ),
        out_shape=[shape((D, FF), f32), shape((FF, D), f32), shape((D, 3 * D), f32), shape((D, D), f32)],
        input_output_aliases={3 + index: index for index in range(len(before))},
        compiler_params=pltpu.CompilerParams(vmem_limit_bytes=16 * MIB),
        cost_estimate=pl.CostEstimate(flops=0, bytes_accessed=11_000_000, transcendentals=0),
        name="place_late" if late else "place_early",
    )(at, *pieces, *before)


def linear(y, xl, c, z, xh):
    return (((y * 2 + xl) * 2 + c) * 4 + z) * 2 + xh


def scene_pairs(slot):
    pairs = []
    for y, xl, c, z, xh in itertools.product(range(4), range(2), range(2), range(4), range(2)):
        target = z ^ slot ^ (0 if xh == c else 2)
        if target < 3:
            pairs.append((linear(y, xl, c, z, xh), linear(y, xl, xh, target, c)))
    return pairs


def to_scene(values, z, flip):
    pieces = []
    for slot in range(SLOTS):
        scene = jnp.minimum(z ^ slot ^ flip, 2)
        pieces.append(lax.ppermute(lax.dynamic_index_in_dim(values, scene, 0, keepdims=False), AXES, scene_pairs(slot)))
    return pieces


def turn(values):
    pairs = [
        (linear(y, xl, c, z, xh), linear(y, xl, xh, z, c))
        for y, xl, c, z, xh in itertools.product(range(4), range(2), range(2), range(4), range(2))
    ]
    return lax.ppermute(values, AXES, pairs)


def slot_block(values, offset, flip):
    return lax.dynamic_slice_in_dim(values, (offset ^ flip) * BLK, BLK, 0)


def for_home(stayed, first, second, both, z, core):
    pieces = jnp.stack([stayed, jnp.where(core == 0, first, second), both, jnp.where(core == 0, second, first)])
    return jnp.stack([lax.dynamic_index_in_dim(pieces, z ^ scene, 0, keepdims=False) for scene in range(3)])


SWAP = ((0, 1), (1, 0))
MASKS = ((1, 3), (3, 1))


def exchange(value, move):
    pairs = []
    for place in itertools.product(range(4), range(4), range(4), range(2)):
        ends = [linear(y, x % 2, c, z, x // 2) for x, y, z, c in (place, move(*place))]
        pairs.append(tuple(ends))
    return lax.ppermute(value, AXES, pairs)


def meet(value, axis, step):
    def move(x, y, z, c):
        at = {"x": x, "y": y, "z": z}
        at[axis] = at[axis] ^ MASKS[c][step]
        return at["x"], at["y"], at["z"], c

    return exchange(value, move)


def swap(value):
    return lax.ppermute(value, "c", SWAP)


ORDERS = ("yxz", "zyx")


def meet_parts(values, stage, step):
    return [meet(value, ORDERS[part][stage], step) for part, value in enumerate(values)]


def add(*terms):
    return functools.reduce(jnp.add, [term.astype(f32) for term in terms]).astype(bf16)


def block_of(blocks, index):
    return lax.dynamic_index_in_dim(blocks, index, 1, keepdims=False)


def put_block(blocks, value, index):
    return lax.dynamic_update_index_in_dim(blocks, value, index, 1)


SMALL = 16


def meet_with(value, small, axis, step):
    high = lax.reduce_precision(small, 8, 7)
    low = lax.reduce_precision(small - high, 8, 7)
    rows = value.reshape(-1, D)
    message = jnp.concatenate([rows, high.astype(bf16), low.astype(bf16)], axis=0)
    arrived = meet(message, axis, step)
    count = rows.shape[0]
    other = arrived[count : count + SMALL].astype(f32) + arrived[count + SMALL :].astype(f32)
    return arrived[:count].reshape(value.shape), (high + low) + other


def hold(*values):
    return lax.optimization_barrier(values)


def body(
    tokens, view_counts, ln1_gain, ln1_shift, qkv_weight, query_bias, value_bias, out_weight, out_bias,
    ln2_gain, ln2_shift, up_weight, up_bias, down_weight, down_bias, cotangent,
):
    core, z, xh = lax.axis_index("c"), lax.axis_index("z"), lax.axis_index("xh")

    flip = jnp.where(xh == core, 0, 2)
    views = jnp.broadcast_to(view_counts.astype(bf16)[:, None, None], (3, BLK, LANES))
    pieces = to_scene(jnp.concatenate([tokens, cotangent, views], axis=2), z, flip)
    vecs = jnp.concatenate([jnp.stack([out_bias, ln2_gain, ln2_shift, down_bias]), jnp.zeros((4, D), f32)])
    gains = jnp.broadcast_to(ln1_gain[None, :], (8, D))
    weight_q, weight_kv = qkv_weight[:, :D], qkv_weight[:, D:]
    pieces, vecs, gains, weight_q, weight_kv = hold(pieces, vecs, gains, weight_q, weight_kv)
    both = jnp.concatenate([piece[:, : 2 * D] for piece in pieces], axis=0)
    views = pieces[0][0, 2 * D].astype(f32)
    x = both[:, :D]

    row = jnp.arange(ROWS, dtype=jnp.int32)
    slot = row // BLK
    position = jnp.concatenate([
        (2 * (z ^ slot ^ flip) + core) * BLK + row % BLK,
        (2 * (z ^ slot ^ (2 - flip)) + 1 - core) * BLK + row % BLK,
    ])
    usable = (position.astype(f32) < views * VIEW_TOK) | (position >= VIEWS_MAX * VIEW_TOK)
    mask = jnp.broadcast_to(jnp.where(usable, 0.0, masked_score).astype(bf16)[:, None], (KEYS, LANES))

    source = x.astype(f32)
    centred = source - jnp.mean(source, axis=1, keepdims=True)
    rstd = lax.rsqrt(jnp.mean(centred * centred, axis=1, keepdims=True) + epsilon)
    normed = (centred * rstd * ln1_gain + ln1_shift).astype(bf16)
    product = lambda weight: jnp.dot(normed, weight, preferred_element_type=f32)
    kv_bias = jnp.concatenate([jnp.zeros((D,), f32), value_bias])
    own = (product(weight_kv) + kv_bias).astype(bf16)
    sibling = swap(own)
    normed_other = swap(normed)
    queries = (product(weight_q) + query_bias).astype(bf16)
    weights, heads_out, linv, attended = attention_forward(queries, own, sibling, mask)

    up_b = up_bias.reshape(NF, 1, FCHUNK)
    y = lax.axis_index("y")
    x_place = lax.axis_index("xh") * 2 + lax.axis_index("xl")
    at = jnp.stack([core, y, z]).astype(jnp.int32)
    output, grad_hidden, grad_branch, grad_att, up_other, up_mine, down_other, down_mine, vec_grads, up_b_grad = (
        feed_forward(at, attended, both, out_weight, vecs, up_b, up_weight, down_weight)
    )

    moving = [swap(up_other), swap(down_other)]
    attended_other, branch_other = swap(attended), swap(grad_branch)
    grad_q, grad_own, sent = attention_backward(at, queries, own, sibling, weights, heads_out, linv, grad_att)

    moving, attended_other, branch_other, sent = hold(moving, attended_other, branch_other, sent)
    arrived = swap(sent)
    pieces = [(up_mine, moving[0]), (down_mine, moving[1])]
    away = [add(mine[2:], other[2:]) for mine, other in pieces]
    halved = meet_parts(away, 0, 0)
    arrived, away = hold(arrived, away)
    keep0, away0, keep1, away1 = squares(
        at, grad_q, grad_own, sent, arrived, grad_branch, branch_other, normed, normed_other, attended, attended_other
    )

    away, grad_hidden = hold([away0, away1], grad_hidden)
    square_halved = meet_parts(away, 0, 0)
    input_grad, small = input_gradient(
        grad_q, grad_own, arrived, qkv_weight, both, grad_hidden, gains, vec_grads, up_b_grad
    )

    halved, square_halved, small, input_grad = hold(halved, square_halved, small, input_grad)
    away = [add(mine[1], other[1], half[1]) for (mine, other), half in zip(pieces, halved)]
    square_away = [add(keep[1], half[1]) for keep, half in zip((keep0, keep1), square_halved)]
    square_quartered = meet_parts(square_away, 0, 1)
    quartered = meet_parts(away, 0, 1)

    def ring_sum(pieces, halved, quartered):
        return [
            add(mine[0], other[0], half[0], quarter)
            for (mine, other), half, quarter in zip(pieces, halved, quartered)
        ]

    ff_own = ring_sum(pieces, halved, quartered)
    square_quartered, ff_own, small = hold(square_quartered, ff_own, small)
    owns = [add(k[0], h[0], q) for k, h, q in zip((keep0, keep1), square_halved, square_quartered)]
    blocks = [
        jnp.concatenate([f, o], axis=0).reshape(NF // 2 + 1, 4, QUARTER // 4, D) for f, o in zip(ff_own, owns)
    ]
    places = [x_place, y]
    first = 1 + 2 * core
    keep = [(block_of(b, p), block_of(b, p ^ (4 - first))) for b, p in zip(blocks, places)]
    away = [jnp.stack([block_of(b, p ^ first), block_of(b, p ^ 2)]) for b, p in zip(blocks, places)]
    second = 4 - first
    back = jnp.concatenate([output, input_grad], axis=1)
    over = jnp.concatenate([slot_block(back, first, flip), slot_block(back, 2, flip)], axis=0)
    keep, away, small, over, back = hold(keep, away, small, over, back)
    over = meet(over, "z", 0)
    one_way = meet(away[0], "x", 0)
    other_way, small = meet_with(away[1], small, "y", 0)

    one_way, other_way, small = hold(one_way, other_way, small)
    halved = [one_way, other_way]
    away, small = hold([add(k[1], h[1]) for k, h in zip(keep, halved)], small)
    one_way = meet(away[0], "x", 1)
    other_way, small = meet_with(away[1], small, "y", 1)

    one_way, other_way, small = hold(one_way, other_way, small)
    quartered = [one_way, other_way]
    ends = [add(k[0], h[0], q) for k, h, q in zip(keep, halved, quartered)]
    for step in range(2):
        ends, small = hold(ends, small)
        one_way, small = meet_with(ends[0], small, "z", step)
        other_way = meet(ends[1], "x", step)
        one_way, other_way, small = hold(one_way, other_way, small)
        ends = [ends[0] + one_way, ends[1] + other_way]

    over_first = over[:BLK]
    over = jnp.concatenate([slot_block(back, second, flip), over[BLK:]], axis=0)
    ends, small, over, over_first = hold(ends, small, over, over_first)
    over = meet(over, "z", 1)
    one_way, small = meet_with(ends[0], small, "x", 1)
    other_way = meet(ends[1], "y", 1)

    one_way, other_way, small = hold(one_way, other_way, small)
    pairs = [jnp.stack([ends[0], one_way]), jnp.stack([ends[1], other_way])]
    pairs, small = hold(pairs, small)
    one_way, small = meet_with(pairs[0], small, "x", 0)
    other_way = meet(pairs[1], "y", 0)

    one_way, other_way, small = hold(one_way, other_way, small)
    owns = []
    for pair, more, p, empty in zip(pairs, (one_way, other_way), places, blocks):
        full = jnp.zeros_like(empty)
        for value, index in ((pair[0], p), (pair[1], p ^ (4 - first)), (more[0], p ^ first), (more[1], p ^ 2)):
            full = put_block(full, value, index)
        owns.append(full.reshape(NF // 2 + 1, QUARTER, D))
    returned = for_home(slot_block(back, 0, flip), over_first, over[:BLK], over[BLK:], z, core)
    owns, small, returned = hold(owns, small, returned)
    arrived = meet_parts(owns, 0, 1)
    returned = turn(returned)

    arrived, small, returned = hold(arrived, small, returned)
    pairs = [jnp.stack([o, a]) for o, a in zip(owns, arrived)]
    pairs, small = hold(pairs, small)
    got = meet_parts(pairs, 0, 0)
    own_other = [swap(v) for v in pairs]
    small_other = swap(small)
    placed = place(at, pairs, True, False)
    output, input_grad = returned[:, :, :D], returned[:, :, D:]

    own_other, small_other, placed, output, input_grad = hold(own_other, small_other, placed, output, input_grad)
    small = small + small_other
    placed = place(at, own_other, False, False, placed)
    got, placed = hold(got, placed)
    got_other = [swap(v) for v in got]
    placed = place(at, got, True, True, placed)
    d_up, d_down, d_qkv, d_out = place(at, got_other, False, True, placed)
    return (
        output, input_grad, small[4], small[5], d_qkv, small[6], small[7], d_out,
        small[0], small[1], small[2], d_up, small[8:12].reshape(FF), d_down, small[3],
    )


def solution(mesh):
    fine = Mesh(mesh.devices.reshape(4, 2, 2, 4, 2), AXES)
    rows = P(("y", "xl", "c"), ("z", "xh"), None)
    placed = (rows, P(("y", "xl", "c"))) + (P(),) * 13 + (rows,)
    return jax.shard_map(
        body, mesh=fine, in_specs=placed, out_specs=(rows, rows) + (P(),) * 13, check_vma=False
    )
```

```python
import functools
import itertools
import math

import jax
import jax.numpy as jnp
from jax import lax
from jax.experimental import pallas as pl
from jax.experimental.pallas import tpu as pltpu
from jax.sharding import Mesh
from jax.sharding import PartitionSpec as P

HEADS = 12
HEAD_DIM = 64
VIEW_TOK = 128
VIEWS_MAX = 8
D = 768
FF = 3072
BLK = 144
SLOTS = 4
ROWS = BLK * SLOTS
KEYS = 2 * ROWS
PAIRS = HEADS // 2
LANES = 128
FCHUNK = 768
QROWS = 288
QUARTER = D // 4
NF = FF // FCHUNK

bf16 = jnp.bfloat16
f32 = jnp.float32
epsilon = 1e-05
masked_score = -1e30
GELU_C = math.sqrt(2.0 / math.pi)
GELU_A = 0.044715

AXES = ("y", "xl", "c", "z", "xh")
MIB = 1024 * 1024


def mm(a, b):
    return lax.dot_general(a, b, (((1,), (0,)), ((), ())), preferred_element_type=f32)


def mm_nt(a, b):
    return lax.dot_general(a, b, (((1,), (1,)), ((), ())), preferred_element_type=f32)


def mm_tn(a, b):
    return lax.dot_general(a, b, (((0,), (0,)), ((), ())), preferred_element_type=f32)


def lane_row(at, first, last):
    lane = lax.broadcasted_iota(jnp.int32, (1, LANES), 1)
    return jnp.where((lane >= first) & (lane < last), 1.0, 0.0).astype(at)


def attention_forward_kernel(q_ref, ko_ref, vo_ref, ks_ref, vs_ref, mask_ref, p_ref, o_ref, linv_ref, att_ref):
    half = [lane_row(bf16, 0, 64), lane_row(bf16, 64, 128)]
    unit = [lane_row(bf16, 64, 65), lane_row(bf16, 0, 1)]
    q = q_ref[...]
    k = jnp.concatenate([ko_ref[...], ks_ref[...]], axis=0)
    v = jnp.concatenate([vo_ref[...], vs_ref[...]], axis=0)
    mask = mask_ref[...]
    lane = lax.broadcasted_iota(jnp.int32, (QROWS, LANES), 1)
    q_now = [q * half[h] + unit[h] for h in range(2)]
    k_now = [k * half[h] + mask * unit[h] for h in range(2)]
    v_now = [v * half[h] + unit[h] for h in range(2)]
    items = [(slice(s * QROWS, (s + 1) * QROWS), h) for s in range(ROWS // QROWS) for h in range(2)]
    done = {}

    def product(number, weights):
        rows, h = items[number]
        out = mm(weights, v_now[h])
        inv = 1.0 / (out[:, 64:65] if h == 0 else out[:, 0:1])
        done[h] = (out * inv, jnp.broadcast_to(inv, (QROWS, LANES)))
        if h == 1:
            out = jnp.where(lane < 64, done[0][0], done[1][0])
            o_ref[rows, :] = out
            att_ref[rows, :] = out.astype(bf16)
            linv_ref[rows, :] = jnp.where(lane < 64, done[0][1], done[1][1])

    scores = mm_nt(q_now[0][items[0][0]], k_now[0])
    before = None
    for number, (rows, h) in enumerate(items):
        following = None
        if number + 1 < len(items):
            next_rows, next_h = items[number + 1]
            following = mm_nt(q_now[next_h][next_rows], k_now[next_h])
        top = jnp.max(scores, axis=1, keepdims=True)
        weights = jnp.exp((scores - top) * 0.125).astype(bf16)
        p_ref[h, rows, :] = weights
        if before is not None:
            product(number - 1, before)
        before, scores = weights, following
    product(len(items) - 1, before)


def head_columns(base):
    return pl.BlockSpec((ROWS, LANES), lambda i, f=base: (0, f + i))


def attention_forward(queries, own, sibling, mask):
    col = head_columns
    return pl.pallas_call(
        attention_forward_kernel,
        grid=(PAIRS,),
        in_specs=[col(0), col(0), col(PAIRS), col(0), col(PAIRS), pl.BlockSpec((KEYS, LANES), lambda i: (0, 0))],
        out_specs=[pl.BlockSpec((2, ROWS, KEYS), lambda i: (i, 0, 0)), col(0), col(0), col(0)],
        out_shape=[
            jax.ShapeDtypeStruct((HEADS, ROWS, KEYS), bf16),
            jax.ShapeDtypeStruct((ROWS, D), f32),
            jax.ShapeDtypeStruct((ROWS, D), f32),
            jax.ShapeDtypeStruct((ROWS, D), bf16),
        ],
        compiler_params=pltpu.CompilerParams(vmem_limit_bytes=60 * MIB),
        cost_estimate=pl.CostEstimate(flops=16 * ROWS * KEYS * D, bytes_accessed=20_000_000, transcendentals=HEADS * ROWS * KEYS),
        name="attention_forward",
    )(queries, own, own, sibling, sibling, mask)


def attention_backward_kernel(
    at_ref, q_ref, ko_ref, vo_ref, ks_ref, vs_ref, p_ref, o_ref, linv_ref, g_ref, gq_ref, gown_ref, sent_ref
):
    half = [lane_row(bf16, 0, 64), lane_row(bf16, 64, 128)]
    two = [lane_row(bf16, 64, 66), lane_row(bf16, 0, 2)]
    lane = lax.broadcasted_iota(jnp.int32, (ROWS, LANES), 1)
    k = jnp.concatenate([ko_ref[...], ks_ref[...]], axis=0)
    v = jnp.concatenate([vo_ref[...], vs_ref[...]], axis=0)
    gs = g_ref[...].astype(f32) * linv_ref[...]
    prod = gs * o_ref[...]
    g_now, v_now = [], []
    for h in range(2):
        mine = (lane < 64) if h == 0 else (lane >= 64)
        base = 64 if h == 0 else 0
        delta = jnp.sum(jnp.where(mine, prod, 0.0), axis=1, keepdims=True)
        high = delta.astype(bf16).astype(f32)
        columns = jnp.where(lane == base, -high, jnp.where(lane == base + 1, high - delta, 0.0))
        g_now.append(jnp.where(mine, gs, columns).astype(bf16))
        v_now.append(v * half[h] + two[h])
    g_turned, q_turned = gs.astype(bf16).T, q_ref[...].T
    head = lambda turned, h: turned[64 * h : 64 * h + 64]
    grad_score = lambda h, diff: (p_ref[h].astype(f32) * diff).astype(bf16)
    diff = mm_nt(g_now[0], v_now[0])
    gv0 = mm(head(g_turned, 0), p_ref[0])
    gs0 = grad_score(0, diff)
    diff = mm_nt(g_now[1], v_now[1])
    gv1 = mm(head(g_turned, 1), p_ref[1])
    gs1 = grad_score(1, diff)
    gk0, gq0 = mm(head(q_turned, 0), gs0), mm(gs0, k)
    gk1, gq1 = mm(head(q_turned, 1), gs1), mm(gs1, k)
    gq = (jnp.where(lane < 64, gq0, gq1) * 0.125).astype(bf16)
    gk = (jnp.concatenate([gk0, gk1], axis=0) * 0.125).T.astype(bf16)
    gv = jnp.concatenate([gv0, gv1], axis=0).T.astype(bf16)
    gq_ref[...] = gq
    gown_ref[0], gown_ref[1] = gk[:ROWS], gv[:ROWS]
    sent_ref[0], sent_ref[1] = gk[ROWS:], gv[ROWS:]
    sent_ref[2] = jnp.where(at_ref[0] == 0, gv[:ROWS], gk[:ROWS])
    sent_ref[3] = gq


def attention_backward(at, queries, own, sibling, weights, heads_out, linv, grad_att):
    col = lambda base: pl.BlockSpec((ROWS, LANES), lambda i, at: (0, base + i))
    several = lambda count: pl.BlockSpec((count, ROWS, LANES), lambda i, at: (0, 0, i))
    return pl.pallas_call(
        attention_backward_kernel,
        grid_spec=pltpu.PrefetchScalarGridSpec(
            num_scalar_prefetch=1, grid=(PAIRS,),
            in_specs=[
                col(0), col(0), col(PAIRS), col(0), col(PAIRS),
                pl.BlockSpec((2, ROWS, KEYS), lambda i, at: (i, 0, 0)),
                col(0), col(0), col(0),
            ],
            out_specs=[col(0), several(2), several(4)],
        ),
        out_shape=[jax.ShapeDtypeStruct(shape, bf16) for shape in ((ROWS, D), (2, ROWS, D), (4, ROWS, D))],
        compiler_params=pltpu.CompilerParams(vmem_limit_bytes=60 * MIB),
        cost_estimate=pl.CostEstimate(flops=32 * ROWS * KEYS * D, bytes_accessed=25_000_000, transcendentals=0),
        name="attention_backward",
    )(at, queries, own, own, sibling, sibling, weights, heads_out, linv, grad_att)


def quarter_blocks(place, core):
    first = 1 + 2 * core
    return place, place ^ (4 - first), place ^ first, place ^ 2


def quarter_rows(block):
    return pl.ds(pl.multiple_of(block * QUARTER, QUARTER), QUARTER)


def put_quarters(ref, buffer, place, core):
    for index, block in enumerate(quarter_blocks(place, core)):
        ref[index, 0] = buffer[quarter_rows(block), :]


def feed_forward_kernel(
    at_ref, att_ref, x_ref, g_ref, ow_ref, vec_ref, upb_ref, up_ref, down_ref,
    out_ref, gh_ref, gb_ref, gatt_ref, up_other_ref, up_mine_ref, down_other_ref, down_mine_ref, vecg_ref, upbg_ref,
    hidden, xhat, rstd_s, normed2, y_acc, gn_acc, buffer,
):
    step = pl.program_id(0)
    out_bias, gain, shift, down_bias = (vec_ref[r : r + 1, :] for r in range(4))

    @pl.when(step == 0)
    def _():
        h = x_ref[...].astype(f32) + mm(att_ref[...], ow_ref[...]) + out_bias
        hidden[...] = h
        centred = h - jnp.mean(h, axis=1, keepdims=True)
        rstd = lax.rsqrt(jnp.mean(centred * centred, axis=1, keepdims=True) + epsilon)
        xh = centred * rstd
        xhat[...] = xh
        rstd_s[...] = jnp.broadcast_to(rstd, (ROWS, LANES))
        normed2[...] = (xh * gain + shift).astype(bf16)
        y_acc[...] = jnp.zeros_like(y_acc)
        gn_acc[...] = jnp.zeros_like(gn_acc)

    g = g_ref[...]
    n2 = normed2[...]
    u = mm(n2, up_ref[...]) + upb_ref[0]
    ga = mm_nt(g, down_ref[...])
    u2 = u * u
    t = jnp.tanh(u * (GELU_C + (GELU_C * GELU_A) * u2))
    hp = 0.5 + 0.5 * t
    active = (u * hp).astype(bf16)
    slope = hp + (0.5 * u) * (1.0 - t * t) * (GELU_C + (3.0 * GELU_C * GELU_A) * u2)
    gu = (ga * slope).astype(bf16)
    y_acc[...] += mm(active, down_ref[...])
    gn_acc[...] += mm_nt(gu, up_ref[...])
    upbg_ref[0] = jnp.sum(gu.astype(f32), axis=0, keepdims=True)
    for part, value, other_ref, mine_ref in (
        (0, mm_tn(n2, gu), up_other_ref, up_mine_ref), (1, mm_tn(active, g), down_other_ref, down_mine_ref),
    ):
        buffer[...] = value.astype(bf16)

        @pl.when(step < NF // 2)
        def _():
            put_quarters(other_ref, buffer, at_ref[1 + part], 1 - at_ref[0])

        @pl.when(step >= NF // 2)
        def _():
            put_quarters(mine_ref, buffer, at_ref[1 + part], at_ref[0])

    @pl.when(step == NF - 1)
    def _():
        out_ref[...] = (hidden[...] + y_acc[...] + down_bias).astype(bf16)
        gn = gn_acc[...]
        xh = xhat[...]
        gf = g_ref[...].astype(f32)
        vecg_ref[...] = jnp.zeros_like(vecg_ref)
        vecg_ref[1:2, :] = jnp.sum(gn * xh, axis=0, keepdims=True)
        vecg_ref[2:3, :] = jnp.sum(gn, axis=0, keepdims=True)
        vecg_ref[3:4, :] = jnp.sum(gf, axis=0, keepdims=True)
        gx = gn * gain
        mean1 = jnp.mean(gx, axis=1, keepdims=True)
        mean2 = jnp.mean(gx * xh, axis=1, keepdims=True)
        gh = gf + rstd_s[:, 0:1] * (gx - mean1 - xh * mean2)
        gh_ref[...] = gh
        vecg_ref[0:1, :] = jnp.sum(gh, axis=0, keepdims=True)
        gb = gh.astype(bf16)
        gb_ref[...] = gb
        gatt_ref[...] = mm_nt(gb, ow_ref[...]).astype(bf16)


def whole(*shape):
    return pl.BlockSpec(shape, lambda s, at: (0,) * len(shape))


TOKEN_SPEC = pl.BlockSpec((ROWS, D), lambda s, at: (0, 0))
COTANGENT_SPEC = pl.BlockSpec((ROWS, D), lambda s, at: (0, 1))


def feed_forward(at, attended, both, out_w, vecs, up_b, up_w, down_w):
    shape = jax.ShapeDtypeStruct
    chunk = lambda s, at: (2 * (1 - at[0]) + s) % NF
    other = pl.BlockSpec((4, 1, QUARTER, D), lambda s, at: (0, jnp.minimum(s, NF // 2 - 1), 0, 0))
    mine = pl.BlockSpec((4, 1, QUARTER, D), lambda s, at: (0, jnp.maximum(s - NF // 2, 0), 0, 0))
    return pl.pallas_call(
        feed_forward_kernel,
        grid_spec=pltpu.PrefetchScalarGridSpec(
            num_scalar_prefetch=1,
            grid=(NF,),
            in_specs=[
                whole(ROWS, D), TOKEN_SPEC, COTANGENT_SPEC, whole(D, D), whole(8, D),
                pl.BlockSpec((1, 1, FCHUNK), lambda s, at: (chunk(s, at), 0, 0)),
                pl.BlockSpec((D, FCHUNK), lambda s, at: (0, chunk(s, at))),
                pl.BlockSpec((FCHUNK, D), lambda s, at: (chunk(s, at), 0)),
            ],
            out_specs=[whole(ROWS, D)] * 4
            + [other, mine, other, mine, whole(8, D), pl.BlockSpec((1, 1, FCHUNK), lambda s, at: (chunk(s, at), 0, 0))],
            scratch_shapes=[
                pltpu.VMEM((ROWS, D), f32), pltpu.VMEM((ROWS, D), f32), pltpu.VMEM((ROWS, LANES), f32),
                pltpu.VMEM((ROWS, D), bf16), pltpu.VMEM((ROWS, D), f32), pltpu.VMEM((ROWS, D), f32),
                pltpu.VMEM((D, D), bf16),
            ],
        ),
        out_shape=[
            shape((ROWS, D), bf16), shape((ROWS, D), f32), shape((ROWS, D), bf16), shape((ROWS, D), bf16),
        ]
        + [shape((4, NF // 2, QUARTER, D), bf16)] * 4
        + [shape((8, D), f32), shape((NF, 1, FCHUNK), f32)],
        compiler_params=pltpu.CompilerParams(vmem_limit_bytes=60 * MIB),
        cost_estimate=pl.CostEstimate(flops=12 * ROWS * D * FF, bytes_accessed=30_000_000, transcendentals=ROWS * FF),
        name="feed_forward",
    )(at, attended, both, both, out_w, vecs, up_b, up_w, down_w)


def squares_kernel(
    at_ref, gq_ref, own_ref, other_ref, arrived_ref, arrived_own_ref, arrived_gq_ref, gb_ref, gb_other_ref,
    normed_ref, normed_other_ref, att_ref, att_other_ref, keep0_ref, away0_ref, keep1_ref, away1_ref,
    joined, joined_other, buffer,
):
    core = at_ref[0]

    def product(part, left, left_other, right, right_other):
        buffer[...] = (mm_tn(left[...], right[...]) + mm_tn(left_other[...], right_other[...])).astype(bf16)
        keep_ref, away_ref = ((keep0_ref, away0_ref), (keep1_ref, away1_ref))[part]
        for index, block in enumerate(quarter_blocks(at_ref[1 + part], core)):
            (keep_ref if index < 2 else away_ref)[index % 2, 0] = buffer[quarter_rows(block), :]

    joined[...] = own_ref[0] + arrived_ref[0]
    joined_other[...] = arrived_own_ref[0] + other_ref[0]

    @pl.when(core == 0)
    def _():
        product(0, normed_ref, normed_other_ref, gq_ref, arrived_gq_ref.at[0])
        product(1, normed_ref, normed_other_ref, joined, joined_other)

    @pl.when(core != 0)
    def _():
        product(0, normed_ref, normed_other_ref, joined, joined_other)
        product(1, att_ref, att_other_ref, gb_ref, gb_other_ref)


def squares(at, gq, own, sent, arrived, *pairs):
    rows = whole(ROWS, D)
    pick = pl.BlockSpec((1, ROWS, D), lambda s, at: (at[0], 0, 0))
    number = lambda n: pl.BlockSpec((1, ROWS, D), lambda s, at: (n, 0, 0))
    return pl.pallas_call(
        squares_kernel,
        grid_spec=pltpu.PrefetchScalarGridSpec(
            num_scalar_prefetch=1, grid=(1,),
            in_specs=[rows, pick, pick, pick, number(2), number(3)] + [rows] * 6,
            out_specs=[whole(2, 1, QUARTER, D)] * 4,
            scratch_shapes=[pltpu.VMEM((ROWS, D), bf16), pltpu.VMEM((ROWS, D), bf16), pltpu.VMEM((D, D), bf16)],
        ),
        out_shape=[jax.ShapeDtypeStruct((2, 1, QUARTER, D), bf16)] * 4,
        compiler_params=pltpu.CompilerParams(vmem_limit_bytes=44 * MIB),
        cost_estimate=pl.CostEstimate(flops=8 * ROWS * D * D, bytes_accessed=13_000_000, transcendentals=0),
        name="squares",
    )(at, gq, own, sent, arrived, arrived, arrived, *pairs)


def input_grad_kernel(
    gq_ref, own_ref, swapped_ref, w_ref, x_ref, gh_ref, gain_ref, vecg_ref, upbg_ref, out_ref, small_ref, right
):
    step = pl.program_id(0)
    right[:, :D] = gq_ref[...]
    right[:, D : 2 * D] = own_ref[0] + swapped_ref[0]
    right[:, 2 * D :] = own_ref[1] + swapped_ref[1]
    grad_normed = mm_nt(right[...], w_ref[...])
    source = x_ref[...].astype(f32)
    centred = source - jnp.mean(source, axis=1, keepdims=True)
    rstd = lax.rsqrt(jnp.mean(centred * centred, axis=1, keepdims=True) + epsilon)
    xhat = centred * rstd
    gx = grad_normed * gain_ref[0:1, :]
    mean1 = jnp.mean(gx, axis=1, keepdims=True)
    mean2 = jnp.mean(gx * xhat, axis=1, keepdims=True)
    out_ref[...] = (gh_ref[...] + rstd * (gx - mean1 - xhat * mean2)).astype(bf16)

    @pl.when(step == 0)
    def _():
        small_ref[...] = jnp.zeros_like(small_ref)
        small_ref[0:4, :] = vecg_ref[0:4, :]
        for f in range(NF):
            small_ref[8 + f : 9 + f, :] = upbg_ref[f]

    small_ref[4:5, :] += jnp.sum(grad_normed * xhat, axis=0, keepdims=True)
    small_ref[5:6, :] += jnp.sum(grad_normed, axis=0, keepdims=True)
    small_ref[6:7, :] += jnp.sum(right[:, :D].astype(f32), axis=0, keepdims=True)
    small_ref[7:8, :] += jnp.sum(right[:, 2 * D :].astype(f32), axis=0, keepdims=True)


def input_gradient(gq, own, swapped, qkv_w, both, grad_hidden, gain, vec_grads, up_b_grad):
    steps = 3
    length = ROWS // steps
    rows = pl.BlockSpec((length, D), lambda s: (s, 0))
    pair = pl.BlockSpec((2, length, D), lambda s: (0, s, 0))
    fixed = lambda *shape: pl.BlockSpec(shape, lambda s: (0,) * len(shape))
    return pl.pallas_call(
        input_grad_kernel,
        grid=(steps,),
        in_specs=[rows, pair, pair, fixed(D, 3 * D), rows, rows, fixed(8, D), fixed(8, D), fixed(NF, 1, FCHUNK)],
        out_specs=[rows, fixed(16, D)],
        out_shape=[jax.ShapeDtypeStruct((ROWS, D), bf16), jax.ShapeDtypeStruct((16, D), f32)],
        scratch_shapes=[pltpu.VMEM((length, 3 * D), bf16)],
        compiler_params=pltpu.CompilerParams(vmem_limit_bytes=60 * MIB),
        cost_estimate=pl.CostEstimate(flops=6 * ROWS * D * D, bytes_accessed=10_000_000, transcendentals=0),
        name="input_gradient",
    )(gq, own, swapped, qkv_w, both, grad_hidden, gain, vec_grads, up_b_grad)


def place_kernel(mine, late, at_ref, source0_ref, source1_ref, *refs):
    up_ref, down_ref, qkv_ref, out_ref, pieces, tiles, in_sems, out_sems = refs[-8:]
    half = at_ref[0] if mine else 1 - at_ref[0]
    sources = (source0_ref, source1_ref)
    plan = []
    for j in range(2):
        block = 2 * half + j
        columns = pl.ds(pl.multiple_of(block * D, D), D)
        for s in range(2):
            rows = [
                quarter_rows(quarter_blocks(at_ref[1 + part], half)[s + (2 if late else 0)]) for part in range(2)
            ]
            down_rows = pl.ds(pl.multiple_of(block * D + rows[1].start, QUARTER), QUARTER)
            plan.append((sources[0].at[s, j], up_ref.at[rows[0], columns], None))
            plan.append((sources[1].at[s, j], down_ref.at[down_rows, :], None))
            last = out_ref.at[rows[j], :] if j == 1 else None
            square_columns = columns if j == 0 else pl.ds(D, D)
            plan.append((sources[j].at[s, 2], qkv_ref.at[rows[j], square_columns], last))
    loads = []
    for number, (source, _, _) in enumerate(plan):
        loads.append(pltpu.make_async_copy(source, pieces.at[number], in_sems.at[number]))
        loads[-1].start()
    for number, (_, target, last) in enumerate(plan):
        loads[number].wait()
        tiles[number] = pieces[number].astype(f32)

        def start(to, number=number):
            pltpu.make_async_copy(tiles.at[number], to, out_sems.at[number]).start()

        if last is None:
            start(target)
        else:
            pl.when(half == 0)(lambda: start(target))
            pl.when(half != 0)(lambda: start(last))
    for number, (_, target, _) in enumerate(plan):
        pltpu.make_async_copy(tiles.at[number], target, out_sems.at[number]).wait()


def place(at, pieces, mine, late, before=()):
    shape = jax.ShapeDtypeStruct
    anywhere = pl.BlockSpec(memory_space=pl.ANY)
    return pl.pallas_call(
        functools.partial(place_kernel, mine, late),
        grid_spec=pltpu.PrefetchScalarGridSpec(
            num_scalar_prefetch=1, grid=(1,),
            in_specs=[anywhere] * (2 + len(before)),
            out_specs=[anywhere] * 4,
            scratch_shapes=[
                pltpu.VMEM((12, QUARTER, D), bf16), pltpu.VMEM((12, QUARTER, D), f32),
                pltpu.SemaphoreType.DMA((12,)), pltpu.SemaphoreType.DMA((12,)),
            ],
        ),
        out_shape=[shape((D, FF), f32), shape((FF, D), f32), shape((D, 3 * D), f32), shape((D, D), f32)],
        input_output_aliases={3 + index: index for index in range(len(before))},
        compiler_params=pltpu.CompilerParams(vmem_limit_bytes=16 * MIB),
        cost_estimate=pl.CostEstimate(flops=0, bytes_accessed=11_000_000, transcendentals=0),
        name="place_late" if late else "place_early",
    )(at, *pieces, *before)


def linear(y, xl, c, z, xh):
    return (((y * 2 + xl) * 2 + c) * 4 + z) * 2 + xh


def scene_pairs(slot):
    pairs = []
    for y, xl, c, z, xh in itertools.product(range(4), range(2), range(2), range(4), range(2)):
        target = z ^ slot ^ (0 if xh == c else 2)
        if target < 3:
            pairs.append((linear(y, xl, c, z, xh), linear(y, xl, xh, target, c)))
    return pairs


def to_scene(arrays, z, flip):
    pieces = []
    for slot in range(SLOTS):
        scene = jnp.minimum(z ^ slot ^ flip, 2)
        message = [lax.dynamic_index_in_dim(array, scene, 0, keepdims=False) for array in arrays]
        pieces.append(lax.ppermute(jnp.concatenate(message, axis=1), AXES, scene_pairs(slot)))
    return pieces


def turn(values):
    pairs = [
        (linear(y, xl, c, z, xh), linear(y, xl, xh, z, c))
        for y, xl, c, z, xh in itertools.product(range(4), range(2), range(2), range(4), range(2))
    ]
    return lax.ppermute(values, AXES, pairs)


def slot_block(values, offset, flip):
    return lax.dynamic_slice_in_dim(values, (offset ^ flip) * BLK, BLK, 0)


def for_home(stayed, first, second, both, z, core):
    pieces = jnp.stack([stayed, jnp.where(core == 0, first, second), both, jnp.where(core == 0, second, first)])
    return jnp.stack([lax.dynamic_index_in_dim(pieces, z ^ scene, 0, keepdims=False) for scene in range(3)])


SWAP = ((0, 1), (1, 0))
MASKS = ((1, 3), (3, 1))


def exchange(value, move):
    pairs = []
    for place in itertools.product(range(4), range(4), range(4), range(2)):
        ends = [linear(y, x % 2, c, z, x // 2) for x, y, z, c in (place, move(*place))]
        pairs.append(tuple(ends))
    return lax.ppermute(value, AXES, pairs)


def meet(value, axis, step):
    def move(x, y, z, c):
        at = {"x": x, "y": y, "z": z}
        at[axis] = at[axis] ^ MASKS[c][step]
        return at["x"], at["y"], at["z"], c

    return exchange(value, move)


def swap(value):
    return lax.ppermute(value, "c", SWAP)


ORDERS = ("yxz", "zyx")


def meet_parts(values, stage, step):
    return [meet(value, ORDERS[part][stage], step) for part, value in enumerate(values)]


def add(*terms):
    return functools.reduce(jnp.add, [term.astype(f32) for term in terms]).astype(bf16)


def block_of(blocks, index):
    return lax.dynamic_index_in_dim(blocks, index, 1, keepdims=False)


def put_block(blocks, value, index):
    return lax.dynamic_update_index_in_dim(blocks, value, index, 1)


SMALL = 16


def meet_with(value, small, axis, step):
    high = lax.reduce_precision(small, 8, 7)
    low = lax.reduce_precision(small - high, 8, 7)
    rows = value.reshape(-1, D)
    message = jnp.concatenate([rows, high.astype(bf16), low.astype(bf16)], axis=0)
    arrived = meet(message, axis, step)
    count = rows.shape[0]
    other = arrived[count : count + SMALL].astype(f32) + arrived[count + SMALL :].astype(f32)
    return arrived[:count].reshape(value.shape), (high + low) + other


def hold(*values):
    return lax.optimization_barrier(values)


def body(
    tokens, view_counts, ln1_gain, ln1_shift, qkv_weight, query_bias, value_bias, out_weight, out_bias,
    ln2_gain, ln2_shift, up_weight, up_bias, down_weight, down_bias, cotangent,
):
    core, z, xh = lax.axis_index("c"), lax.axis_index("z"), lax.axis_index("xh")

    flip = jnp.where(xh == core, 0, 2)
    views = jnp.broadcast_to(view_counts.astype(bf16)[:, None, None], (3, BLK, LANES))
    pieces = to_scene((tokens, cotangent, views), z, flip)
    vecs = jnp.concatenate([jnp.stack([out_bias, ln2_gain, ln2_shift, down_bias]), jnp.zeros((4, D), f32)])
    gains = jnp.broadcast_to(ln1_gain[None, :], (8, D))
    weight_q, weight_kv = qkv_weight[:, :D], qkv_weight[:, D:]
    pieces, vecs, gains, weight_q, weight_kv = hold(pieces, vecs, gains, weight_q, weight_kv)
    both = jnp.concatenate([piece[:, : 2 * D] for piece in pieces], axis=0)
    views = pieces[0][0, 2 * D].astype(f32)
    x = both[:, :D]

    row = jnp.arange(ROWS, dtype=jnp.int32)
    slot = row // BLK
    position = jnp.concatenate([
        (2 * (z ^ slot ^ flip) + core) * BLK + row % BLK,
        (2 * (z ^ slot ^ (2 - flip)) + 1 - core) * BLK + row % BLK,
    ])
    usable = (position.astype(f32) < views * VIEW_TOK) | (position >= VIEWS_MAX * VIEW_TOK)
    mask = jnp.broadcast_to(jnp.where(usable, 0.0, masked_score).astype(bf16)[:, None], (KEYS, LANES))

    source = x.astype(f32)
    centred = source - jnp.mean(source, axis=1, keepdims=True)
    rstd = lax.rsqrt(jnp.mean(centred * centred, axis=1, keepdims=True) + epsilon)
    normed = (centred * rstd * ln1_gain + ln1_shift).astype(bf16)
    product = lambda weight: jnp.dot(normed, weight, preferred_element_type=f32)
    kv_bias = jnp.concatenate([jnp.zeros((D,), f32), value_bias])
    own = (product(weight_kv) + kv_bias).astype(bf16)
    sibling = swap(own)
    normed_other = swap(normed)
    queries = (product(weight_q) + query_bias).astype(bf16)
    weights, heads_out, linv, attended = attention_forward(queries, own, sibling, mask)

    up_b = up_bias.reshape(NF, 1, FCHUNK)
    y = lax.axis_index("y")
    x_place = lax.axis_index("xh") * 2 + lax.axis_index("xl")
    at = jnp.stack([core, y, z]).astype(jnp.int32)
    output, grad_hidden, grad_branch, grad_att, up_other, up_mine, down_other, down_mine, vec_grads, up_b_grad = (
        feed_forward(at, attended, both, out_weight, vecs, up_b, up_weight, down_weight)
    )

    moving = [swap(up_other), swap(down_other)]
    attended_other, branch_other = swap(attended), swap(grad_branch)
    grad_q, grad_own, sent = attention_backward(at, queries, own, sibling, weights, heads_out, linv, grad_att)

    moving, attended_other, branch_other, sent = hold(moving, attended_other, branch_other, sent)
    arrived = swap(sent)
    pieces = [(up_mine, moving[0]), (down_mine, moving[1])]
    away = [add(mine[2:], other[2:]) for mine, other in pieces]
    halved = meet_parts(away, 0, 0)
    arrived, away = hold(arrived, away)
    keep0, away0, keep1, away1 = squares(
        at, grad_q, grad_own, sent, arrived, grad_branch, branch_other, normed, normed_other, attended, attended_other
    )

    away, grad_hidden = hold([away0, away1], grad_hidden)
    square_halved = meet_parts(away, 0, 0)
    halved, grad_hidden = hold(halved, grad_hidden)
    away = [add(mine[1], other[1], half[1]) for (mine, other), half in zip(pieces, halved)]
    away, grad_hidden = hold(away, grad_hidden)
    quartered = meet_parts(away, 0, 1)
    input_grad, small = input_gradient(
        grad_q, grad_own, arrived, qkv_weight, both, grad_hidden, gains, vec_grads, up_b_grad
    )

    square_halved, small, input_grad = hold(square_halved, small, input_grad)
    square_away = [add(keep[1], half[1]) for keep, half in zip((keep0, keep1), square_halved)]
    square_away, quartered = hold(square_away, quartered)
    square_quartered = meet_parts(square_away, 0, 1)

    def ring_sum(pieces, halved, quartered):
        return [
            add(mine[0], other[0], half[0], quarter)
            for (mine, other), half, quarter in zip(pieces, halved, quartered)
        ]

    ff_own = ring_sum(pieces, halved, quartered)
    square_quartered, ff_own, small = hold(square_quartered, ff_own, small)
    owns = [add(k[0], h[0], q) for k, h, q in zip((keep0, keep1), square_halved, square_quartered)]
    blocks = [
        jnp.concatenate([f, o], axis=0).reshape(NF // 2 + 1, 4, QUARTER // 4, D) for f, o in zip(ff_own, owns)
    ]
    places = [x_place, y]
    first = 1 + 2 * core
    keep = [(block_of(b, p), block_of(b, p ^ (4 - first))) for b, p in zip(blocks, places)]
    away = [jnp.stack([block_of(b, p ^ first), block_of(b, p ^ 2)]) for b, p in zip(blocks, places)]
    second = 4 - first
    back = jnp.concatenate([output, input_grad], axis=1)
    over = jnp.concatenate([slot_block(back, first, flip), slot_block(back, 2, flip)], axis=0)
    keep, away, small, over, back = hold(keep, away, small, over, back)
    over = meet(over, "z", 0)
    one_way = meet(away[0], "x", 0)
    other_way, small = meet_with(away[1], small, "y", 0)

    one_way, other_way, small = hold(one_way, other_way, small)
    halved = [one_way, other_way]
    away, small = hold([add(k[1], h[1]) for k, h in zip(keep, halved)], small)
    one_way = meet(away[0], "x", 1)
    other_way, small = meet_with(away[1], small, "y", 1)

    one_way, other_way, small = hold(one_way, other_way, small)
    quartered = [one_way, other_way]
    ends = [add(k[0], h[0], q) for k, h, q in zip(keep, halved, quartered)]
    for step in range(2):
        ends, small = hold(ends, small)
        one_way, small = meet_with(ends[0], small, "z", step)
        other_way = meet(ends[1], "x", step)
        one_way, other_way, small = hold(one_way, other_way, small)
        ends = [ends[0] + one_way, ends[1] + other_way]

    over_first = over[:BLK]
    over = jnp.concatenate([slot_block(back, second, flip), over[BLK:]], axis=0)
    ends, small, over, over_first = hold(ends, small, over, over_first)
    over = meet(over, "z", 1)
    one_way, small = meet_with(ends[0], small, "x", 1)
    other_way = meet(ends[1], "y", 1)

    one_way, other_way, small = hold(one_way, other_way, small)
    pairs = [jnp.stack([ends[0], one_way]), jnp.stack([ends[1], other_way])]
    pairs, small = hold(pairs, small)
    one_way, small = meet_with(pairs[0], small, "x", 0)
    other_way = meet(pairs[1], "y", 0)

    one_way, other_way, small = hold(one_way, other_way, small)
    owns = []
    for pair, more, p, empty in zip(pairs, (one_way, other_way), places, blocks):
        full = jnp.zeros_like(empty)
        for value, index in ((pair[0], p), (pair[1], p ^ (4 - first)), (more[0], p ^ first), (more[1], p ^ 2)):
            full = put_block(full, value, index)
        owns.append(full.reshape(NF // 2 + 1, QUARTER, D))
    returned = for_home(slot_block(back, 0, flip), over_first, over[:BLK], over[BLK:], z, core)
    owns, small, returned = hold(owns, small, returned)
    arrived = meet_parts(owns, 0, 1)
    returned = turn(returned)

    arrived, small, returned = hold(arrived, small, returned)
    pairs = [jnp.stack([o, a]) for o, a in zip(owns, arrived)]
    pairs, small = hold(pairs, small)
    got = meet_parts(pairs, 0, 0)
    own_other = [swap(v) for v in pairs]
    small_other = swap(small)
    placed = place(at, pairs, True, False)
    output, input_grad = returned[:, :, :D], returned[:, :, D:]

    own_other, small_other, placed, output, input_grad = hold(own_other, small_other, placed, output, input_grad)
    small = small + small_other
    placed = place(at, own_other, False, False, placed)
    got, placed = hold(got, placed)
    got_other = [swap(v) for v in got]
    placed = place(at, got, True, True, placed)
    d_up, d_down, d_qkv, d_out = place(at, got_other, False, True, placed)
    return (
        output, input_grad, small[4], small[5], d_qkv, small[6], small[7], d_out,
        small[0], small[1], small[2], d_up, small[8:12].reshape(FF), d_down, small[3],
    )


def solution(mesh):
    fine = Mesh(mesh.devices.reshape(4, 2, 2, 4, 2), AXES)
    rows = P(("y", "xl", "c"), ("z", "xh"), None)
    placed = (rows, P(("y", "xl", "c"))) + (P(),) * 13 + (rows,)
    return jax.shard_map(
        body, mesh=fine, in_specs=placed, out_specs=(rows, rows) + (P(),) * 13, check_vma=False
    )
```

```python
import functools
import itertools
import math

import jax
import jax.numpy as jnp
from jax import lax
from jax.experimental import pallas as pl
from jax.experimental.pallas import tpu as pltpu
from jax.sharding import Mesh
from jax.sharding import PartitionSpec as P

HEADS = 12
HEAD_DIM = 64
VIEW_TOK = 128
VIEWS_MAX = 8
D = 768
FF = 3072
BLK = 144
SLOTS = 4
ROWS = BLK * SLOTS
KEYS = 2 * ROWS
PAIRS = HEADS // 2
LANES = 128
FCHUNK = 768
QROWS = 288
QUARTER = D // 4
NF = FF // FCHUNK

bf16 = jnp.bfloat16
f32 = jnp.float32
epsilon = 1e-05
masked_score = -1e30
GELU_C = math.sqrt(2.0 / math.pi)
GELU_A = 0.044715

AXES = ("y", "xl", "c", "z", "xh")
MIB = 1024 * 1024


def mm(a, b):
    return lax.dot_general(a, b, (((1,), (0,)), ((), ())), preferred_element_type=f32)


def mm_nt(a, b):
    return lax.dot_general(a, b, (((1,), (1,)), ((), ())), preferred_element_type=f32)


def mm_tn(a, b):
    return lax.dot_general(a, b, (((0,), (0,)), ((), ())), preferred_element_type=f32)


def lane_row(at, first, last):
    lane = lax.broadcasted_iota(jnp.int32, (1, LANES), 1)
    return jnp.where((lane >= first) & (lane < last), 1.0, 0.0).astype(at)


def key_mask(at_ref):
    core, z, flip, views = (at_ref[index] for index in (0, 3, 4, 5))
    row = lax.broadcasted_iota(jnp.int32, (BLK, LANES), 0)
    blocks = []
    for part in range(2):
        for slot in range(SLOTS):
            turned = flip if part == 0 else 2 - flip
            first = (2 * (z ^ slot ^ turned) + (core if part == 0 else 1 - core)) * BLK
            usable = (row < views * VIEW_TOK - first) | (row >= VIEWS_MAX * VIEW_TOK - first)
            blocks.append(jnp.where(usable, 0.0, masked_score).astype(bf16))
    return jnp.concatenate(blocks, axis=0)


def attention_forward_kernel(at_ref, q_ref, ko_ref, vo_ref, ks_ref, vs_ref, p_ref, o_ref, linv_ref, att_ref):
    half = [lane_row(bf16, 0, 64), lane_row(bf16, 64, 128)]
    unit = [lane_row(bf16, 64, 65), lane_row(bf16, 0, 1)]
    q = q_ref[...]
    k = jnp.concatenate([ko_ref[...], ks_ref[...]], axis=0)
    v = jnp.concatenate([vo_ref[...], vs_ref[...]], axis=0)
    mask = key_mask(at_ref)
    lane = lax.broadcasted_iota(jnp.int32, (QROWS, LANES), 1)
    q_now = [q * half[h] + unit[h] for h in range(2)]
    k_now = [k * half[h] + mask * unit[h] for h in range(2)]
    v_now = [v * half[h] + unit[h] for h in range(2)]
    items = [(slice(s * QROWS, (s + 1) * QROWS), h) for s in range(ROWS // QROWS) for h in range(2)]
    done = {}

    def product(number, weights):
        rows, h = items[number]
        out = mm(weights, v_now[h])
        inv = 1.0 / (out[:, 64:65] if h == 0 else out[:, 0:1])
        done[h] = (out * inv, jnp.broadcast_to(inv, (QROWS, LANES)))
        if h == 1:
            out = jnp.where(lane < 64, done[0][0], done[1][0])
            o_ref[rows, :] = out
            att_ref[rows, :] = out.astype(bf16)
            linv_ref[rows, :] = jnp.where(lane < 64, done[0][1], done[1][1])

    scores = mm_nt(q_now[0][items[0][0]], k_now[0])
    before = None
    for number, (rows, h) in enumerate(items):
        following = None
        if number + 1 < len(items):
            next_rows, next_h = items[number + 1]
            following = mm_nt(q_now[next_h][next_rows], k_now[next_h])
        top = jnp.max(scores, axis=1, keepdims=True)
        weights = jnp.exp((scores - top) * 0.125).astype(bf16)
        p_ref[h, rows, :] = weights
        if before is not None:
            product(number - 1, before)
        before, scores = weights, following
    product(len(items) - 1, before)


def head_columns(base):
    return pl.BlockSpec((ROWS, LANES), lambda i, f=base: (0, f + i))


def attention_forward(at, queries, own, sibling):
    col = lambda base: pl.BlockSpec((ROWS, LANES), lambda i, at: (0, base + i))
    return pl.pallas_call(
        attention_forward_kernel,
        grid_spec=pltpu.PrefetchScalarGridSpec(
            num_scalar_prefetch=1, grid=(PAIRS,),
            in_specs=[col(0), col(0), col(PAIRS), col(0), col(PAIRS)],
            out_specs=[pl.BlockSpec((2, ROWS, KEYS), lambda i, at: (i, 0, 0)), col(0), col(0), col(0)],
        ),
        out_shape=[
            jax.ShapeDtypeStruct((HEADS, ROWS, KEYS), bf16),
            jax.ShapeDtypeStruct((ROWS, D), f32),
            jax.ShapeDtypeStruct((ROWS, D), f32),
            jax.ShapeDtypeStruct((ROWS, D), bf16),
        ],
        compiler_params=pltpu.CompilerParams(vmem_limit_bytes=60 * MIB),
        cost_estimate=pl.CostEstimate(flops=16 * ROWS * KEYS * D, bytes_accessed=20_000_000, transcendentals=HEADS * ROWS * KEYS),
        name="attention_forward",
    )(at, queries, own, own, sibling, sibling)


def attention_backward_kernel(
    at_ref, q_ref, ko_ref, vo_ref, ks_ref, vs_ref, p_ref, o_ref, linv_ref, g_ref, gq_ref, gown_ref, sent_ref
):
    half = [lane_row(bf16, 0, 64), lane_row(bf16, 64, 128)]
    two = [lane_row(bf16, 64, 66), lane_row(bf16, 0, 2)]
    lane = lax.broadcasted_iota(jnp.int32, (ROWS, LANES), 1)
    k = jnp.concatenate([ko_ref[...], ks_ref[...]], axis=0)
    v = jnp.concatenate([vo_ref[...], vs_ref[...]], axis=0)
    gs = g_ref[...].astype(f32) * linv_ref[...]
    prod = gs * o_ref[...]
    g_now, v_now = [], []
    for h in range(2):
        mine = (lane < 64) if h == 0 else (lane >= 64)
        base = 64 if h == 0 else 0
        delta = jnp.sum(jnp.where(mine, prod, 0.0), axis=1, keepdims=True)
        high = delta.astype(bf16).astype(f32)
        columns = jnp.where(lane == base, -high, jnp.where(lane == base + 1, high - delta, 0.0))
        g_now.append(jnp.where(mine, gs, columns).astype(bf16))
        v_now.append(v * half[h] + two[h])
    g_turned, q_turned = gs.astype(bf16).T, q_ref[...].T
    head = lambda turned, h: turned[64 * h : 64 * h + 64]
    grad_score = lambda h, diff: (p_ref[h].astype(f32) * diff).astype(bf16)
    diff = mm_nt(g_now[0], v_now[0])
    gv0 = mm(head(g_turned, 0), p_ref[0])
    gs0 = grad_score(0, diff)
    diff = mm_nt(g_now[1], v_now[1])
    gv1 = mm(head(g_turned, 1), p_ref[1])
    gs1 = grad_score(1, diff)
    gk0, gq0 = mm(head(q_turned, 0), gs0), mm(gs0, k)
    gk1, gq1 = mm(head(q_turned, 1), gs1), mm(gs1, k)
    gq = (jnp.where(lane < 64, gq0, gq1) * 0.125).astype(bf16)
    gk = (jnp.concatenate([gk0, gk1], axis=0) * 0.125).T.astype(bf16)
    gv = jnp.concatenate([gv0, gv1], axis=0).T.astype(bf16)
    gq_ref[...] = gq
    gown_ref[0], gown_ref[1] = gk[:ROWS], gv[:ROWS]
    sent_ref[0], sent_ref[1] = gk[ROWS:], gv[ROWS:]
    sent_ref[2] = jnp.where(at_ref[0] == 0, gv[:ROWS], gk[:ROWS])
    sent_ref[3] = gq


def attention_backward(at, queries, own, sibling, weights, heads_out, linv, grad_att):
    col = lambda base: pl.BlockSpec((ROWS, LANES), lambda i, at: (0, base + i))
    several = lambda count: pl.BlockSpec((count, ROWS, LANES), lambda i, at: (0, 0, i))
    return pl.pallas_call(
        attention_backward_kernel,
        grid_spec=pltpu.PrefetchScalarGridSpec(
            num_scalar_prefetch=1, grid=(PAIRS,),
            in_specs=[
                col(0), col(0), col(PAIRS), col(0), col(PAIRS),
                pl.BlockSpec((2, ROWS, KEYS), lambda i, at: (i, 0, 0)),
                col(0), col(0), col(0),
            ],
            out_specs=[col(0), several(2), several(4)],
        ),
        out_shape=[jax.ShapeDtypeStruct(shape, bf16) for shape in ((ROWS, D), (2, ROWS, D), (4, ROWS, D))],
        compiler_params=pltpu.CompilerParams(vmem_limit_bytes=60 * MIB),
        cost_estimate=pl.CostEstimate(flops=32 * ROWS * KEYS * D, bytes_accessed=25_000_000, transcendentals=0),
        name="attention_backward",
    )(at, queries, own, own, sibling, sibling, weights, heads_out, linv, grad_att)


def quarter_blocks(place, core):
    first = 1 + 2 * core
    return place, place ^ (4 - first), place ^ first, place ^ 2


def quarter_rows(block):
    return pl.ds(pl.multiple_of(block * QUARTER, QUARTER), QUARTER)


def put_quarters(ref, buffer, place, core):
    for index, block in enumerate(quarter_blocks(place, core)):
        ref[index, 0] = buffer[quarter_rows(block), :]


def feed_forward_kernel(
    at_ref, att_ref, x_ref, g_ref, ow_ref, vec_ref, upb_ref, up_ref, down_ref,
    out_ref, gh_ref, gb_ref, gatt_ref, up_other_ref, up_mine_ref, down_other_ref, down_mine_ref, vecg_ref, upbg_ref,
    hidden, xhat, rstd_s, normed2, y_acc, gn_acc, buffer,
):
    step = pl.program_id(0)
    out_bias, gain, shift, down_bias = (vec_ref[r : r + 1, :] for r in range(4))

    @pl.when(step == 0)
    def _():
        h = x_ref[...].astype(f32) + mm(att_ref[...], ow_ref[...]) + out_bias
        hidden[...] = h
        centred = h - jnp.mean(h, axis=1, keepdims=True)
        rstd = lax.rsqrt(jnp.mean(centred * centred, axis=1, keepdims=True) + epsilon)
        xh = centred * rstd
        xhat[...] = xh
        rstd_s[...] = jnp.broadcast_to(rstd, (ROWS, LANES))
        normed2[...] = (xh * gain + shift).astype(bf16)
        y_acc[...] = jnp.zeros_like(y_acc)
        gn_acc[...] = jnp.zeros_like(gn_acc)

    g = g_ref[...]
    n2 = normed2[...]
    u = mm(n2, up_ref[...]) + upb_ref[0]
    ga = mm_nt(g, down_ref[...])
    u2 = u * u
    t = jnp.tanh(u * (GELU_C + (GELU_C * GELU_A) * u2))
    hp = 0.5 + 0.5 * t
    active = (u * hp).astype(bf16)
    slope = hp + (0.5 * u) * (1.0 - t * t) * (GELU_C + (3.0 * GELU_C * GELU_A) * u2)
    gu = (ga * slope).astype(bf16)
    y_acc[...] += mm(active, down_ref[...])
    gn_acc[...] += mm_nt(gu, up_ref[...])
    upbg_ref[0] = jnp.sum(gu.astype(f32), axis=0, keepdims=True)
    for part, value, other_ref, mine_ref in (
        (0, mm_tn(n2, gu), up_other_ref, up_mine_ref), (1, mm_tn(active, g), down_other_ref, down_mine_ref),
    ):
        buffer[...] = value.astype(bf16)

        @pl.when(step < NF // 2)
        def _():
            put_quarters(other_ref, buffer, at_ref[1 + part], 1 - at_ref[0])

        @pl.when(step >= NF // 2)
        def _():
            put_quarters(mine_ref, buffer, at_ref[1 + part], at_ref[0])

    @pl.when(step == NF - 1)
    def _():
        out_ref[...] = (hidden[...] + y_acc[...] + down_bias).astype(bf16)
        gn = gn_acc[...]
        xh = xhat[...]
        gf = g_ref[...].astype(f32)
        vecg_ref[...] = jnp.zeros_like(vecg_ref)
        vecg_ref[1:2, :] = jnp.sum(gn * xh, axis=0, keepdims=True)
        vecg_ref[2:3, :] = jnp.sum(gn, axis=0, keepdims=True)
        vecg_ref[3:4, :] = jnp.sum(gf, axis=0, keepdims=True)
        gx = gn * gain
        mean1 = jnp.mean(gx, axis=1, keepdims=True)
        mean2 = jnp.mean(gx * xh, axis=1, keepdims=True)
        gh = gf + rstd_s[:, 0:1] * (gx - mean1 - xh * mean2)
        gh_ref[...] = gh
        vecg_ref[0:1, :] = jnp.sum(gh, axis=0, keepdims=True)
        gb = gh.astype(bf16)
        gb_ref[...] = gb
        gatt_ref[...] = mm_nt(gb, ow_ref[...]).astype(bf16)


def whole(*shape):
    return pl.BlockSpec(shape, lambda s, at: (0,) * len(shape))


TOKEN_SPEC = pl.BlockSpec((ROWS, D), lambda s, at: (0, 0))
COTANGENT_SPEC = pl.BlockSpec((ROWS, D), lambda s, at: (0, 1))


def feed_forward(at, attended, both, out_w, vecs, up_b, up_w, down_w):
    shape = jax.ShapeDtypeStruct
    chunk = lambda s, at: (2 * (1 - at[0]) + s) % NF
    other = pl.BlockSpec((4, 1, QUARTER, D), lambda s, at: (0, jnp.minimum(s, NF // 2 - 1), 0, 0))
    mine = pl.BlockSpec((4, 1, QUARTER, D), lambda s, at: (0, jnp.maximum(s - NF // 2, 0), 0, 0))
    return pl.pallas_call(
        feed_forward_kernel,
        grid_spec=pltpu.PrefetchScalarGridSpec(
            num_scalar_prefetch=1,
            grid=(NF,),
            in_specs=[
                whole(ROWS, D), TOKEN_SPEC, COTANGENT_SPEC, whole(D, D), whole(8, D),
                pl.BlockSpec((1, 1, FCHUNK), lambda s, at: (chunk(s, at), 0, 0)),
                pl.BlockSpec((D, FCHUNK), lambda s, at: (0, chunk(s, at))),
                pl.BlockSpec((FCHUNK, D), lambda s, at: (chunk(s, at), 0)),
            ],
            out_specs=[whole(ROWS, D)] * 4
            + [other, mine, other, mine, whole(8, D), pl.BlockSpec((1, 1, FCHUNK), lambda s, at: (chunk(s, at), 0, 0))],
            scratch_shapes=[
                pltpu.VMEM((ROWS, D), f32), pltpu.VMEM((ROWS, D), f32), pltpu.VMEM((ROWS, LANES), f32),
                pltpu.VMEM((ROWS, D), bf16), pltpu.VMEM((ROWS, D), f32), pltpu.VMEM((ROWS, D), f32),
                pltpu.VMEM((D, D), bf16),
            ],
        ),
        out_shape=[
            shape((ROWS, D), bf16), shape((ROWS, D), f32), shape((ROWS, D), bf16), shape((ROWS, D), bf16),
        ]
        + [shape((4, NF // 2, QUARTER, D), bf16)] * 4
        + [shape((8, D), f32), shape((NF, 1, FCHUNK), f32)],
        compiler_params=pltpu.CompilerParams(vmem_limit_bytes=60 * MIB),
        cost_estimate=pl.CostEstimate(flops=12 * ROWS * D * FF, bytes_accessed=30_000_000, transcendentals=ROWS * FF),
        name="feed_forward",
    )(at, attended, both, both, out_w, vecs, up_b, up_w, down_w)


def squares_kernel(
    at_ref, gq_ref, own_ref, other_ref, arrived_ref, arrived_own_ref, arrived_gq_ref, gb_ref, gb_other_ref,
    normed_ref, normed_other_ref, att_ref, att_other_ref, keep0_ref, away0_ref, keep1_ref, away1_ref,
    joined, joined_other, buffer,
):
    core = at_ref[0]

    def product(part, left, left_other, right, right_other):
        buffer[...] = (mm_tn(left[...], right[...]) + mm_tn(left_other[...], right_other[...])).astype(bf16)
        keep_ref, away_ref = ((keep0_ref, away0_ref), (keep1_ref, away1_ref))[part]
        for index, block in enumerate(quarter_blocks(at_ref[1 + part], core)):
            (keep_ref if index < 2 else away_ref)[index % 2, 0] = buffer[quarter_rows(block), :]

    joined[...] = own_ref[0] + arrived_ref[0]
    joined_other[...] = arrived_own_ref[0] + other_ref[0]

    @pl.when(core == 0)
    def _():
        product(0, normed_ref, normed_other_ref, gq_ref, arrived_gq_ref.at[0])
        product(1, normed_ref, normed_other_ref, joined, joined_other)

    @pl.when(core != 0)
    def _():
        product(0, normed_ref, normed_other_ref, joined, joined_other)
        product(1, att_ref, att_other_ref, gb_ref, gb_other_ref)


def squares(at, gq, own, sent, arrived, *pairs):
    rows = whole(ROWS, D)
    pick = pl.BlockSpec((1, ROWS, D), lambda s, at: (at[0], 0, 0))
    number = lambda n: pl.BlockSpec((1, ROWS, D), lambda s, at: (n, 0, 0))
    return pl.pallas_call(
        squares_kernel,
        grid_spec=pltpu.PrefetchScalarGridSpec(
            num_scalar_prefetch=1, grid=(1,),
            in_specs=[rows, pick, pick, pick, number(2), number(3)] + [rows] * 6,
            out_specs=[whole(2, 1, QUARTER, D)] * 4,
            scratch_shapes=[pltpu.VMEM((ROWS, D), bf16), pltpu.VMEM((ROWS, D), bf16), pltpu.VMEM((D, D), bf16)],
        ),
        out_shape=[jax.ShapeDtypeStruct((2, 1, QUARTER, D), bf16)] * 4,
        compiler_params=pltpu.CompilerParams(vmem_limit_bytes=44 * MIB),
        cost_estimate=pl.CostEstimate(flops=8 * ROWS * D * D, bytes_accessed=13_000_000, transcendentals=0),
        name="squares",
    )(at, gq, own, sent, arrived, arrived, arrived, *pairs)


def input_grad_kernel(
    gq_ref, own_ref, swapped_ref, w_ref, x_ref, gh_ref, gain_ref, vecg_ref, upbg_ref, out_ref, small_ref, right
):
    step = pl.program_id(0)
    right[:, :D] = gq_ref[...]
    right[:, D : 2 * D] = own_ref[0] + swapped_ref[0]
    right[:, 2 * D :] = own_ref[1] + swapped_ref[1]
    grad_normed = mm_nt(right[...], w_ref[...])
    source = x_ref[...].astype(f32)
    centred = source - jnp.mean(source, axis=1, keepdims=True)
    rstd = lax.rsqrt(jnp.mean(centred * centred, axis=1, keepdims=True) + epsilon)
    xhat = centred * rstd
    gx = grad_normed * gain_ref[0:1, :]
    mean1 = jnp.mean(gx, axis=1, keepdims=True)
    mean2 = jnp.mean(gx * xhat, axis=1, keepdims=True)
    out_ref[...] = (gh_ref[...] + rstd * (gx - mean1 - xhat * mean2)).astype(bf16)

    @pl.when(step == 0)
    def _():
        small_ref[...] = jnp.zeros_like(small_ref)
        small_ref[0:4, :] = vecg_ref[0:4, :]
        for f in range(NF):
            small_ref[8 + f : 9 + f, :] = upbg_ref[f]

    small_ref[4:5, :] += jnp.sum(grad_normed * xhat, axis=0, keepdims=True)
    small_ref[5:6, :] += jnp.sum(grad_normed, axis=0, keepdims=True)
    small_ref[6:7, :] += jnp.sum(right[:, :D].astype(f32), axis=0, keepdims=True)
    small_ref[7:8, :] += jnp.sum(right[:, 2 * D :].astype(f32), axis=0, keepdims=True)


def input_gradient(gq, own, swapped, qkv_w, both, grad_hidden, gain, vec_grads, up_b_grad):
    steps = 3
    length = ROWS // steps
    rows = pl.BlockSpec((length, D), lambda s: (s, 0))
    pair = pl.BlockSpec((2, length, D), lambda s: (0, s, 0))
    fixed = lambda *shape: pl.BlockSpec(shape, lambda s: (0,) * len(shape))
    return pl.pallas_call(
        input_grad_kernel,
        grid=(steps,),
        in_specs=[rows, pair, pair, fixed(D, 3 * D), rows, rows, fixed(1, D), fixed(8, D), fixed(NF, 1, FCHUNK)],
        out_specs=[rows, fixed(16, D)],
        out_shape=[jax.ShapeDtypeStruct((ROWS, D), bf16), jax.ShapeDtypeStruct((16, D), f32)],
        scratch_shapes=[pltpu.VMEM((length, 3 * D), bf16)],
        compiler_params=pltpu.CompilerParams(vmem_limit_bytes=60 * MIB),
        cost_estimate=pl.CostEstimate(flops=6 * ROWS * D * D, bytes_accessed=10_000_000, transcendentals=0),
        name="input_gradient",
    )(gq, own, swapped, qkv_w, both, grad_hidden, gain, vec_grads, up_b_grad)


def place_kernel(mine, late, at_ref, source0_ref, source1_ref, *refs):
    up_ref, down_ref, qkv_ref, out_ref, pieces, tiles, in_sems, out_sems = refs[-8:]
    half = at_ref[0] if mine else 1 - at_ref[0]
    sources = (source0_ref, source1_ref)
    plan = []
    for j in range(2):
        block = 2 * half + j
        columns = pl.ds(pl.multiple_of(block * D, D), D)
        for s in range(2):
            rows = [
                quarter_rows(quarter_blocks(at_ref[1 + part], half)[s + (2 if late else 0)]) for part in range(2)
            ]
            down_rows = pl.ds(pl.multiple_of(block * D + rows[1].start, QUARTER), QUARTER)
            plan.append((sources[0].at[s, j], up_ref.at[rows[0], columns], None))
            plan.append((sources[1].at[s, j], down_ref.at[down_rows, :], None))
            last = out_ref.at[rows[j], :] if j == 1 else None
            square_columns = columns if j == 0 else pl.ds(D, D)
            plan.append((sources[j].at[s, 2], qkv_ref.at[rows[j], square_columns], last))
    loads = []
    for number, (source, _, _) in enumerate(plan):
        loads.append(pltpu.make_async_copy(source, pieces.at[number], in_sems.at[number]))
        loads[-1].start()
    for number, (_, target, last) in enumerate(plan):
        loads[number].wait()
        tiles[number] = pieces[number].astype(f32)

        def start(to, number=number):
            pltpu.make_async_copy(tiles.at[number], to, out_sems.at[number]).start()

        if last is None:
            start(target)
        else:
            pl.when(half == 0)(lambda: start(target))
            pl.when(half != 0)(lambda: start(last))
    for number, (_, target, _) in enumerate(plan):
        pltpu.make_async_copy(tiles.at[number], target, out_sems.at[number]).wait()


def place(at, pieces, mine, late, before=()):
    shape = jax.ShapeDtypeStruct
    anywhere = pl.BlockSpec(memory_space=pl.ANY)
    return pl.pallas_call(
        functools.partial(place_kernel, mine, late),
        grid_spec=pltpu.PrefetchScalarGridSpec(
            num_scalar_prefetch=1, grid=(1,),
            in_specs=[anywhere] * (2 + len(before)),
            out_specs=[anywhere] * 4,
            scratch_shapes=[
                pltpu.VMEM((12, QUARTER, D), bf16), pltpu.VMEM((12, QUARTER, D), f32),
                pltpu.SemaphoreType.DMA((12,)), pltpu.SemaphoreType.DMA((12,)),
            ],
        ),
        out_shape=[shape((D, FF), f32), shape((FF, D), f32), shape((D, 3 * D), f32), shape((D, D), f32)],
        input_output_aliases={3 + index: index for index in range(len(before))},
        compiler_params=pltpu.CompilerParams(vmem_limit_bytes=16 * MIB),
        cost_estimate=pl.CostEstimate(flops=0, bytes_accessed=11_000_000, transcendentals=0),
        name="place_late" if late else "place_early",
    )(at, *pieces, *before)


def linear(y, xl, c, z, xh):
    return (((y * 2 + xl) * 2 + c) * 4 + z) * 2 + xh


def scene_pairs(slot):
    pairs = []
    for y, xl, c, z, xh in itertools.product(range(4), range(2), range(2), range(4), range(2)):
        target = z ^ slot ^ (0 if xh == c else 2)
        if target < 3:
            pairs.append((linear(y, xl, c, z, xh), linear(y, xl, xh, target, c)))
    return pairs


def to_scene(arrays, z, flip):
    pieces = []
    for slot in range(SLOTS):
        scene = jnp.minimum(z ^ slot ^ flip, 2)
        message = [lax.dynamic_index_in_dim(array, scene, 0, keepdims=False) for array in arrays]
        pieces.append(lax.ppermute(jnp.concatenate(message, axis=1), AXES, scene_pairs(slot)))
    return pieces


def turn(values):
    pairs = [
        (linear(y, xl, c, z, xh), linear(y, xl, xh, z, c))
        for y, xl, c, z, xh in itertools.product(range(4), range(2), range(2), range(4), range(2))
    ]
    return lax.ppermute(values, AXES, pairs)


def slot_block(values, offset, flip):
    return lax.dynamic_slice_in_dim(values, (offset ^ flip) * BLK, BLK, 0)


def for_home(stayed, first, second, both, z, core):
    pieces = jnp.stack([stayed, jnp.where(core == 0, first, second), both, jnp.where(core == 0, second, first)])
    return jnp.stack([lax.dynamic_index_in_dim(pieces, z ^ scene, 0, keepdims=False) for scene in range(3)])


SWAP = ((0, 1), (1, 0))
MASKS = ((1, 3), (3, 1))


def exchange(value, move):
    pairs = []
    for place in itertools.product(range(4), range(4), range(4), range(2)):
        ends = [linear(y, x % 2, c, z, x // 2) for x, y, z, c in (place, move(*place))]
        pairs.append(tuple(ends))
    return lax.ppermute(value, AXES, pairs)


def meet(value, axis, step):
    def move(x, y, z, c):
        at = {"x": x, "y": y, "z": z}
        at[axis] = at[axis] ^ MASKS[c][step]
        return at["x"], at["y"], at["z"], c

    return exchange(value, move)


def swap(value):
    return lax.ppermute(value, "c", SWAP)


ORDERS = ("yxz", "zyx")


def meet_parts(values, stage, step):
    return [meet(value, ORDERS[part][stage], step) for part, value in enumerate(values)]


def add(*terms):
    return functools.reduce(jnp.add, [term.astype(f32) for term in terms]).astype(bf16)


def block_of(blocks, index):
    return lax.dynamic_index_in_dim(blocks, index, 1, keepdims=False)


def put_block(blocks, value, index):
    return lax.dynamic_update_index_in_dim(blocks, value, index, 1)


SMALL = 16


def meet_with(value, small, axis, step):
    high = lax.reduce_precision(small, 8, 7)
    low = lax.reduce_precision(small - high, 8, 7)
    rows = value.reshape(-1, D)
    message = jnp.concatenate([rows, high.astype(bf16), low.astype(bf16)], axis=0)
    arrived = meet(message, axis, step)
    count = rows.shape[0]
    other = arrived[count : count + SMALL].astype(f32) + arrived[count + SMALL :].astype(f32)
    return arrived[:count].reshape(value.shape), (high + low) + other


def hold(*values):
    return lax.optimization_barrier(values)


def body(
    tokens, view_counts, ln1_gain, ln1_shift, qkv_weight, query_bias, value_bias, out_weight, out_bias,
    ln2_gain, ln2_shift, up_weight, up_bias, down_weight, down_bias, cotangent,
):
    core, z, xh = lax.axis_index("c"), lax.axis_index("z"), lax.axis_index("xh")

    flip = jnp.where(xh == core, 0, 2)
    views = jnp.broadcast_to(view_counts.astype(bf16)[:, None, None], (3, BLK, LANES))
    pieces = to_scene((tokens, cotangent, views), z, flip)
    vecs = jnp.concatenate([jnp.stack([out_bias, ln2_gain, ln2_shift, down_bias]), jnp.zeros((4, D), f32)])
    gains = ln1_gain.reshape(1, D)
    weight_q, weight_kv = qkv_weight[:, :D], qkv_weight[:, D:]
    pieces, vecs, gains, weight_q, weight_kv = hold(pieces, vecs, gains, weight_q, weight_kv)
    both = jnp.concatenate([piece[:, : 2 * D] for piece in pieces], axis=0)
    views = pieces[0][0, 2 * D].astype(f32)
    x = both[:, :D]

    y = lax.axis_index("y")
    x_place = lax.axis_index("xh") * 2 + lax.axis_index("xl")
    at = jnp.stack([core, y, z, z, flip, views.astype(jnp.int32)]).astype(jnp.int32)

    source = x.astype(f32)
    centred = source - jnp.mean(source, axis=1, keepdims=True)
    rstd = lax.rsqrt(jnp.mean(centred * centred, axis=1, keepdims=True) + epsilon)
    normed = (centred * rstd * ln1_gain + ln1_shift).astype(bf16)
    product = lambda weight: jnp.dot(normed, weight, preferred_element_type=f32)
    kv_bias = jnp.concatenate([jnp.zeros((D,), f32), value_bias])
    own = (product(weight_kv) + kv_bias).astype(bf16)
    sibling = swap(own)
    normed_other = swap(normed)
    queries = (product(weight_q) + query_bias).astype(bf16)
    weights, heads_out, linv, attended = attention_forward(at, queries, own, sibling)

    up_b = up_bias.reshape(NF, 1, FCHUNK)
    output, grad_hidden, grad_branch, grad_att, up_other, up_mine, down_other, down_mine, vec_grads, up_b_grad = (
        feed_forward(at, attended, both, out_weight, vecs, up_b, up_weight, down_weight)
    )

    moving = [swap(up_other), swap(down_other)]
    attended_other, branch_other = swap(attended), swap(grad_branch)
    grad_q, grad_own, sent = attention_backward(at, queries, own, sibling, weights, heads_out, linv, grad_att)

    moving, attended_other, branch_other, sent = hold(moving, attended_other, branch_other, sent)
    arrived = swap(sent)
    pieces = [(up_mine, moving[0]), (down_mine, moving[1])]
    away = [add(mine[2:], other[2:]) for mine, other in pieces]
    halved = meet_parts(away, 0, 0)
    arrived, away = hold(arrived, away)
    keep0, away0, keep1, away1 = squares(
        at, grad_q, grad_own, sent, arrived, grad_branch, branch_other, normed, normed_other, attended, attended_other
    )

    away, grad_hidden = hold([away0, away1], grad_hidden)
    square_halved = meet_parts(away, 0, 0)
    halved, grad_hidden = hold(halved, grad_hidden)
    away = [add(mine[1], other[1], half[1]) for (mine, other), half in zip(pieces, halved)]
    away, grad_hidden = hold(away, grad_hidden)
    quartered = meet_parts(away, 0, 1)
    input_grad, small = input_gradient(
        grad_q, grad_own, arrived, qkv_weight, both, grad_hidden, gains, vec_grads, up_b_grad
    )

    square_halved, small, input_grad = hold(square_halved, small, input_grad)
    square_away = [add(keep[1], half[1]) for keep, half in zip((keep0, keep1), square_halved)]
    square_away, quartered = hold(square_away, quartered)
    square_quartered = meet_parts(square_away, 0, 1)

    def ring_sum(pieces, halved, quartered):
        return [
            add(mine[0], other[0], half[0], quarter)
            for (mine, other), half, quarter in zip(pieces, halved, quartered)
        ]

    ff_own = ring_sum(pieces, halved, quartered)
    square_quartered, ff_own, small = hold(square_quartered, ff_own, small)
    owns = [add(k[0], h[0], q) for k, h, q in zip((keep0, keep1), square_halved, square_quartered)]
    blocks = [
        jnp.concatenate([f, o], axis=0).reshape(NF // 2 + 1, 4, QUARTER // 4, D) for f, o in zip(ff_own, owns)
    ]
    places = [x_place, y]
    first = 1 + 2 * core
    keep = [(block_of(b, p), block_of(b, p ^ (4 - first))) for b, p in zip(blocks, places)]
    away = [jnp.stack([block_of(b, p ^ first), block_of(b, p ^ 2)]) for b, p in zip(blocks, places)]
    second = 4 - first
    back = jnp.concatenate([output, input_grad], axis=1)
    over = jnp.concatenate([slot_block(back, first, flip), slot_block(back, 2, flip)], axis=0)
    keep, away, small, over, back = hold(keep, away, small, over, back)
    over = meet(over, "z", 0)
    one_way = meet(away[0], "x", 0)
    other_way, small = meet_with(away[1], small, "y", 0)

    one_way, other_way, small = hold(one_way, other_way, small)
    halved = [one_way, other_way]
    away, small = hold([add(k[1], h[1]) for k, h in zip(keep, halved)], small)
    one_way = meet(away[0], "x", 1)
    other_way, small = meet_with(away[1], small, "y", 1)

    one_way, other_way, small = hold(one_way, other_way, small)
    quartered = [one_way, other_way]
    ends = [add(k[0], h[0], q) for k, h, q in zip(keep, halved, quartered)]
    for step in range(2):
        ends, small = hold(ends, small)
        one_way, small = meet_with(ends[0], small, "z", step)
        other_way = meet(ends[1], "x", step)
        one_way, other_way, small = hold(one_way, other_way, small)
        ends = [ends[0] + one_way, ends[1] + other_way]

    over_first = over[:BLK]
    over = jnp.concatenate([slot_block(back, second, flip), over[BLK:]], axis=0)
    ends, small, over, over_first = hold(ends, small, over, over_first)
    over = meet(over, "z", 1)
    one_way, small = meet_with(ends[0], small, "x", 1)
    other_way = meet(ends[1], "y", 1)

    one_way, other_way, small = hold(one_way, other_way, small)
    pairs = [jnp.stack([ends[0], one_way]), jnp.stack([ends[1], other_way])]
    pairs, small = hold(pairs, small)
    one_way, small = meet_with(pairs[0], small, "x", 0)
    other_way = meet(pairs[1], "y", 0)

    one_way, other_way, small = hold(one_way, other_way, small)
    owns = []
    for pair, more, p, empty in zip(pairs, (one_way, other_way), places, blocks):
        full = jnp.zeros_like(empty)
        for value, index in ((pair[0], p), (pair[1], p ^ (4 - first)), (more[0], p ^ first), (more[1], p ^ 2)):
            full = put_block(full, value, index)
        owns.append(full.reshape(NF // 2 + 1, QUARTER, D))
    returned = for_home(slot_block(back, 0, flip), over_first, over[:BLK], over[BLK:], z, core)
    owns, small, returned = hold(owns, small, returned)
    arrived = meet_parts(owns, 0, 1)
    returned = turn(returned)

    arrived, small, returned = hold(arrived, small, returned)
    pairs = [jnp.stack([o, a]) for o, a in zip(owns, arrived)]
    pairs, small = hold(pairs, small)
    got = meet_parts(pairs, 0, 0)
    own_other = [swap(v) for v in pairs]
    small_other = swap(small)
    placed = place(at, pairs, True, False)
    output, input_grad = returned[:, :, :D], returned[:, :, D:]

    own_other, small_other, placed, output, input_grad = hold(own_other, small_other, placed, output, input_grad)
    small = small + small_other
    placed = place(at, own_other, False, False, placed)
    got, placed = hold(got, placed)
    got_other = [swap(v) for v in got]
    placed = place(at, got, True, True, placed)
    d_up, d_down, d_qkv, d_out = place(at, got_other, False, True, placed)
    return (
        output, input_grad, small[4], small[5], d_qkv, small[6], small[7], d_out,
        small[0], small[1], small[2], d_up, small[8:12].reshape(FF), d_down, small[3],
    )


def solution(mesh):
    fine = Mesh(mesh.devices.reshape(4, 2, 2, 4, 2), AXES)
    rows = P(("y", "xl", "c"), ("z", "xh"), None)
    placed = (rows, P(("y", "xl", "c"))) + (P(),) * 13 + (rows,)
    return jax.shard_map(
        body, mesh=fine, in_specs=placed, out_specs=(rows, rows) + (P(),) * 13, check_vma=False
    )
```
